32 devices in a mesh: dp: 32 (over z, y, x, core).
Axes of the slice: x: 2, y: 2, z: 4, core: 2. Of those that a mesh axis runs over, the one named last changes fastest.
Arguments:
- target: bfloat16 [128, 144, 512], P('dp'), may hold values from -6 to 6
- memory: bfloat16 [512, 128, 512], P('dp'), may hold values from -6 to 6
- target_segments: int32 [128, 144], P('dp'), may hold values from 0 to 2, as said below
- memory_segments: int32 [128, 512], P('dp'), may hold values from 0 to 2, as said below
- cotangent: bfloat16 [128, 144, 512], P('dp'), may hold values from -6 to 6
- self_query: bfloat16 [512, 512], replicated, may hold values from -0.0625 to 0.0625
- self_key: bfloat16 [512, 512], replicated, may hold values from -0.25 to 0.25
- self_value: bfloat16 [512, 512], replicated, may hold values from -0.25 to 0.25
- self_output: bfloat16 [512, 512], replicated, may hold values from -0.75 to 0.75
- relative_bias: bfloat16 [32, 8], replicated, may hold values from -4 to 4
- self_gain: bfloat16 [512], replicated, may hold values from 0.5 to 1.5
- cross_query: bfloat16 [512, 512], replicated, may hold values from -0.0625 to 0.0625
- cross_key: bfloat16 [512, 512], replicated, may hold values from -0.25 to 0.25
- cross_value: bfloat16 [512, 512], replicated, may hold values from -0.25 to 0.25
- cross_output: bfloat16 [512, 512], replicated, may hold values from -1 to 1
- cross_gain: bfloat16 [512], replicated, may hold values from 0.5 to 1.5
- ffn_gain: bfloat16 [512], replicated, may hold values from 0.5 to 1.5
- ffn_in: bfloat16 [512, 2048], replicated, may hold values from -0.25 to 0.25
- ffn_out: bfloat16 [2048, 512], replicated, may hold values from -0.125 to 0.125
Outputs:
- layer_out: bfloat16 [128, 144, 512], P('dp')
- target_grad: bfloat16 [128, 144, 512], P('dp')
- memory_grad: bfloat16 [512, 128, 512], P('dp')
- self_query_grad: float32 [512, 512], replicated
- self_key_grad: float32 [512, 512], replicated
- self_value_grad: float32 [512, 512], replicated
- self_output_grad: float32 [512, 512], replicated
- relative_bias_grad: float32 [32, 8], replicated
- self_gain_grad: float32 [512], replicated
- cross_query_grad: float32 [512, 512], replicated
- cross_key_grad: float32 [512, 512], replicated
- cross_value_grad: float32 [512, 512], replicated
- cross_output_grad: float32 [512, 512], replicated
- cross_gain_grad: float32 [512], replicated
- ffn_gain_grad: float32 [512], replicated
- ffn_in_grad: float32 [512, 2048], replicated
- ffn_out_grad: float32 [2048, 512], replicated
The draws below stay inside these ranges and needn't reach their ends.
Inputs may be any that keep to these rules, and one draw needn't show every extreme that they name: `target_segments`: in every row the document numbers never fall along the positions, begin at 0 and take every value up to 2, so each document has target and memory positions. `memory_segments`: in every row the document numbers never fall along the positions, begin at 0 and take every value up to 2.
All inputs are finite; a program needn't handle non-finite values.
Results may differ from the reference program's by a relative error of at most 0.025.
The reference program's roundings to bfloat16 on the way count: a program that leaves them out, or rounds other values in their place, can miss the bound.
Values may be sent and summed in bfloat16 or wider, within the bound.
No kernel may reach another device: no remote copies, remote signals or barrier semaphores. Data moves between devices by JAX's collectives and lax.ppermute only.
A program may use at most 128 MiB of HBM per device.

```python
import jax
import jax.numpy as jnp
import numpy as np
from jax import lax

D = 512
H = 8
DH = 64
FF = 2048
NB = 32
MAXDIST = 128
TGT = 144
MEM = 512
NSEG = 3
ROWS = 128


def cut_segments(key, rows_count, length):
    keys_all = jax.random.split(key, rows_count)
    places = jnp.arange(length)

    def one_line(line_key):
        cuts = jax.random.permutation(line_key, length - 1)[:NSEG - 1] + 1
        return jnp.sum((places[:, None] >= cuts[None, :]).astype(jnp.int32), axis=1)
    return jax.vmap(one_line)(keys_all).astype(jnp.int32)


def draw_target_segments(key, part):
    key = jax.random.fold_in(key, 11)
    return cut_segments(key, ROWS, TGT)


def draw_memory_segments(key, part):
    key = jax.random.fold_in(key, 23)
    return cut_segments(key, ROWS, MEM)


def steps_of(own_key, shape, pieces, low, largest):
    def one(position, blocks):
        steps = jax.random.uniform(jax.random.fold_in(jax.random.fold_in(own_key, 6), position), (blocks,), jnp.float32, low / len(pieces), largest / len(pieces))
        return jnp.repeat(jnp.exp(steps), shape[position] // blocks).reshape((-1,) + (1,) * (len(shape) - position - 1))

    loudness = one(*pieces[0])
    for cut in pieces[1:]:
        loudness = loudness * one(*cut)
    return loudness


def noise(stream_key, extent, scale, bound, shards=(), kind=jnp.bfloat16):
    level = steps_of(stream_key, extent, shards, -0.22, 0.18) if shards else 1.0
    drawn = jax.random.normal(stream_key, extent, jnp.float32) * scale * level
    return jnp.minimum(jnp.maximum(drawn, -bound), bound).astype(kind)


def setup_inputs(seed: int = 0) -> dict:
    key_list = jax.random.split(jax.random.key(seed), 20)
    return {
        "target": noise(key_list[0], (ROWS, TGT, D), 1.0, 6.0, ((0, 32),)),
        "memory": noise(key_list[1], (MEM, ROWS, D), 1.0, 6.0, ((0, 32),)),
        "target_segments": draw_target_segments(jax.random.fold_in(key_list[19], 71), 0),
        "memory_segments": draw_memory_segments(jax.random.fold_in(key_list[19], 71), 0),
        "cotangent": noise(key_list[4], (ROWS, TGT, D), 1.0, 6.0, ((0, 32),)),
        "self_query": noise(key_list[5], (D, H * DH), (16 * D) ** -0.5, 0.0625),
        "self_key": noise(key_list[6], (D, H * DH), D ** -0.5, 0.25),
        "self_value": noise(key_list[7], (D, H * DH), D ** -0.5, 0.25),
        "self_output": noise(key_list[8], (H * DH, D), (D // 8) ** -0.5, 0.75),
        "relative_bias": noise(key_list[9], (NB, H), 1.0, 4.0),
        "self_gain": jnp.clip(1.0 + 0.1 * jax.random.normal(key_list[10], (D,), jnp.float32), 0.5, 1.5).astype(jnp.bfloat16),
        "cross_query": noise(key_list[11], (D, H * DH), (16 * D) ** -0.5, 0.0625),
        "cross_key": noise(key_list[12], (D, H * DH), D ** -0.5, 0.25),
        "cross_value": noise(key_list[13], (D, H * DH), D ** -0.5, 0.25),
        "cross_output": noise(key_list[14], (H * DH, D), (D // 16) ** -0.5, 1.0),
        "cross_gain": jnp.clip(1.0 + 0.1 * jax.random.normal(key_list[15], (D,), jnp.float32), 0.5, 1.5).astype(jnp.bfloat16),
        "ffn_gain": jnp.clip(1.0 + 0.1 * jax.random.normal(key_list[16], (D,), jnp.float32), 0.5, 1.5).astype(jnp.bfloat16),
        "ffn_in": noise(key_list[17], (D, FF), D ** -0.5, 0.25),
        "ffn_out": noise(key_list[18], (FF, D), FF ** -0.5, 0.125),
    }


@jax.custom_vjp
def low(v):
    return lax.optimization_barrier(v.astype(jnp.bfloat16)).astype(jnp.float32)

@jax.custom_vjp
def low_back(v):
    return v

def low_keep(v):
    return (low(v), None)

def low_pass(kept, grad):
    return (grad,)

def back_keep(v):
    return (v, None)

def back_low(kept, grad):
    return (low(grad),)
low.defvjp(low_keep, low_pass)
low_back.defvjp(back_keep, back_low)
EPS = 1e-06
HIGH = lax.Precision.HIGHEST

def both_ways(tensor):
    return low_back(low(tensor))

def bucket_table(length):
    exact = NB // 2
    offsets = np.arange(length)[:, None] - np.arange(length)[None, :]
    distance = np.maximum(offsets, 0)
    scaled = np.log(np.maximum(distance, exact) / exact) / np.log(MAXDIST / exact) * (NB - exact)
    farther = np.minimum(exact + scaled.astype(np.int32), NB - 1)
    return np.where(distance < exact, distance, farther).astype(np.int32)

def norm_apply(tensor, weight_gain):
    return tensor * lax.rsqrt(lax.optimization_barrier(jnp.mean(tensor * tensor, axis=-1, keepdims=True)) + EPS) * weight_gain

def matmul(left, right):
    return jnp.dot(left, right, precision=HIGH, preferred_element_type=jnp.float32)

def one_row(params, packed):
    sq_w, sk_w, sv_w, so_w, rel_bias, gain_one, cq_w, ck_w, cv_w, co_w, gain_two, gain_three, up_w, down_w = params
    tokens, memory_row, target_seg, memory_seg = packed
    shaped = (TGT, H, DH)
    normed_one = low(norm_apply(tokens, gain_one))
    queries = both_ways(matmul(normed_one, sq_w)).reshape(shaped)
    self_keys = both_ways(matmul(normed_one, sk_w)).reshape(shaped)
    values = both_ways(matmul(normed_one, sv_w)).reshape(shaped)
    table = bucket_table(TGT)
    bias_full = jnp.transpose(rel_bias[table], (2, 0, 1))
    scores = low_back(jnp.einsum('ihd,jhd->hij', queries, self_keys, precision=HIGH) + bias_full)
    causal = np.tril(np.ones((TGT, TGT), dtype=bool))
    self_mask = jnp.logical_and(causal, target_seg[:, None] == target_seg[None, :])
    weights_one = low(jax.nn.softmax(jnp.where(self_mask[None], scores, -1000000000.0), axis=-1))
    attended = both_ways(jnp.einsum('hij,jhd->ihd', weights_one, values, precision=HIGH)).reshape(TGT, H * DH)
    after_self = tokens + low_back(matmul(attended, so_w))
    normed_two = low(norm_apply(after_self, gain_two))
    cross_queries = both_ways(matmul(normed_two, cq_w)).reshape(shaped)
    cross_keys = both_ways(matmul(memory_row, ck_w)).reshape(MEM, H, DH)
    cross_values = both_ways(matmul(memory_row, cv_w)).reshape(MEM, H, DH)
    cross_mask = target_seg[:, None] == memory_seg[None, :]
    scores_two = low_back(jnp.einsum('ihd,jhd->hij', cross_queries, cross_keys, precision=HIGH))
    weights_two = low(jax.nn.softmax(jnp.where(cross_mask[None], scores_two, -1000000000.0), axis=-1))
    attended_two = both_ways(jnp.einsum('hij,jhd->ihd', weights_two, cross_values, precision=HIGH)).reshape(TGT, H * DH)
    after_cross = after_self + low_back(matmul(attended_two, co_w))
    normed_three = low(norm_apply(after_cross, gain_three))
    activation = low_back(matmul(normed_three, up_w))
    hidden = low(jax.nn.gelu(activation, approximate=True))
    return after_cross + low_back(matmul(hidden, down_w))

def reference(target, memory, target_segments, memory_segments, cotangent, self_query, self_key, self_value, self_output, relative_bias, self_gain, cross_query, cross_key, cross_value, cross_output, cross_gain, ffn_gain, ffn_in, ffn_out):
    weights = tuple((matrix.astype(jnp.float32) for matrix in (self_query, self_key, self_value, self_output, relative_bias, self_gain, cross_query, cross_key, cross_value, cross_output, cross_gain, ffn_gain, ffn_in, ffn_out)))

    def forward(target_f, memory_f, *params):
        memory_rows = jnp.transpose(memory_f, (1, 0, 2))

        def one_step(packed):
            return one_row(params, packed)
        return lax.map(jax.checkpoint(one_step), (target_f, memory_rows, target_segments, memory_segments))
    result, pull = jax.vjp(forward, target.astype(jnp.float32), memory.astype(jnp.float32), *weights)
    grads = pull(cotangent.astype(jnp.float32))
    return (result.astype(jnp.bfloat16), grads[0].astype(jnp.bfloat16), grads[1].astype(jnp.bfloat16), grads[2], grads[3], grads[4], grads[5], grads[6], grads[7], grads[8], grads[9], grads[10], grads[11], grads[12], grads[13], grads[14], grads[15])
```

```python
import jax
import jax.numpy as jnp
import numpy as np
from jax import lax
from jax.sharding import PartitionSpec as P

NB = 32
MAXDIST = 128


EPS = 1e-06


def bucket_table(length):
    exact = NB // 2
    offsets = np.arange(length)[:, None] - np.arange(length)[None, :]
    distance = np.maximum(offsets, 0)
    scaled = np.log(np.maximum(distance, exact) / exact) / np.log(MAXDIST / exact) * (NB - exact)
    farther = np.minimum(exact + scaled.astype(np.int32), NB - 1)
    return np.where(distance < exact, distance, farther).astype(np.int32)


def product(left, right):
    return jnp.dot(left, right, preferred_element_type=jnp.float32)


def product_left(left, right):
    return lax.dot_general(
        left, right, (((0,), (0,)), ((), ())), preferred_element_type=jnp.float32
    )


def product_right(left, right):
    return lax.dot_general(
        left, right, (((1,), (1,)), ((), ())), preferred_element_type=jnp.float32
    )


def norm_forward(tensor, weight_gain):
    factor = lax.rsqrt(jnp.mean(tensor * tensor, axis=-1, keepdims=True) + EPS)
    return (tensor * factor * weight_gain, factor)


def norm_backward(tensor, factor, weight_gain, incoming):
    shaped = incoming * weight_gain
    gain_grad = jnp.sum(incoming * tensor * factor, axis=0)
    inner = jnp.mean(tensor * shaped, axis=-1, keepdims=True)
    return (factor * shaped - tensor * factor * factor * factor * inner, gain_grad)


def softmax_back(probs, upstream):
    return (probs * (upstream - jnp.sum(upstream * probs, axis=-1, keepdims=True))).astype(
        jnp.bfloat16
    )


def factors_of(n):
    factors = [2]
    n //= 2
    while n > 1:
        factor = 4 if n % 4 == 0 else n
        factors.append(factor)
        n //= factor
    return factors


def partners(n, stride, factor, j):
    moves = []
    for i in range(n):
        digit = (i // stride) % factor
        moves.append((i, i + ((digit ^ j) - digit) * stride))
    return moves


def phases():
    n = lax.axis_size("dp")
    me = lax.axis_index("dp")
    stride = 1
    out = []
    for factor in factors_of(n):
        digit = (me // stride) % factor
        out.append((factor, digit, [partners(n, stride, factor, j) for j in range(factor)]))
        stride *= factor
    return out


def sum_blocks(blocks):
    k, _, columns = blocks.shape
    held = blocks.astype(jnp.bfloat16)
    for factor, digit, moves in phases():
        held = held.reshape(k, factor, -1, columns)
        total = lax.dynamic_index_in_dim(held, digit, axis=1, keepdims=False).astype(jnp.float32)
        for j in range(1, factor):
            send = lax.dynamic_index_in_dim(held, digit ^ j, axis=1, keepdims=False)
            total = total + lax.ppermute(send, "dp", moves[j]).astype(jnp.float32)
        held = total.astype(jnp.bfloat16)
    for factor, digit, moves in phases()[::-1]:
        parts = [held] + [lax.ppermute(held, "dp", moves[j]) for j in range(1, factor)]
        stacked = jnp.stack(parts, axis=0)
        ordered = [
            lax.dynamic_index_in_dim(stacked, digit ^ a, axis=0, keepdims=False)
            for a in range(factor)
        ]
        held = jnp.stack(ordered, axis=1).reshape(k, -1, columns)
    return held.astype(jnp.float32)


def sum_small(small):
    for factor, _, moves in phases():
        terms = [small] + [lax.ppermute(small, "dp", moves[j]) for j in range(1, factor)]
        while len(terms) > 1:
            terms = [terms[i] + terms[i + 1] for i in range(0, len(terms), 2)]
        small = terms[0]
    return small


def body(
    target,
    memory,
    target_segments,
    memory_segments,
    cotangent,
    self_query,
    self_key,
    self_value,
    self_output,
    relative_bias,
    self_gain,
    cross_query,
    cross_key,
    cross_value,
    cross_output,
    cross_gain,
    ffn_gain,
    ffn_in,
    ffn_out,
):
    rows_here = target.shape[0]
    length = target.shape[1]
    width = target.shape[2]
    span = memory.shape[0] * lax.axis_size("dp")
    heads = relative_bias.shape[1]
    head_size = self_query.shape[1] // heads
    inner_width = heads * head_size
    count = rows_here * length
    bf16 = jnp.bfloat16
    f32 = jnp.float32
    memory_rows = lax.all_to_all(memory, "dp", split_axis=1, concat_axis=0, tiled=True)
    cross_keys = jnp.einsum(
        "mrd,de->mre", memory_rows, cross_key, preferred_element_type=f32
    ).astype(bf16)
    cross_values = jnp.einsum(
        "mrd,de->mre", memory_rows, cross_value, preferred_element_type=f32
    ).astype(bf16)
    cross_keys = cross_keys.reshape(span, rows_here, heads, head_size)
    cross_values = cross_values.reshape(span, rows_here, heads, head_size)
    table = bucket_table(length)
    onehot = jnp.asarray(table[None, :, :] == np.arange(NB)[:, None, None], dtype=bf16)
    causal = np.tril(np.ones((length, length), dtype=bool))
    self_mask = jnp.logical_and(
        causal[None], target_segments[:, :, None] == target_segments[:, None, :]
    )[:, None]
    cross_mask = (target_segments[:, :, None] == memory_segments[:, None, :])[:, None]
    bias_full = jnp.einsum("bh,bij->hij", relative_bias, onehot, preferred_element_type=f32)
    gain_one = self_gain.astype(f32)
    gain_two = cross_gain.astype(f32)
    gain_three = ffn_gain.astype(f32)
    tokens = target.reshape(count, width).astype(f32)
    normed_full, factor_one = norm_forward(tokens, gain_one)
    normed_one = normed_full.astype(bf16)
    queries = product(normed_one, self_query).astype(bf16)
    self_keys = product(normed_one, self_key).astype(bf16)
    values = product(normed_one, self_value).astype(bf16)
    queries_h = queries.reshape(rows_here, length, heads, head_size)
    keys_h = self_keys.reshape(rows_here, length, heads, head_size)
    values_h = values.reshape(rows_here, length, heads, head_size)

    def self_scores():
        raw = (
            jnp.einsum("rihd,rjhd->rhij", queries_h, keys_h, preferred_element_type=f32)
            + bias_full[None]
        )
        return jnp.where(self_mask, raw, -1000000000.0)

    scores_one = self_scores()
    total_one = jax.nn.logsumexp(scores_one, axis=-1, keepdims=True)
    probs_one = jnp.exp(scores_one - total_one).astype(bf16)
    attended = (
        jnp.einsum("rhij,rjhd->rihd", probs_one, values_h, preferred_element_type=f32)
        .astype(bf16)
        .reshape(count, inner_width)
    )
    after_self = tokens + product(attended, self_output)
    normed_mid, factor_two = norm_forward(after_self, gain_two)
    normed_two = normed_mid.astype(bf16)
    cross_queries = product(normed_two, cross_query).astype(bf16)
    cross_queries_h = cross_queries.reshape(rows_here, length, heads, head_size)

    def cross_scores():
        raw = jnp.einsum("rihd,mrhd->rhim", cross_queries_h, cross_keys, preferred_element_type=f32)
        return jnp.where(cross_mask, raw, -1000000000.0)

    scores_two = cross_scores()
    total_two = jax.nn.logsumexp(scores_two, axis=-1, keepdims=True)
    probs_two = jnp.exp(scores_two - total_two).astype(bf16)
    attended_two = (
        jnp.einsum("rhim,mrhd->rihd", probs_two, cross_values, preferred_element_type=f32)
        .astype(bf16)
        .reshape(count, inner_width)
    )
    after_cross = after_self + product(attended_two, cross_output)
    normed_last, factor_three = norm_forward(after_cross, gain_three)
    normed_three = normed_last.astype(bf16)
    activation = product(normed_three, ffn_in)
    hidden = jax.nn.gelu(activation, approximate=True).astype(bf16)
    layer_out = after_cross + product(hidden, ffn_out)
    upstream = cotangent.reshape(count, width)
    upstream_f = upstream.astype(f32)
    ffn_out_grad = product_left(hidden, upstream)
    hidden_grad = product_right(upstream, ffn_out)
    gelu_pull = jax.vjp(lambda pre_act: jax.nn.gelu(pre_act, approximate=True), activation)[1]
    act_grad = gelu_pull(hidden_grad)[0].astype(bf16)
    ffn_in_grad = product_left(normed_three, act_grad)
    back_three = product_right(act_grad, ffn_in)
    norm_grad_three, ffn_gain_grad = norm_backward(
        after_cross, factor_three, gain_three, back_three
    )
    grad_two = upstream_f + norm_grad_three
    grad_two_low = grad_two.astype(bf16)
    cross_output_grad = product_left(attended_two, grad_two_low)
    attended_two_grad = (
        product_right(grad_two_low, cross_output)
        .astype(bf16)
        .reshape(rows_here, length, heads, head_size)
    )
    probs_two_full = jnp.exp(cross_scores() - total_two)
    probs_two_low = probs_two_full.astype(bf16)
    upstream_two = jnp.einsum(
        "rihd,mrhd->rhim", attended_two_grad, cross_values, preferred_element_type=f32
    )
    value_two_grad = (
        jnp.einsum("rhim,rihd->mrhd", probs_two_low, attended_two_grad, preferred_element_type=f32)
        .astype(bf16)
        .reshape(span, rows_here, inner_width)
    )
    scores_two_grad = softmax_back(probs_two_full, upstream_two)
    query_two_grad = (
        jnp.einsum("rhim,mrhd->rihd", scores_two_grad, cross_keys, preferred_element_type=f32)
        .astype(bf16)
        .reshape(count, inner_width)
    )
    key_two_grad = (
        jnp.einsum("rhim,rihd->mrhd", scores_two_grad, cross_queries_h, preferred_element_type=f32)
        .astype(bf16)
        .reshape(span, rows_here, inner_width)
    )
    cross_query_grad = product_left(normed_two, query_two_grad)
    back_two = product_right(query_two_grad, cross_query)
    cross_key_grad = jnp.einsum(
        "mrd,mre->de", memory_rows, key_two_grad, preferred_element_type=f32
    )
    cross_value_grad = jnp.einsum(
        "mrd,mre->de", memory_rows, value_two_grad, preferred_element_type=f32
    )
    memory_rows_grad = (
        jnp.einsum("mre,de->mrd", key_two_grad, cross_key, preferred_element_type=f32)
        + jnp.einsum("mre,de->mrd", value_two_grad, cross_value, preferred_element_type=f32)
    ).astype(bf16)
    memory_grad = lax.all_to_all(memory_rows_grad, "dp", split_axis=0, concat_axis=1, tiled=True)
    norm_grad_two, cross_gain_grad = norm_backward(after_self, factor_two, gain_two, back_two)
    grad_one = grad_two + norm_grad_two
    grad_one_low = grad_one.astype(bf16)
    self_output_grad = product_left(attended, grad_one_low)
    attended_grad = (
        product_right(grad_one_low, self_output)
        .astype(bf16)
        .reshape(rows_here, length, heads, head_size)
    )
    probs_one_full = jnp.exp(self_scores() - total_one)
    probs_one_low = probs_one_full.astype(bf16)
    upstream_one = jnp.einsum(
        "rihd,rjhd->rhij", attended_grad, values_h, preferred_element_type=f32
    )
    value_grad = (
        jnp.einsum("rhij,rihd->rjhd", probs_one_low, attended_grad, preferred_element_type=f32)
        .astype(bf16)
        .reshape(count, inner_width)
    )
    scores_one_grad = softmax_back(probs_one_full, upstream_one)
    relative_bias_grad = jnp.einsum(
        "rhij,bij->bh", scores_one_grad, onehot, preferred_element_type=f32
    )
    query_grad = (
        jnp.einsum("rhij,rjhd->rihd", scores_one_grad, keys_h, preferred_element_type=f32)
        .astype(bf16)
        .reshape(count, inner_width)
    )
    key_grad = (
        jnp.einsum("rhij,rihd->rjhd", scores_one_grad, queries_h, preferred_element_type=f32)
        .astype(bf16)
        .reshape(count, inner_width)
    )
    self_query_grad = product_left(normed_one, query_grad)
    self_key_grad = product_left(normed_one, key_grad)
    self_value_grad = product_left(normed_one, value_grad)
    back_one = (
        product_right(query_grad, self_query)
        + product_right(key_grad, self_key)
        + product_right(value_grad, self_value)
    )
    norm_grad_one, self_gain_grad = norm_backward(tokens, factor_one, gain_one, back_one)
    target_grad = (grad_one + norm_grad_one).astype(bf16).reshape(rows_here, length, width)
    ffn_sum = sum_blocks(
        jnp.concatenate(
            [
                jnp.swapaxes(ffn_in_grad.astype(bf16).reshape(width, -1, width), 0, 1),
                ffn_out_grad.astype(bf16).reshape(-1, width, width),
            ],
            axis=0,
        )
    )
    parts = ffn_sum.shape[0] // 2
    ffn_in_grad = jnp.swapaxes(ffn_sum[:parts], 0, 1).reshape(width, -1)
    ffn_out_grad = ffn_sum[parts:].reshape(-1, width)
    cross_output_grad, cross_query_grad, cross_key_grad, cross_value_grad = sum_blocks(
        jnp.stack([cross_output_grad, cross_query_grad, cross_key_grad, cross_value_grad])
    )
    self_output_grad, self_query_grad, self_key_grad, self_value_grad = sum_blocks(
        jnp.stack([self_output_grad, self_query_grad, self_key_grad, self_value_grad])
    )
    flat = jnp.concatenate(
        [self_gain_grad, cross_gain_grad, ffn_gain_grad, relative_bias_grad.reshape(-1)]
    )
    size = flat.shape[0]
    flat = jnp.pad(flat, (0, -size % 1024)).reshape(-1, 128)
    flat = sum_small(flat).reshape(-1)
    self_gain_grad = flat[:width]
    cross_gain_grad = flat[width : 2 * width]
    ffn_gain_grad = flat[2 * width : 3 * width]
    relative_bias_grad = flat[3 * width : size].reshape(relative_bias_grad.shape)
    return (
        layer_out.astype(bf16).reshape(rows_here, length, width),
        target_grad,
        memory_grad,
        self_query_grad,
        self_key_grad,
        self_value_grad,
        self_output_grad,
        relative_bias_grad,
        self_gain_grad,
        cross_query_grad,
        cross_key_grad,
        cross_value_grad,
        cross_output_grad,
        cross_gain_grad,
        ffn_gain_grad,
        ffn_in_grad,
        ffn_out_grad,
    )


def solution(mesh):
    in_specs = (
        P("dp", None, None),
        P("dp", None, None),
        P("dp", None),
        P("dp", None),
        P("dp", None, None),
        P(),
        P(),
        P(),
        P(),
        P(),
        P(),
        P(),
        P(),
        P(),
        P(),
        P(),
        P(),
        P(),
        P(),
    )
    out_specs = (
        P("dp", None, None),
        P("dp", None, None),
        P("dp", None, None),
        P(),
        P(),
        P(),
        P(),
        P(),
        P(),
        P(),
        P(),
        P(),
        P(),
        P(),
        P(),
        P(),
        P(),
    )
    return jax.shard_map(body, mesh=mesh, in_specs=in_specs, out_specs=out_specs, check_vma=False)
```

```python
import functools

import jax
import jax.numpy as jnp
import numpy as np
from jax import lax
from jax.experimental import pallas as pl
from jax.experimental.pallas import tpu as pltpu
from jax.sharding import PartitionSpec as P

NB = 32
MAXDIST = 128
EPS = 1e-06
GROUP = 256
MASKED = -1000000000.0
VMEM_LIMIT = 56 * 1024 * 1024
BF16 = jnp.bfloat16
F32 = jnp.float32


def bucket_table(length):
    exact = NB // 2
    offsets = np.arange(length)[:, None] - np.arange(length)[None, :]
    distance = np.maximum(offsets, 0)
    scaled = np.log(np.maximum(distance, exact) / exact) / np.log(MAXDIST / exact) * (NB - exact)
    farther = np.minimum(exact + scaled.astype(np.int32), NB - 1)
    return np.where(distance < exact, distance, farther).astype(np.int32)


def dot_nn(left, right):
    return lax.dot_general(left, right, (((1,), (0,)), ((), ())), preferred_element_type=F32)


def dot_nt(left, right):
    return lax.dot_general(left, right, (((1,), (1,)), ((), ())), preferred_element_type=F32)


def dot_tn(left, right):
    return lax.dot_general(left, right, (((0,), (0,)), ((), ())), preferred_element_type=F32)


def norm_factor(tensor):
    return lax.rsqrt(jnp.mean(tensor * tensor, axis=-1, keepdims=True) + EPS)


def norm_backward(tensor, gain, incoming):
    factor = norm_factor(tensor)
    scaled = tensor * factor
    shaped = incoming * gain
    inner = jnp.mean(scaled * shaped, axis=-1, keepdims=True)
    return factor * (shaped - scaled * inner), incoming * scaled


def head_masks(head_size, dtype):
    lane = lax.broadcasted_iota(jnp.int32, (1, GROUP), 1)
    return [
        jnp.where(lane // head_size == h, 1.0, 0.0).astype(dtype)
        for h in range(GROUP // head_size)
    ]


def stack_heads(tensor, masks):
    return jnp.concatenate([tensor * mask for mask in masks], axis=0)


def merge_heads(stacked, masks, length):
    out = stacked[:length] * masks[0]
    for h in range(1, len(masks)):
        out = out + stacked[h * length : (h + 1) * length] * masks[h]
    return out


def softmax_rows(scores):
    top = jnp.max(scores, axis=-1, keepdims=True)
    grown = jnp.exp(scores - top)
    return grown * (1.0 / jnp.sum(grown, axis=-1, keepdims=True))


def self_forward_kernel(
    rows,
    length,
    head_size,
    x_ref,
    column_ref,
    line_ref,
    bias_ref,
    query_ref,
    key_ref,
    value_ref,
    output_ref,
    cross_query_ref,
    gain_one_ref,
    gain_two_ref,
    h1_ref,
    q_ref,
    k_ref,
    v_ref,
    p_ref,
    o_ref,
    y1_ref,
    h2_ref,
    cq_ref,
):
    masks = head_masks(head_size, BF16)
    masks_f = head_masks(head_size, F32)
    x = x_ref[...].astype(F32)
    h1 = (x * norm_factor(x) * gain_one_ref[...]).astype(BF16)
    h1_ref[...] = h1
    q_ref[...] = dot_nn(h1, query_ref[...]).astype(BF16)
    k_ref[...] = dot_nn(h1, key_ref[...]).astype(BF16)
    v_ref[...] = dot_nn(h1, value_ref[...]).astype(BF16)
    i = lax.broadcasted_iota(jnp.int32, (length, length), 0)
    j = lax.broadcasted_iota(jnp.int32, (length, length), 1)

    def row(r, carry):
        here = pl.ds(pl.multiple_of(r * length, 16), length)
        allowed = jnp.logical_and(j <= i, column_ref[r] == line_ref[r])
        shift = jnp.where(allowed, 0.0, MASKED)
        for g in range(q_ref.shape[1] // GROUP):
            lanes = pl.ds(g * GROUP, GROUP)
            scores = dot_nt(stack_heads(q_ref[here, lanes], masks), k_ref[here, lanes])
            probs = []
            for h in range(len(masks)):
                one = scores[h * length : (h + 1) * length]
                one = one + bias_ref[g * len(masks) + h] + shift
                probs.append(softmax_rows(one).astype(BF16))
            stacked = jnp.concatenate(probs, axis=0)
            size = stacked.shape[0]
            p_ref[r, g * size : (g + 1) * size, :] = stacked
            mixed = merge_heads(dot_nn(stacked, v_ref[here, lanes]), masks_f, length)
            o_ref[here, lanes] = mixed.astype(BF16)
        return carry

    lax.fori_loop(0, rows, row, 0)
    y1 = x + dot_nn(o_ref[...], output_ref[...])
    y1_ref[...] = y1
    h2 = (y1 * norm_factor(y1) * gain_two_ref[...]).astype(BF16)
    h2_ref[...] = h2
    cq_ref[...] = dot_nn(h2, cross_query_ref[...]).astype(BF16)


def cross_forward_kernel(
    length,
    head_size,
    cq_ref,
    mem_ref,
    y1_ref,
    column_ref,
    line_ref,
    key_ref,
    value_ref,
    output_ref,
    ck_ref,
    cv_ref,
    p_ref,
    o_ref,
    y2_ref,
):
    masks = head_masks(head_size, BF16)
    masks_f = head_masks(head_size, F32)
    mem = mem_ref[...].reshape(ck_ref.shape[1], -1)
    ck_ref[0] = dot_nn(mem, key_ref[...]).astype(BF16)
    cv_ref[0] = dot_nn(mem, value_ref[...]).astype(BF16)
    shift = jnp.where(column_ref[0] == line_ref[0], 0.0, MASKED)
    for g in range(cq_ref.shape[2] // GROUP):
        lanes = slice(g * GROUP, (g + 1) * GROUP)
        scores = dot_nt(stack_heads(cq_ref[0, :, lanes], masks), ck_ref[0, :, lanes])
        probs = []
        for h in range(len(masks)):
            one = scores[h * length : (h + 1) * length] + shift
            probs.append(softmax_rows(one).astype(BF16))
        stacked = jnp.concatenate(probs, axis=0)
        size = stacked.shape[0]
        p_ref[0, g * size : (g + 1) * size, :] = stacked
        mixed = merge_heads(dot_nn(stacked, cv_ref[0, :, lanes]), masks_f, length)
        o_ref[0, :, lanes] = mixed.astype(BF16)
    y2_ref[0] = y1_ref[0] + dot_nn(o_ref[0], output_ref[...])


def ffn_kernel(
    chunks,
    core_ref,
    y2_ref,
    cot_ref,
    gain_ref,
    in_ref,
    out_ref,
    layer_ref,
    dy2_ref,
    gain_grad_ref,
    keep_ref,
    send_ref,
    h3_ref,
    total_ref,
    back_ref,
    grad_ref,
):
    step = pl.program_id(0)
    half = keep_ref.shape[2]

    @pl.when(step == 0)
    def _():
        y2 = y2_ref[...]
        h3_ref[...] = (y2 * norm_factor(y2) * gain_ref[...]).astype(BF16)
        total_ref[...] = y2
        back_ref[...] = jnp.zeros_like(back_ref)

    h3 = h3_ref[...]
    cot = cot_ref[...]
    act = dot_nn(h3, in_ref[...])
    square = act * act
    root = float(np.sqrt(2.0 / np.pi))
    tanh = jnp.tanh(root * act * (1.0 + 0.044715 * square))
    gate = 0.5 + 0.5 * tanh
    hidden = (act * gate).astype(BF16)
    slope = gate + (0.5 * root) * act * (1.0 - tanh * tanh) * (1.0 + 3 * 0.044715 * square)
    act_grad = (slope * dot_nt(cot, out_ref[...])).astype(BF16)
    total_ref[...] += dot_nn(hidden, out_ref[...])
    back_ref[...] += dot_nt(act_grad, in_ref[...])
    grad_ref[0] = dot_tn(h3, act_grad)
    grad_ref[1] = dot_tn(hidden, cot)
    mine = pl.ds(pl.multiple_of(core_ref[0] * half, half), half)
    other = pl.ds(pl.multiple_of((1 - core_ref[0]) * half, half), half)
    for part in range(2):
        keep_ref[part, 0] = grad_ref[part, mine, :].astype(BF16)
        send_ref[part, 0] = grad_ref[part, other, :].astype(BF16)

    @pl.when(step == chunks - 1)
    def _():
        layer_ref[...] = total_ref[...].astype(BF16)
        grad, gain_grad = norm_backward(y2_ref[...], gain_ref[...], back_ref[...])
        dy2_ref[...] = cot_ref[...].astype(F32) + grad
        gain_grad_ref[...] = jnp.sum(gain_grad, axis=0, keepdims=True)


def cross_backward_kernel(
    rows,
    length,
    head_size,
    core_ref,
    dy2_ref,
    cq_ref,
    ck_ref,
    cv_ref,
    p_ref,
    o_ref,
    mem_ref,
    h2_ref,
    y1_ref,
    gain_ref,
    query_ref,
    key_ref,
    value_ref,
    output_ref,
    mem_grad_ref,
    dy1_ref,
    gain_grad_ref,
    keep_ref,
    send_ref,
    grad_ref,
    dk_ref,
    dv_ref,
    dq_ref,
    gain_total_ref,
):
    step = pl.program_id(0)
    half = keep_ref.shape[1]
    masks = head_masks(head_size, BF16)
    masks_f = head_masks(head_size, F32)

    @pl.when(step == 0)
    def _():
        grad_ref[...] = jnp.zeros_like(grad_ref)
        gain_total_ref[...] = jnp.zeros_like(gain_total_ref)

    c2 = dy2_ref[0].astype(BF16)
    do = dot_nt(c2, output_ref[...]).astype(BF16)
    grad_ref[0] += dot_tn(o_ref[0], c2)
    for g in range(cq_ref.shape[2] // GROUP):
        lanes = slice(g * GROUP, (g + 1) * GROUP)
        queries = stack_heads(cq_ref[0, :, lanes], masks)
        outs = stack_heads(do[:, lanes], masks)
        upstream = dot_nt(outs, cv_ref[0, :, lanes])
        size = upstream.shape[0]
        probs = p_ref[0, g * size : (g + 1) * size, :]
        dv_ref[:, lanes] = dot_tn(probs, outs).astype(BF16)
        pieces = []
        for h in range(len(masks)):
            prob = probs[h * length : (h + 1) * length].astype(F32)
            up = upstream[h * length : (h + 1) * length]
            pieces.append((prob * (up - jnp.sum(prob * up, axis=-1, keepdims=True))).astype(BF16))
        ds = jnp.concatenate(pieces, axis=0)
        dk_ref[:, lanes] = dot_tn(ds, queries).astype(BF16)
        mixed = merge_heads(dot_nn(ds, ck_ref[0, :, lanes]), masks_f, length)
        dq_ref[:, lanes] = mixed.astype(BF16)
    dk = dk_ref[...]
    dv = dv_ref[...]
    dq = dq_ref[...]
    mem_grad = (dot_nt(dk, key_ref[...]) + dot_nt(dv, value_ref[...])).astype(BF16)
    mem_grad_ref[...] = mem_grad.reshape(mem_grad_ref.shape)
    mem = mem_ref[...].reshape(dk.shape[0], -1)
    grad_ref[1] += dot_tn(h2_ref[0], dq)
    grad_ref[2] += dot_tn(mem, dk)
    grad_ref[3] += dot_tn(mem, dv)
    grad, gain_grad = norm_backward(y1_ref[0], gain_ref[...], dot_nt(dq, query_ref[...]))
    dy1_ref[0] = dy2_ref[0] + grad
    gain_total_ref[...] += jnp.sum(gain_grad, axis=0, keepdims=True)

    @pl.when(step == rows - 1)
    def _():
        gain_grad_ref[...] = gain_total_ref[...]
        mine = pl.ds(pl.multiple_of(core_ref[0] * half, half), half)
        other = pl.ds(pl.multiple_of((1 - core_ref[0]) * half, half), half)
        for part in range(4):
            keep_ref[part] = grad_ref[part, mine, :].astype(BF16)
            send_ref[part] = grad_ref[part, other, :].astype(BF16)


def self_backward_kernel(
    rows,
    length,
    head_size,
    core_ref,
    dy1_ref,
    q_ref,
    k_ref,
    v_ref,
    p_ref,
    o_ref,
    h1_ref,
    x_ref,
    gain_ref,
    query_ref,
    key_ref,
    value_ref,
    output_ref,
    dx_ref,
    gain_grad_ref,
    bias_grad_ref,
    keep_ref,
    send_ref,
    grad_ref,
    dq_ref,
    dk_ref,
    dv_ref,
    gain_total_ref,
):
    step = pl.program_id(0)
    half = keep_ref.shape[1]
    masks = head_masks(head_size, BF16)
    masks_f = head_masks(head_size, F32)

    @pl.when(step == 0)
    def _():
        grad_ref[...] = jnp.zeros_like(grad_ref)
        gain_total_ref[...] = jnp.zeros_like(gain_total_ref)
        bias_grad_ref[...] = jnp.zeros_like(bias_grad_ref)

    c1 = dy1_ref[0].astype(BF16)
    do = dot_nt(c1, output_ref[...]).astype(BF16)
    grad_ref[0] += dot_tn(o_ref[0], c1)
    for g in range(q_ref.shape[2] // GROUP):
        lanes = slice(g * GROUP, (g + 1) * GROUP)
        queries = stack_heads(q_ref[0, :, lanes], masks)
        outs = stack_heads(do[:, lanes], masks)
        upstream = dot_nt(outs, v_ref[0, :, lanes])
        size = upstream.shape[0]
        probs = p_ref[0, g * size : (g + 1) * size, :]
        dv_ref[:, lanes] = dot_tn(probs, outs).astype(BF16)
        pieces = []
        for h in range(len(masks)):
            prob = probs[h * length : (h + 1) * length].astype(F32)
            up = upstream[h * length : (h + 1) * length]
            one = (prob * (up - jnp.sum(prob * up, axis=-1, keepdims=True))).astype(BF16)
            bias_grad_ref[g * len(masks) + h] += one.astype(F32)
            pieces.append(one)
        ds = jnp.concatenate(pieces, axis=0)
        dk_ref[:, lanes] = dot_tn(ds, queries).astype(BF16)
        mixed = merge_heads(dot_nn(ds, k_ref[0, :, lanes]), masks_f, length)
        dq_ref[:, lanes] = mixed.astype(BF16)
    dq = dq_ref[...]
    dk = dk_ref[...]
    dv = dv_ref[...]
    h1 = h1_ref[0]
    grad_ref[1] += dot_tn(h1, dq)
    grad_ref[2] += dot_tn(h1, dk)
    grad_ref[3] += dot_tn(h1, dv)
    back = dot_nt(dq, query_ref[...]) + dot_nt(dk, key_ref[...]) + dot_nt(dv, value_ref[...])
    grad, gain_grad = norm_backward(x_ref[0].astype(F32), gain_ref[...], back)
    dx_ref[0] = (dy1_ref[0] + grad).astype(BF16)
    gain_total_ref[...] += jnp.sum(gain_grad, axis=0, keepdims=True)

    @pl.when(step == rows - 1)
    def _():
        gain_grad_ref[...] = gain_total_ref[...]
        mine = pl.ds(pl.multiple_of(core_ref[0] * half, half), half)
        other = pl.ds(pl.multiple_of((1 - core_ref[0]) * half, half), half)
        for part in range(4):
            keep_ref[part] = grad_ref[part, mine, :].astype(BF16)
            send_ref[part] = grad_ref[part, other, :].astype(BF16)


def factors_of(n):
    factors = [2]
    n //= 2
    while n > 1:
        factor = 4 if n % 4 == 0 else n
        factors.append(factor)
        n //= factor
    return factors


def partners(n, stride, factor, j):
    moves = []
    for i in range(n):
        digit = (i // stride) % factor
        moves.append((i, i + ((digit ^ j) - digit) * stride))
    return moves


def phases():
    n = lax.axis_size("dp")
    me = lax.axis_index("dp")
    stride = 1
    out = []
    for factor in factors_of(n):
        digit = (me // stride) % factor
        out.append((factor, digit, [partners(n, stride, factor, j) for j in range(factor)]))
        stride *= factor
    return out


def sum_blocks(keep, send):
    k, _, columns = keep.shape
    steps = phases()
    moves = steps[0][2]
    held = (keep.astype(F32) + lax.ppermute(send, "dp", moves[1]).astype(F32)).astype(BF16)
    for factor, digit, moves in steps[1:]:
        held = held.reshape(k, factor, -1, columns)
        total = lax.dynamic_index_in_dim(held, digit, axis=1, keepdims=False).astype(F32)
        for j in range(1, factor):
            sent = lax.dynamic_index_in_dim(held, digit ^ j, axis=1, keepdims=False)
            total = total + lax.ppermute(sent, "dp", moves[j]).astype(F32)
        held = total.astype(BF16)
    for factor, digit, moves in steps[::-1]:
        parts = [held] + [lax.ppermute(held, "dp", moves[j]) for j in range(1, factor)]
        stacked = jnp.stack(parts, axis=0)
        ordered = [
            lax.dynamic_index_in_dim(stacked, digit ^ a, axis=0, keepdims=False)
            for a in range(factor)
        ]
        held = jnp.stack(ordered, axis=1).reshape(k, -1, columns)
    return held.astype(F32)


def sum_small(small):
    for factor, _, moves in phases():
        terms = [small] + [lax.ppermute(small, "dp", moves[j]) for j in range(1, factor)]
        while len(terms) > 1:
            terms = [terms[i] + terms[i + 1] for i in range(0, len(terms), 2)]
        small = terms[0]
    return small


def whole(*shape):
    return pl.BlockSpec(shape, lambda *_: (0,) * len(shape))


def per_row(*shape):
    return pl.BlockSpec((1, *shape), lambda r, *_: (r,) + (0,) * len(shape))


def struct(shape, dtype):
    return jax.ShapeDtypeStruct(shape, dtype)


def params():
    return pltpu.CompilerParams(vmem_limit_bytes=VMEM_LIMIT)


def body(
    target,
    memory,
    target_segments,
    memory_segments,
    cotangent,
    self_query,
    self_key,
    self_value,
    self_output,
    relative_bias,
    self_gain,
    cross_query,
    cross_key,
    cross_value,
    cross_output,
    cross_gain,
    ffn_gain,
    ffn_in,
    ffn_out,
):
    devices = lax.axis_size("dp")
    rows, length, width = target.shape
    held = memory.shape[0]
    span = held * devices
    heads = relative_bias.shape[1]
    inner = self_query.shape[1]
    head_size = inner // heads
    hidden_width = ffn_in.shape[1]
    chunks = hidden_width // width
    count = rows * length
    stacked = heads * length
    core = (lax.axis_index("dp") % 2).astype(jnp.int32).reshape(1)
    smem = pl.BlockSpec(memory_space=pltpu.SMEM)

    outgoing = jnp.swapaxes(memory, 0, 1).reshape(devices, rows, held, width)
    mem = lax.all_to_all(outgoing, "dp", split_axis=0, concat_axis=0, tiled=True)

    gain_one = self_gain.astype(F32).reshape(1, width)
    gain_two = cross_gain.astype(F32).reshape(1, width)
    gain_three = ffn_gain.astype(F32).reshape(1, width)
    table = bucket_table(length)
    onehot = jnp.asarray(table[None, :, :] == np.arange(NB)[:, None, None], dtype=BF16)
    bias = jnp.einsum("bh,bij->hij", relative_bias, onehot, preferred_element_type=F32)
    column = target_segments.reshape(rows, length, 1)
    line = target_segments.reshape(rows, 1, length)
    mem_line = memory_segments.reshape(rows, 1, span)

    tokens = struct((count, inner), BF16)
    h1, q, k, v, p1, o1, y1, h2, cq = pl.pallas_call(
        functools.partial(self_forward_kernel, rows, length, head_size),
        out_shape=[
            tokens,
            tokens,
            tokens,
            tokens,
            struct((rows, stacked, length), BF16),
            tokens,
            struct((count, width), F32),
            tokens,
            tokens,
        ],
        compiler_params=params(),
        name="self_forward",
    )(
        target.reshape(count, width),
        column,
        line,
        bias,
        self_query,
        self_key,
        self_value,
        self_output,
        cross_query,
        gain_one,
        gain_two,
    )
    by_row = (rows, length, width)
    y1 = y1.reshape(by_row)
    cq = cq.reshape(by_row)
    mem_spec = pl.BlockSpec((devices, 1, held, width), lambda r: (0, r, 0, 0))
    square = whole(width, inner)
    token_spec = per_row(length, width)
    ck, cv, p2, o2, y2 = pl.pallas_call(
        functools.partial(cross_forward_kernel, length, head_size),
        grid=(rows,),
        in_specs=[
            token_spec,
            mem_spec,
            token_spec,
            per_row(length, 1),
            per_row(1, span),
            square,
            square,
            square,
        ],
        out_specs=[
            per_row(span, inner),
            per_row(span, inner),
            per_row(stacked, span),
            token_spec,
            token_spec,
        ],
        out_shape=[
            struct((rows, span, inner), BF16),
            struct((rows, span, inner), BF16),
            struct((rows, stacked, span), BF16),
            struct(by_row, BF16),
            struct(by_row, F32),
        ],
        compiler_params=params(),
        name="cross_forward",
    )(cq, mem, y1, column, mem_line, cross_key, cross_value, cross_output)

    half = width // 2
    full = whole(count, width)
    part_spec = pl.BlockSpec((2, 1, half, width), lambda c: (0, c, 0, 0))
    part = struct((2, chunks, half, width), BF16)
    layer_out, dy2, ffn_gain_grad, ffn_keep, ffn_send = pl.pallas_call(
        functools.partial(ffn_kernel, chunks),
        grid=(chunks,),
        in_specs=[
            smem,
            full,
            full,
            whole(1, width),
            pl.BlockSpec((width, width), lambda c: (0, c)),
            pl.BlockSpec((width, width), lambda c: (c, 0)),
        ],
        out_specs=[full, full, whole(1, width), part_spec, part_spec],
        out_shape=[
            struct((count, width), BF16),
            struct((count, width), F32),
            struct((1, width), F32),
            part,
            part,
        ],
        scratch_shapes=[
            pltpu.VMEM((count, width), BF16),
            pltpu.VMEM((count, width), F32),
            pltpu.VMEM((count, width), F32),
            pltpu.VMEM((2, width, width), F32),
        ],
        compiler_params=params(),
        name="ffn",
    )(core, y2.reshape(count, width), cotangent.reshape(count, width), gain_three, ffn_in, ffn_out)

    four = struct((4, half, width), BF16)
    four_spec = whole(4, half, width)
    mem_grad, dy1, cross_gain_grad, cross_keep, cross_send = pl.pallas_call(
        functools.partial(cross_backward_kernel, rows, length, head_size),
        grid=(rows,),
        in_specs=[
            smem,
            token_spec,
            token_spec,
            per_row(span, inner),
            per_row(span, inner),
            per_row(stacked, span),
            token_spec,
            mem_spec,
            token_spec,
            token_spec,
            whole(1, width),
            square,
            square,
            square,
            square,
        ],
        out_specs=[mem_spec, token_spec, whole(1, width), four_spec, four_spec],
        out_shape=[
            struct(mem.shape, BF16),
            struct(by_row, F32),
            struct((1, width), F32),
            four,
            four,
        ],
        scratch_shapes=[
            pltpu.VMEM((4, width, inner), F32),
            pltpu.VMEM((span, inner), BF16),
            pltpu.VMEM((span, inner), BF16),
            pltpu.VMEM((length, inner), BF16),
            pltpu.VMEM((1, width), F32),
        ],
        compiler_params=params(),
        name="cross_backward",
    )(
        core,
        dy2.reshape(by_row),
        cq,
        ck,
        cv,
        p2,
        o2,
        mem,
        h2.reshape(by_row),
        y1,
        gain_two,
        cross_query,
        cross_key,
        cross_value,
        cross_output,
    )
    returned = lax.all_to_all(mem_grad, "dp", split_axis=0, concat_axis=0, tiled=True)
    memory_grad = jnp.swapaxes(returned.reshape(devices * rows, held, width), 0, 1)

    target_grad, self_gain_grad, bias_total, self_keep, self_send = pl.pallas_call(
        functools.partial(self_backward_kernel, rows, length, head_size),
        grid=(rows,),
        in_specs=[
            smem,
            token_spec,
            token_spec,
            token_spec,
            token_spec,
            per_row(stacked, length),
            token_spec,
            token_spec,
            token_spec,
            whole(1, width),
            square,
            square,
            square,
            square,
        ],
        out_specs=[
            token_spec,
            whole(1, width),
            whole(heads, length, length),
            four_spec,
            four_spec,
        ],
        out_shape=[
            struct(by_row, BF16),
            struct((1, width), F32),
            struct((heads, length, length), F32),
            four,
            four,
        ],
        scratch_shapes=[
            pltpu.VMEM((4, width, inner), F32),
            pltpu.VMEM((length, inner), BF16),
            pltpu.VMEM((length, inner), BF16),
            pltpu.VMEM((length, inner), BF16),
            pltpu.VMEM((1, width), F32),
        ],
        compiler_params=params(),
        name="self_backward",
    )(
        core,
        dy1,
        q.reshape(by_row),
        k.reshape(by_row),
        v.reshape(by_row),
        p1,
        o1.reshape(by_row),
        h1.reshape(by_row),
        target,
        gain_one,
        self_query,
        self_key,
        self_value,
        self_output,
    )
    relative_bias_grad = jnp.einsum("hij,bij->bh", bias_total, onehot.astype(F32))

    ffn_sum = sum_blocks(
        ffn_keep.reshape(2 * chunks, half, width), ffn_send.reshape(2 * chunks, half, width)
    )
    ffn_in_grad = jnp.swapaxes(ffn_sum[:chunks], 0, 1).reshape(width, -1)
    ffn_out_grad = ffn_sum[chunks:].reshape(-1, width)
    cross_output_grad, cross_query_grad, cross_key_grad, cross_value_grad = sum_blocks(
        cross_keep, cross_send
    )
    self_output_grad, self_query_grad, self_key_grad, self_value_grad = sum_blocks(
        self_keep, self_send
    )
    flat = jnp.concatenate(
        [
            self_gain_grad.reshape(-1),
            cross_gain_grad.reshape(-1),
            ffn_gain_grad.reshape(-1),
            relative_bias_grad.reshape(-1),
        ]
    )
    size = flat.shape[0]
    flat = jnp.pad(flat, (0, -size % 1024)).reshape(-1, 128)
    flat = sum_small(flat).reshape(-1)
    return (
        layer_out.reshape(by_row),
        target_grad,
        memory_grad,
        self_query_grad,
        self_key_grad,
        self_value_grad,
        self_output_grad,
        flat[3 * width : size].reshape(relative_bias.shape),
        flat[:width],
        cross_query_grad,
        cross_key_grad,
        cross_value_grad,
        cross_output_grad,
        flat[width : 2 * width],
        flat[2 * width : 3 * width],
        ffn_in_grad,
        ffn_out_grad,
    )


def solution(mesh):
    rows3 = P("dp", None, None)
    rows2 = P("dp", None)
    in_specs = (rows3, rows3, rows2, rows2, rows3) + (P(),) * 14
    out_specs = (rows3, rows3, rows3) + (P(),) * 14
    return jax.shard_map(body, mesh=mesh, in_specs=in_specs, out_specs=out_specs, check_vma=False)
```

```python
import functools

import jax
import jax.numpy as jnp
import numpy as np
from jax import lax
from jax.experimental import pallas as pl
from jax.experimental.pallas import tpu as pltpu
from jax.sharding import PartitionSpec as P

NB = 32
MAXDIST = 128
EPS = 1e-06
GROUP = 256
CARRIED = 16
MASKED = -1000000000.0
VMEM_LIMIT = 24 * 1024 * 1024
BF16 = jnp.bfloat16
F32 = jnp.float32


def bucket_table(length):
    exact = NB // 2
    offsets = np.arange(length)[:, None] - np.arange(length)[None, :]
    distance = np.maximum(offsets, 0)
    scaled = np.log(np.maximum(distance, exact) / exact) / np.log(MAXDIST / exact) * (NB - exact)
    farther = np.minimum(exact + scaled.astype(np.int32), NB - 1)
    return np.where(distance < exact, distance, farther).astype(np.int32)


def dot_nn(left, right):
    return lax.dot_general(left, right, (((1,), (0,)), ((), ())), preferred_element_type=F32)


def dot_nt(left, right):
    return lax.dot_general(left, right, (((1,), (1,)), ((), ())), preferred_element_type=F32)


def dot_tn(left, right):
    return lax.dot_general(left, right, (((0,), (0,)), ((), ())), preferred_element_type=F32)


def norm_factor(tensor):
    return lax.rsqrt(jnp.mean(tensor * tensor, axis=-1, keepdims=True) + EPS)


def norm_backward(tensor, gain, incoming):
    factor = norm_factor(tensor)
    scaled = tensor * factor
    shaped = incoming * gain
    inner = jnp.mean(scaled * shaped, axis=-1, keepdims=True)
    return factor * (shaped - scaled * inner), incoming * scaled


def head_masks(head_size, dtype):
    lane = lax.broadcasted_iota(jnp.int32, (1, GROUP), 1)
    return [
        jnp.where(lane // head_size == h, 1.0, 0.0).astype(dtype)
        for h in range(GROUP // head_size)
    ]


def stack_heads(tensor, masks):
    return jnp.concatenate([tensor * mask for mask in masks], axis=0)


def merge_heads(stacked, masks, length):
    out = stacked[:length] * masks[0]
    for h in range(1, len(masks)):
        out = out + stacked[h * length : (h + 1) * length] * masks[h]
    return out


def row_parts(size, index):
    return pl.ds(pl.multiple_of(index * size, 16), size)


def softmax_rows(scores):
    top = jnp.max(scores, axis=-1, keepdims=True)
    grown = jnp.exp(scores - top)
    return grown * (1.0 / jnp.sum(grown, axis=-1, keepdims=True))


def self_forward_kernel(
    rows,
    length,
    head_size,
    x_ref,
    column_ref,
    line_ref,
    bias_ref,
    query_ref,
    key_ref,
    value_ref,
    output_ref,
    cross_query_ref,
    gain_one_ref,
    gain_two_ref,
    h1_ref,
    q_ref,
    k_ref,
    v_ref,
    p_ref,
    o_ref,
    y1_ref,
    h2_ref,
    cq_ref,
):
    masks = head_masks(head_size, BF16)
    masks_f = head_masks(head_size, F32)
    x = x_ref[...].astype(F32)
    h1 = (x * norm_factor(x) * gain_one_ref[...]).astype(BF16)
    h1_ref[...] = h1
    q_ref[...] = dot_nn(h1, query_ref[...]).astype(BF16)
    k_ref[...] = dot_nn(h1, key_ref[...]).astype(BF16)
    v_ref[...] = dot_nn(h1, value_ref[...]).astype(BF16)
    i = lax.broadcasted_iota(jnp.int32, (length, length), 0)
    j = lax.broadcasted_iota(jnp.int32, (length, length), 1)

    def row(r, carry):
        here = pl.ds(pl.multiple_of(r * length, 16), length)
        allowed = jnp.logical_and(j <= i, column_ref[r] == line_ref[r])
        shift = jnp.where(allowed, 0.0, MASKED)
        for g in range(q_ref.shape[1] // GROUP):
            lanes = pl.ds(g * GROUP, GROUP)
            scores = dot_nt(stack_heads(q_ref[here, lanes], masks), k_ref[here, lanes])
            probs = []
            for h in range(len(masks)):
                one = scores[h * length : (h + 1) * length]
                one = one + bias_ref[g * len(masks) + h] + shift
                probs.append(softmax_rows(one).astype(BF16))
            stacked = jnp.concatenate(probs, axis=0)
            size = stacked.shape[0]
            p_ref[r, g * size : (g + 1) * size, :] = stacked
            mixed = merge_heads(dot_nn(stacked, v_ref[here, lanes]), masks_f, length)
            o_ref[here, lanes] = mixed.astype(BF16)
        return carry

    lax.fori_loop(0, rows, row, 0)
    y1 = x + dot_nn(o_ref[...], output_ref[...])
    y1_ref[...] = y1
    h2 = (y1 * norm_factor(y1) * gain_two_ref[...]).astype(BF16)
    h2_ref[...] = h2
    cq_ref[...] = dot_nn(h2, cross_query_ref[...]).astype(BF16)


def cross_forward_kernel(
    length,
    head_size,
    cq_ref,
    mem_ref,
    y1_ref,
    column_ref,
    line_ref,
    key_ref,
    value_ref,
    output_ref,
    ck_ref,
    cv_ref,
    p_ref,
    o_ref,
    y2_ref,
):
    masks = head_masks(head_size, BF16)
    masks_f = head_masks(head_size, F32)
    mem = mem_ref[...].reshape(ck_ref.shape[1], -1)
    ck_ref[0] = dot_nn(mem, key_ref[...]).astype(BF16)
    cv_ref[0] = dot_nn(mem, value_ref[...]).astype(BF16)
    shift = jnp.where(column_ref[0] == line_ref[0], 0.0, MASKED)
    for g in range(cq_ref.shape[2] // GROUP):
        lanes = slice(g * GROUP, (g + 1) * GROUP)
        scores = dot_nt(stack_heads(cq_ref[0, :, lanes], masks), ck_ref[0, :, lanes])
        probs = []
        for h in range(len(masks)):
            one = scores[h * length : (h + 1) * length] + shift
            probs.append(softmax_rows(one).astype(BF16))
        stacked = jnp.concatenate(probs, axis=0)
        size = stacked.shape[0]
        p_ref[0, g * size : (g + 1) * size, :] = stacked
        mixed = merge_heads(dot_nn(stacked, cv_ref[0, :, lanes]), masks_f, length)
        o_ref[0, :, lanes] = mixed.astype(BF16)
    y2_ref[0] = y1_ref[0] + dot_nn(o_ref[0], output_ref[...])


def ffn_kernel(
    chunks,
    core_ref,
    y2_ref,
    cot_ref,
    gain_ref,
    in_ref,
    out_ref,
    layer_ref,
    dy2_ref,
    gain_grad_ref,
    keep_ref,
    send_ref,
    h3_ref,
    total_ref,
    back_ref,
    grad_ref,
):
    step = pl.program_id(0)

    @pl.when(step == 0)
    def _():
        y2 = y2_ref[...]
        h3_ref[...] = (y2 * norm_factor(y2) * gain_ref[...]).astype(BF16)
        total_ref[...] = y2
        back_ref[...] = jnp.zeros_like(back_ref)

    h3 = h3_ref[...]
    cot = cot_ref[...]
    act = dot_nn(h3, in_ref[...])
    square = act * act
    root = float(np.sqrt(2.0 / np.pi))
    tanh = jnp.tanh(root * act * (1.0 + 0.044715 * square))
    gate = 0.5 + 0.5 * tanh
    hidden = (act * gate).astype(BF16)
    slope = gate + (0.5 * root) * act * (1.0 - tanh * tanh) * (1.0 + 3 * 0.044715 * square)
    act_grad = (slope * dot_nt(cot, out_ref[...])).astype(BF16)
    total_ref[...] += dot_nn(hidden, out_ref[...])
    back_ref[...] += dot_nt(act_grad, in_ref[...])
    half = keep_ref.shape[2]
    mine = row_parts(half, core_ref[0])
    other = row_parts(half, 1 - core_ref[0])
    grad_ref[0] = dot_tn(h3, act_grad)
    grad_ref[1] = dot_tn(hidden, cot)
    for part in range(2):
        keep_ref[part, 0] = grad_ref[part, mine, :].astype(BF16)
        send_ref[part, 0] = grad_ref[part, other, :].astype(BF16)

    @pl.when(step == chunks - 1)
    def _():
        layer_ref[...] = total_ref[...].astype(BF16)
        grad, gain_grad = norm_backward(y2_ref[...], gain_ref[...], back_ref[...])
        dy2_ref[...] = cot_ref[...].astype(F32) + grad
        gain_grad_ref[...] = jnp.sum(gain_grad, axis=0, keepdims=True)


def cross_backward_kernel(
    length,
    head_size,
    dy2_ref,
    cq_ref,
    ck_ref,
    cv_ref,
    p_ref,
    y1_ref,
    gain_ref,
    query_ref,
    output_ref,
    dy1_ref,
    gain_grad_ref,
    dq_ref,
    dk_ref,
    dv_ref,
):
    masks = head_masks(head_size, BF16)
    masks_f = head_masks(head_size, F32)

    @pl.when(pl.program_id(0) == 0)
    def _():
        gain_grad_ref[...] = jnp.zeros_like(gain_grad_ref)

    c2 = dy2_ref[0].astype(BF16)
    do = dot_nt(c2, output_ref[...]).astype(BF16)
    for g in range(cq_ref.shape[2] // GROUP):
        lanes = slice(g * GROUP, (g + 1) * GROUP)
        queries = stack_heads(cq_ref[0, :, lanes], masks)
        outs = stack_heads(do[:, lanes], masks)
        upstream = dot_nt(outs, cv_ref[0, :, lanes])
        size = upstream.shape[0]
        probs = p_ref[0, g * size : (g + 1) * size, :]
        dv_ref[0, :, lanes] = dot_tn(probs, outs).astype(BF16)
        pieces = []
        for h in range(len(masks)):
            prob = probs[h * length : (h + 1) * length].astype(F32)
            up = upstream[h * length : (h + 1) * length]
            pieces.append((prob * (up - jnp.sum(prob * up, axis=-1, keepdims=True))).astype(BF16))
        ds = jnp.concatenate(pieces, axis=0)
        dk_ref[0, :, lanes] = dot_tn(ds, queries).astype(BF16)
        mixed = merge_heads(dot_nn(ds, ck_ref[0, :, lanes]), masks_f, length)
        dq_ref[0, :, lanes] = mixed.astype(BF16)
    back = dot_nt(dq_ref[0], query_ref[...])
    grad, gain_grad = norm_backward(y1_ref[0], gain_ref[...], back)
    dy1_ref[0] = dy2_ref[0] + grad
    gain_grad_ref[...] += jnp.sum(gain_grad, axis=0, keepdims=True)


def cross_grads_kernel(
    rows,
    core_ref,
    after_ref,
    dk_ref,
    dv_ref,
    mem_ref,
    dq_ref,
    h2_ref,
    o_ref,
    dy2_ref,
    key_ref,
    value_ref,
    mem_grad_ref,
    keep_ref,
    send_ref,
    grad_ref,
):
    step = pl.program_id(0)
    dk = dk_ref[0]
    dv = dv_ref[0]
    mem = mem_ref[...].reshape(dk.shape[0], -1)
    mem_grad = (dot_nt(dk, key_ref[...]) + dot_nt(dv, value_ref[...])).astype(BF16)
    mem_grad_ref[...] = mem_grad.reshape(mem_grad_ref.shape)

    @pl.when(step == 0)
    def _():
        grad_ref[0] = dot_tn(o_ref[...], dy2_ref[...].astype(BF16))
        grad_ref[1] = dot_tn(h2_ref[...], dq_ref[...])
        grad_ref[2] = dot_tn(mem, dk)
        grad_ref[3] = dot_tn(mem, dv)

    @pl.when(step > 0)
    def _():
        grad_ref[2] += dot_tn(mem, dk)
        grad_ref[3] += dot_tn(mem, dv)

    @pl.when(step == rows - 1)
    def _():
        write_grads(core_ref, grad_ref, [keep_ref], [send_ref])


def write_grads(core_ref, grad_ref, keeps, sends):
    half = grad_ref.shape[1] // 2
    mine = row_parts(half, core_ref[0])
    other = row_parts(half, 1 - core_ref[0])
    part = 0
    for keep_ref, send_ref in zip(keeps, sends):
        for block in range(keep_ref.shape[0] // half):
            here = slice(block * half, (block + 1) * half)
            keep_ref[here, :] = grad_ref[part, mine, :].astype(BF16)
            send_ref[here, :] = grad_ref[part, other, :].astype(BF16)
            part += 1


def self_backward_kernel(
    rows,
    length,
    head_size,
    core_ref,
    after_ref,
    dy1_ref,
    q_ref,
    k_ref,
    v_ref,
    p_ref,
    o_ref,
    h1_ref,
    x_ref,
    gain_ref,
    query_ref,
    key_ref,
    value_ref,
    output_ref,
    cross_gain_ref,
    ffn_gain_ref,
    buckets_ref,
    dx_ref,
    keep_ref,
    next_keep_ref,
    last_keep_ref,
    send_ref,
    next_send_ref,
    last_send_ref,
    grad_ref,
    c1_ref,
    dq_ref,
    dk_ref,
    dv_ref,
    gain_total_ref,
    bias_grad_ref,
):
    step = pl.program_id(0)
    masks = head_masks(head_size, BF16)
    masks_f = head_masks(head_size, F32)
    here = pl.ds(pl.multiple_of(step * length, 16), length)

    @pl.when(step == 0)
    def _():
        gain_total_ref[...] = jnp.zeros_like(gain_total_ref)
        bias_grad_ref[...] = jnp.zeros_like(bias_grad_ref)

    c1 = dy1_ref[0].astype(BF16)
    c1_ref[here, :] = c1
    do = dot_nt(c1, output_ref[...]).astype(BF16)
    for g in range(q_ref.shape[2] // GROUP):
        lanes = slice(g * GROUP, (g + 1) * GROUP)
        queries = stack_heads(q_ref[0, :, lanes], masks)
        outs = stack_heads(do[:, lanes], masks)
        upstream = dot_nt(outs, v_ref[0, :, lanes])
        size = upstream.shape[0]
        probs = p_ref[0, g * size : (g + 1) * size, :]
        dv_ref[here, lanes] = dot_tn(probs, outs).astype(BF16)
        pieces = []
        for h in range(len(masks)):
            prob = probs[h * length : (h + 1) * length].astype(F32)
            up = upstream[h * length : (h + 1) * length]
            one = (prob * (up - jnp.sum(prob * up, axis=-1, keepdims=True))).astype(BF16)
            bias_grad_ref[g * len(masks) + h] += one.astype(F32)
            pieces.append(one)
        ds = jnp.concatenate(pieces, axis=0)
        dk_ref[here, lanes] = dot_tn(ds, queries).astype(BF16)
        mixed = merge_heads(dot_nn(ds, k_ref[0, :, lanes]), masks_f, length)
        dq_ref[here, lanes] = mixed.astype(BF16)
    back = dot_nt(dq_ref[here, :], query_ref[...])
    back = back + dot_nt(dk_ref[here, :], key_ref[...])
    back = back + dot_nt(dv_ref[here, :], value_ref[...])
    grad, gain_grad = norm_backward(x_ref[0].astype(F32), gain_ref[...], back)
    dx_ref[0] = (dy1_ref[0] + grad).astype(BF16)
    gain_total_ref[...] += jnp.sum(gain_grad, axis=0, keepdims=True)

    @pl.when(step == rows - 1)
    def _():
        h1 = h1_ref[...]
        grad_ref[0] = dot_tn(o_ref[...], c1_ref[...])
        grad_ref[1] = dot_tn(h1, dq_ref[...])
        grad_ref[2] = dot_tn(h1, dk_ref[...])
        grad_ref[3] = dot_tn(h1, dv_ref[...])
        keeps = [keep_ref, next_keep_ref, last_keep_ref]
        sends = [send_ref, next_send_ref, last_send_ref]
        write_grads(core_ref, grad_ref, keeps, sends)
        heads = bias_grad_ref.shape[0]
        lanes = buckets_ref.shape[0]
        flip = jnp.where(
            lax.broadcasted_iota(jnp.int32, (length, length), 0)
            + lax.broadcasted_iota(jnp.int32, (length, length), 1)
            == length - 1,
            1.0,
            0.0,
        ).astype(BF16)
        diagonals = []
        for h in range(heads):
            flipped = dot_nn(flip, bias_grad_ref[h].astype(BF16))
            padded = jnp.concatenate([flipped, jnp.zeros((length, lanes - length), F32)], axis=1)
            skewed = pltpu.roll(padded, 0, 1, stride=1, stride_axis=0)
            diagonals.append(jnp.sum(skewed, axis=0, keepdims=True))
        sums = dot_nn(jnp.concatenate(diagonals, axis=0), buckets_ref[...])
        small = jnp.concatenate(
            [
                gain_total_ref[...],
                cross_gain_ref[...],
                ffn_gain_ref[...],
                sums,
                jnp.zeros((CARRIED - 3 - heads, sums.shape[1]), F32),
            ],
            axis=0,
        ).astype(BF16)
        for result in (last_keep_ref, last_send_ref):
            result[result.shape[0] - CARRIED :, :] = small


def factors_of(n):
    factors = []
    for factor in (2, 2, 2):
        if n % factor == 0 and n > 1:
            factors.append(factor)
            n //= factor
    while n > 1:
        factor = 4 if n % 4 == 0 else n
        factors.append(factor)
        n //= factor
    return factors


def partners(n, stride, factor, j):
    moves = []
    for i in range(n):
        digit = (i // stride) % factor
        moves.append((i, i + ((digit ^ j) - digit) * stride))
    return moves


def move_kernel(plan, operands, digits_ref, *refs):
    ins, outs = refs[:operands], refs[operands:]

    def rows_at(place, size):
        if isinstance(place, int):
            return slice(place, place + size)
        base, digit, j = place
        start = base + (digits_ref[digit] ^ j) * size
        return pl.ds(pl.multiple_of(start, 16), size)

    for out, to, sources, come, size in plan:
        if len(sources) == 1:
            rows = ins[sources[0]][rows_at(come, size), :]
        else:
            terms = [ins[source][rows_at(come, size), :].astype(F32) for source in sources]
            while len(terms) > 1:
                terms = [terms[i] + terms[i + 1] for i in range(0, len(terms), 2)]
            rows = terms[0].astype(BF16)
        outs[len(outs) - 1 - out][rows_at(to, size), :] = rows


def move_rows(plan, sizes, operands, digits, after):
    columns = operands[0].shape[1]
    vmem = pl.BlockSpec(memory_space=pltpu.VMEM)
    results = pl.pallas_call(
        functools.partial(move_kernel, plan, len(operands)),
        in_specs=[pl.BlockSpec(memory_space=pltpu.SMEM)]
        + [vmem] * len(operands)
        + [pl.BlockSpec(memory_space=pl.ANY)] * len(after),
        out_specs=[vmem] * len(sizes),
        out_shape=[struct((size, columns), BF16) for size in sizes[::-1]],
        compiler_params=params(),
        cost_estimate=cost(0, 4 * sum(sizes) * columns),
        name="move_rows",
    )(digits, *operands, *after)
    return results[::-1]


def unpack_kernel(layout, half, core_ref, own_ref, other_ref, *refs):
    outs = refs[-1 - max(entry[0] for entry in layout) :]
    width = own_ref.shape[1]
    start = 0
    for out, row, column, offset, size in layout:
        columns = pl.ds(column * width, width)
        for ref, core in ((own_ref, core_ref[0]), (other_ref, 1 - core_ref[0])):
            first = pl.multiple_of(row * 2 * half + core * half + offset, 16)
            rows = ref[start : start + size, :].astype(F32)
            outs[out][pl.ds(first, size), columns] = rows
        start += size


def unpack(own, other, core, layout, half, shapes, after):
    vmem = pl.BlockSpec(memory_space=pltpu.VMEM)
    return pl.pallas_call(
        functools.partial(unpack_kernel, layout, half),
        in_specs=[pl.BlockSpec(memory_space=pltpu.SMEM), vmem, vmem]
        + [pl.BlockSpec(memory_space=pl.ANY)] * len(after),
        out_specs=[vmem] * len(shapes),
        out_shape=[struct(shape, F32) for shape in shapes],
        compiler_params=params(),
        cost_estimate=cost(0, 12 * own.shape[0] * own.shape[1]),
        name="unpack",
    )(core, own, other, *after)


def swap_cores(rows):
    n = lax.axis_size("dp")
    return lax.ppermute(rows, "dp", [(i, i ^ 1) for i in range(n)])


class Bucket:
    def __init__(self, lanes, carried=0):
        n, me = lax.axis_size("dp"), lax.axis_index("dp")
        self.carried = carried
        self.factors = factors_of(n)
        self.moves, digits, stride = [], [], 1
        for factor in self.factors:
            digits.append((me // stride) % factor)
            self.moves.append([partners(n, stride, factor, j) for j in range(factor)])
            stride *= factor
        self.digits = jnp.stack(digits).astype(jnp.int32)
        self.lanes = lanes

    def send(self, rows, phase, j):
        return lax.ppermute(rows, "dp", self.moves[phase][j])

    def first(self, *after):
        operands, plan, sizes = [], [], []
        for lane, chunks in enumerate(self.lanes):
            start = 0
            for mine, theirs, base, rows in chunks:
                at = []
                for operand in (mine, theirs):
                    if not any(operand is other for other in operands):
                        operands.append(operand)
                    at += [k for k, other in enumerate(operands) if other is operand]
                for j in range(2):
                    plan.append((2 * lane + j, start, at, (base, 1 + lane, j), rows // 2))
                start += rows // 2
            sizes += [start, start]
        if self.carried:
            plan += [(2 + j, sizes[2], at, base + rows, self.carried) for j in range(2)]
            sizes[2] += self.carried
            sizes[3] += self.carried
        own, out, own_too, out_too = move_rows(plan, sizes, operands, self.digits, after)
        self.size = sizes[0]
        self.terms = [[own, self.send(out, 1, 1)], [own_too, self.send(out_too, 2, 1)]]
        return own

    def second(self, *after):
        size = self.size = self.size // 2
        operands = self.terms[0] + self.terms[1]
        plan = []
        for lane in range(2):
            at = [2 * lane, 2 * lane + 1]
            for j in range(2):
                plan.append((2 * lane + j, 0, at, (0, 2 - lane, j), size))
        sizes = [size] * 2 + [size + self.carried] * 2
        if self.carried:
            plan += [(2 + j, size, [2, 3], 2 * size, self.carried) for j in range(2)]
        own, out, own_too, out_too = move_rows(plan, sizes, operands, self.digits, after)
        self.terms = [[own, self.send(out, 2, 1)], [own_too, self.send(out_too, 1, 1)]]
        self.joined = False
        return own

    def third(self, phase, *after):
        parts = self.factors[phase] if phase < len(self.factors) else 1
        size = self.size // parts
        plan = []
        for j in range(parts):
            for lane in range(2):
                if self.joined:
                    at, base = list(range(len(self.terms))), lane * self.size
                else:
                    at, base = [2 * lane, 2 * lane + 1], 0
                come = (base, phase, j) if parts > 1 else base
                plan.append((j, lane * size, at, come, size))
            if self.carried:
                base = 2 * self.size if self.joined else self.size
                plan.append((j, 2 * size, at, base, self.carried))
        operands = self.terms if self.joined else self.terms[0] + self.terms[1]
        total = 2 * size + self.carried
        own, *others = move_rows(plan, [total] * parts, operands, self.digits, after)
        self.size, self.joined = size, True
        if parts > 1:
            self.terms = [own] + [self.send(o, phase, j + 1) for j, o in enumerate(others)]
        else:
            self.sums = own[2 * size :].astype(F32)
            self.pieces = [own[: 2 * size] if self.carried else own]
            self.spread(phase - 1)
        return own

    def spread(self, phase):
        held = self.pieces[0]
        self.pieces += [self.send(held, phase, j) for j in range(1, self.factors[phase])]

    def back(self, phase, *after):
        parts, size = self.factors[phase], self.size
        plan = []
        for j in range(parts):
            for lane in range(2):
                out = 0 if phase > 3 else lane
                base = lane * size * parts if phase > 3 else 0
                plan.append((out, (base, phase, j), [j], lane * size, size))
        self.size = size * parts
        sizes = [2 * self.size] if phase > 3 else [self.size] * 2
        held = move_rows(plan, sizes, self.pieces, self.digits, after)
        if phase > 3:
            self.pieces = list(held)
            self.spread(phase - 1)
        else:
            self.pieces = [held[0], self.send(held[0], 2, 1), held[1], self.send(held[1], 1, 1)]
        return held[0]

    def back_second(self, *after):
        size = self.size
        plan = [
            (lane, (0, 2 - lane, j), [2 * lane + j], 0, size) for lane in range(2) for j in range(2)
        ]
        self.size = 2 * size
        held = move_rows(plan, [self.size] * 2, self.pieces, self.digits, after)
        self.pieces = [held[0], self.send(held[0], 1, 1), held[1], self.send(held[1], 2, 1)]
        return held[0]

    def back_first(self, *after):
        size = self.size
        plan = [
            (0, (2 * lane * size, 1 + lane, j), [2 * lane + j], 0, size)
            for lane in range(2)
            for j in range(2)
        ]
        (held,) = move_rows(plan, [4 * size], self.pieces, self.digits, after)
        self.pieces = [held, self.send(held, 0, 1)]
        return held

    def finish(self, core, layout, half, shapes, *after):
        return unpack(*self.pieces, core, layout, half, shapes, after)


def cost(flops, nbytes, transcendentals=0):
    return pl.CostEstimate(
        flops=int(flops), bytes_accessed=int(nbytes), transcendentals=int(transcendentals)
    )


def whole(*shape):
    return pl.BlockSpec(shape, lambda *_: (0,) * len(shape))


def per_row(*shape):
    return pl.BlockSpec((1, *shape), lambda r, *_: (r,) + (0,) * len(shape))


def struct(shape, dtype):
    return jax.ShapeDtypeStruct(shape, dtype)


def params():
    return pltpu.CompilerParams(vmem_limit_bytes=VMEM_LIMIT)


def body(
    target,
    memory,
    target_segments,
    memory_segments,
    cotangent,
    self_query,
    self_key,
    self_value,
    self_output,
    relative_bias,
    self_gain,
    cross_query,
    cross_key,
    cross_value,
    cross_output,
    cross_gain,
    ffn_gain,
    ffn_in,
    ffn_out,
):
    devices = lax.axis_size("dp")
    rows, length, width = target.shape
    held = memory.shape[0]
    span = held * devices
    heads = relative_bias.shape[1]
    inner = self_query.shape[1]
    head_size = inner // heads
    hidden_width = ffn_in.shape[1]
    chunks = hidden_width // width
    count = rows * length
    stacked = heads * length
    core = (lax.axis_index("dp") % 2).astype(jnp.int32).reshape(1)
    smem = pl.BlockSpec(memory_space=pltpu.SMEM)

    outgoing = jnp.swapaxes(memory, 0, 1).reshape(devices, rows, held, width)
    mem = lax.all_to_all(outgoing, "dp", split_axis=0, concat_axis=0, tiled=True)

    gain_one = self_gain.astype(F32).reshape(1, width)
    gain_two = cross_gain.astype(F32).reshape(1, width)
    gain_three = ffn_gain.astype(F32).reshape(1, width)
    table = bucket_table(length)
    onehot = jnp.asarray(table[None, :, :] == np.arange(NB)[:, None, None], dtype=BF16)
    bias = jnp.einsum("bh,bij->hij", relative_bias, onehot, preferred_element_type=F32)
    column = target_segments.reshape(rows, length, 1)
    line = target_segments.reshape(rows, 1, length)
    mem_line = memory_segments.reshape(rows, 1, span)

    tokens = struct((count, inner), BF16)
    h1, q, k, v, p1, o1, y1, h2, cq = pl.pallas_call(
        functools.partial(self_forward_kernel, rows, length, head_size),
        out_shape=[
            tokens,
            tokens,
            tokens,
            tokens,
            struct((rows, stacked, length), BF16),
            tokens,
            struct((count, width), F32),
            tokens,
            tokens,
        ],
        compiler_params=params(),
        cost_estimate=cost(2 * count * width * inner * 5, 12 * count * width),
        name="self_forward",
    )(
        target.reshape(count, width),
        column,
        line,
        bias,
        self_query,
        self_key,
        self_value,
        self_output,
        cross_query,
        gain_one,
        gain_two,
    )
    by_row = (rows, length, width)
    y1 = y1.reshape(by_row)
    cq = cq.reshape(by_row)
    h2 = h2.reshape(by_row)
    h1, q, k, v, o1 = (a.reshape(by_row) for a in (h1, q, k, v, o1))
    half = width // 2
    square = whole(width, inner)
    line_spec = whole(1, width)
    any_spec = pl.BlockSpec(memory_space=pl.ANY)
    here = per_row(length, width)
    mem_spec = pl.BlockSpec((devices, 1, held, width), lambda r: (0, r, 0, 0))
    keys_spec = per_row(span, inner)
    keys = struct((rows, span, inner), BF16)
    ck, cv, p2, o2, y2 = pl.pallas_call(
        functools.partial(cross_forward_kernel, length, head_size),
        grid=(rows,),
        in_specs=[
            here,
            mem_spec,
            here,
            per_row(length, 1),
            per_row(1, span),
            square,
            square,
            square,
        ],
        out_specs=[keys_spec, keys_spec, per_row(stacked, span), here, here],
        out_shape=[
            keys,
            keys,
            struct((rows, stacked, span), BF16),
            struct(by_row, BF16),
            struct(by_row, F32),
        ],
        compiler_params=params(),
        cost_estimate=cost(4 * rows * span * width * inner, 10 * rows * span * width),
        name="cross_forward",
    )(cq, mem, y1, column, mem_line, cross_key, cross_value, cross_output)

    full = whole(count, width)
    part_spec = pl.BlockSpec((2, 1, half, width), lambda c: (0, c, 0, 0))
    part = struct((2, chunks, half, width), BF16)
    layer_out, dy2, ffn_gain_grad, ffn_keep, ffn_send = pl.pallas_call(
        functools.partial(ffn_kernel, chunks),
        grid=(chunks,),
        in_specs=[
            smem,
            full,
            full,
            line_spec,
            pl.BlockSpec((width, width), lambda c: (0, c)),
            pl.BlockSpec((width, width), lambda c: (c, 0)),
        ],
        out_specs=[full, full, line_spec, part_spec, part_spec],
        out_shape=[
            struct((count, width), BF16),
            struct((count, width), F32),
            struct((1, width), F32),
            part,
            part,
        ],
        scratch_shapes=[
            pltpu.VMEM((count, width), BF16),
            pltpu.VMEM((count, width), F32),
            pltpu.VMEM((count, width), F32),
            pltpu.VMEM((2, width, width), F32),
        ],
        compiler_params=params(),
        cost_estimate=cost(12 * count * width * hidden_width, 10 * width * hidden_width),
        name="ffn",
    )(core, y2.reshape(count, width), cotangent.reshape(count, width), gain_three, ffn_in, ffn_out)

    ffn_keep = ffn_keep.reshape(-1, width)
    ffn_other = swap_cores(ffn_send.reshape(-1, width))
    rows_each = chunks * half
    ffn_sum = Bucket([[(ffn_keep, ffn_other, lane * rows_each, rows_each)] for lane in range(2)])

    dy1, cross_gain_grad, dq, dk, dv = pl.pallas_call(
        functools.partial(cross_backward_kernel, length, head_size),
        grid=(rows,),
        in_specs=[
            here,
            here,
            keys_spec,
            keys_spec,
            per_row(stacked, span),
            here,
            line_spec,
            square,
            square,
        ],
        out_specs=[here, line_spec, here, keys_spec, keys_spec],
        out_shape=[
            struct(by_row, F32),
            struct((1, width), F32),
            struct(by_row, BF16),
            keys,
            keys,
        ],
        compiler_params=params(),
        cost_estimate=cost(4 * rows * span * width * inner, 10 * rows * span * width),
        name="cross_backward",
    )(dy2.reshape(by_row), cq, ck, cv, p2, y1, gain_two, cross_query, cross_output)
    passed = ffn_sum.first(dy1)

    halves = struct((4 * half, width), BF16)
    halves_spec = whole(4 * half, width)
    mem_grad, cross_keep, cross_send = pl.pallas_call(
        functools.partial(cross_grads_kernel, rows),
        grid=(rows,),
        in_specs=[
            smem,
            any_spec,
            keys_spec,
            keys_spec,
            mem_spec,
            full,
            full,
            full,
            full,
            square,
            square,
        ],
        out_specs=[mem_spec, halves_spec, halves_spec],
        out_shape=[struct(mem.shape, BF16), halves, halves],
        scratch_shapes=[pltpu.VMEM((4, width, inner), F32)],
        compiler_params=params(),
        cost_estimate=cost(4 * rows * span * width * inner, 10 * rows * span * width),
        name="cross_grads",
    )(
        core,
        passed,
        dk,
        dv,
        mem,
        dq.reshape(count, inner),
        h2.reshape(count, width),
        o2.reshape(count, inner),
        dy2,
        cross_key,
        cross_value,
    )
    returned = lax.all_to_all(mem_grad, "dp", split_axis=0, concat_axis=0, tiled=True)
    cross_other = swap_cores(cross_send)

    lanes = 256
    buckets = np.zeros((lanes, width), np.float32)
    for n in range(length):
        buckets[length - 1 - n, table[n, 0]] = 1.0
    packed = [struct((size, width), BF16) for size in (2 * half, half, half + CARRIED)] * 2
    target_grad, *self_halves = pl.pallas_call(
        functools.partial(self_backward_kernel, rows, length, head_size),
        grid=(rows,),
        in_specs=[
            smem,
            any_spec,
            here,
            here,
            here,
            here,
            per_row(stacked, length),
            full,
            full,
            here,
            line_spec,
            square,
            square,
            square,
            square,
            line_spec,
            line_spec,
            whole(lanes, width),
        ],
        out_specs=[here] + [whole(*one.shape) for one in packed],
        out_shape=[struct(by_row, BF16)] + packed,
        scratch_shapes=[
            pltpu.VMEM((4, width, inner), F32),
            pltpu.VMEM((count, width), BF16),
            pltpu.VMEM((count, inner), BF16),
            pltpu.VMEM((count, inner), BF16),
            pltpu.VMEM((count, inner), BF16),
            pltpu.VMEM((1, width), F32),
            pltpu.VMEM((heads, length, length), F32),
        ],
        compiler_params=params(),
        cost_estimate=cost(2 * count * width * inner * 12, 12 * count * width),
        name="self_backward",
    )(
        core,
        mem_grad,
        dy1,
        q,
        k,
        v,
        p1,
        o1.reshape(count, inner),
        h1.reshape(count, width),
        target,
        gain_one,
        self_query,
        self_key,
        self_value,
        self_output,
        cross_gain_grad,
        ffn_gain_grad,
        jnp.asarray(buckets),
    )
    attention_sum = Bucket(
        [
            [(cross_keep, cross_other, 0, 4 * half)],
            [
                (keep, swap_cores(send), 0, blocks * half)
                for blocks, keep, send in zip((2, 1, 1), self_halves[:3], self_halves[3:])
            ],
        ],
        CARRIED,
    )

    phases = len(ffn_sum.factors)
    passed = ffn_sum.second(target_grad)
    passed = attention_sum.first(passed)
    passed = ffn_sum.third(3, passed)
    passed = attention_sum.second(passed)
    for phase in range(4, phases + 1):
        passed = ffn_sum.third(phase, passed)
        passed = attention_sum.third(phase - 1, passed)
    for phase in range(phases - 1, 2, -1):
        passed = ffn_sum.back(phase, passed)
        if phase == phases - 1:
            passed = attention_sum.third(phases, passed)
        else:
            passed = attention_sum.back(phase + 1, passed)
    passed = ffn_sum.back_second(passed)
    passed = attention_sum.back(3, passed, returned)
    passed = ffn_sum.back_first(passed)
    passed = attention_sum.back_second(passed)
    ffn_layout = [(0, 0, c, 0, half) for c in range(chunks)]
    ffn_layout += [(1, c, 0, 0, half) for c in range(chunks)]
    ffn_in_grad, ffn_out_grad = ffn_sum.finish(
        core, ffn_layout, half, [(width, hidden_width), (hidden_width, width)], passed
    )
    memory_grad = jnp.swapaxes(returned.reshape(devices * rows, held, width), 0, 1)
    small = attention_sum.sums
    passed = attention_sum.back_first(ffn_in_grad, memory_grad, small)
    attention_layout = [(part, 0, 0, 0, half) for part in range(4)]
    for part in range(2):
        attention_layout += [(4 + part, 0, 0, 0, half)]
        attention_layout += [(out, 0, 0, part * half // 2, half // 2) for out in (6, 7)]
    (
        cross_output_grad,
        cross_query_grad,
        cross_key_grad,
        cross_value_grad,
        self_output_grad,
        self_query_grad,
        self_key_grad,
        self_value_grad,
    ) = attention_sum.finish(core, attention_layout, half, [(width, inner)] * 8)
    return (
        layer_out.reshape(by_row),
        target_grad,
        memory_grad,
        self_query_grad,
        self_key_grad,
        self_value_grad,
        self_output_grad,
        small[3 : 3 + heads, :NB].T,
        small[0],
        cross_query_grad,
        cross_key_grad,
        cross_value_grad,
        cross_output_grad,
        small[1],
        small[2],
        ffn_in_grad,
        ffn_out_grad,
    )


def solution(mesh):
    rows3 = P("dp", None, None)
    rows2 = P("dp", None)
    in_specs = (rows3, rows3, rows2, rows2, rows3) + (P(),) * 14
    out_specs = (rows3, rows3, rows3) + (P(),) * 14
    return jax.shard_map(body, mesh=mesh, in_specs=in_specs, out_specs=out_specs, check_vma=False)
```

```python
import functools

import jax
import jax.numpy as jnp
import numpy as np
from jax import lax
from jax.experimental import pallas as pl
from jax.experimental.pallas import tpu as pltpu
from jax.sharding import PartitionSpec as P

NB = 32
MAXDIST = 128
EPS = 1e-06
GROUP = 256
CARRIED = 16
MASKED = -1000000000.0
VMEM_LIMIT = 56 * 1024 * 1024
MOVE_LIMIT = 16 * 1024 * 1024
BF16 = jnp.bfloat16
F32 = jnp.float32


def bucket_table(length):
    exact = NB // 2
    offsets = np.arange(length)[:, None] - np.arange(length)[None, :]
    distance = np.maximum(offsets, 0)
    scaled = np.log(np.maximum(distance, exact) / exact) / np.log(MAXDIST / exact) * (NB - exact)
    farther = np.minimum(exact + scaled.astype(np.int32), NB - 1)
    return np.where(distance < exact, distance, farther).astype(np.int32)


def dot_nn(left, right):
    return lax.dot_general(left, right, (((1,), (0,)), ((), ())), preferred_element_type=F32)


def dot_nt(left, right):
    return lax.dot_general(left, right, (((1,), (1,)), ((), ())), preferred_element_type=F32)


def dot_tn(left, right):
    return lax.dot_general(left, right, (((0,), (0,)), ((), ())), preferred_element_type=F32)


def norm_factor(tensor):
    return lax.rsqrt(jnp.mean(tensor * tensor, axis=-1, keepdims=True) + EPS)


def norm_backward(tensor, gain, incoming):
    factor = norm_factor(tensor)
    scaled = tensor * factor
    shaped = incoming * gain
    inner = jnp.mean(scaled * shaped, axis=-1, keepdims=True)
    return factor * (shaped - scaled * inner), incoming * scaled


def head_masks(head_size, dtype):
    lane = lax.broadcasted_iota(jnp.int32, (1, GROUP), 1)
    return [
        jnp.where(lane // head_size == h, 1.0, 0.0).astype(dtype)
        for h in range(GROUP // head_size)
    ]


def stack_heads(tensor, masks):
    return jnp.concatenate([tensor * mask for mask in masks], axis=0)


def merge_heads(stacked, masks, length):
    out = stacked[:length] * masks[0]
    for h in range(1, len(masks)):
        out = out + stacked[h * length : (h + 1) * length] * masks[h]
    return out


def row_parts(size, index):
    return pl.ds(pl.multiple_of(index * size, 16), size)


def softmax_rows(scores):
    top = jnp.max(scores, axis=-1, keepdims=True)
    grown = jnp.exp(scores - top)
    return grown * (1.0 / jnp.sum(grown, axis=-1, keepdims=True))


def self_forward_kernel(
    rows,
    length,
    head_size,
    x_ref,
    column_ref,
    line_ref,
    bias_ref,
    query_ref,
    key_ref,
    value_ref,
    output_ref,
    cross_query_ref,
    gain_one_ref,
    gain_two_ref,
    h1_ref,
    q_ref,
    k_ref,
    v_ref,
    p_ref,
    o_ref,
    y1_ref,
    h2_ref,
    cq_ref,
):
    masks = head_masks(head_size, BF16)
    masks_f = head_masks(head_size, F32)
    x = x_ref[...].astype(F32)
    h1 = (x * norm_factor(x) * gain_one_ref[...]).astype(BF16)
    h1_ref[...] = h1
    q_ref[...] = dot_nn(h1, query_ref[...]).astype(BF16)
    k_ref[...] = dot_nn(h1, key_ref[...]).astype(BF16)
    v_ref[...] = dot_nn(h1, value_ref[...]).astype(BF16)
    i = lax.broadcasted_iota(jnp.int32, (length, length), 0)
    j = lax.broadcasted_iota(jnp.int32, (length, length), 1)

    def row(r, carry):
        here = pl.ds(pl.multiple_of(r * length, 16), length)
        allowed = jnp.logical_and(j <= i, column_ref[r] == line_ref[r])
        shift = jnp.where(allowed, 0.0, MASKED)
        for g in range(q_ref.shape[1] // GROUP):
            lanes = pl.ds(g * GROUP, GROUP)
            scores = dot_nt(stack_heads(q_ref[here, lanes], masks), k_ref[here, lanes])
            probs = []
            for h in range(len(masks)):
                one = scores[h * length : (h + 1) * length]
                one = one + bias_ref[g * len(masks) + h] + shift
                probs.append(softmax_rows(one).astype(BF16))
            stacked = jnp.concatenate(probs, axis=0)
            size = stacked.shape[0]
            p_ref[r, g * size : (g + 1) * size, :] = stacked
            mixed = merge_heads(dot_nn(stacked, v_ref[here, lanes]), masks_f, length)
            o_ref[here, lanes] = mixed.astype(BF16)
        return carry

    lax.fori_loop(0, rows, row, 0)
    y1 = x + dot_nn(o_ref[...], output_ref[...])
    y1_ref[...] = y1
    h2 = (y1 * norm_factor(y1) * gain_two_ref[...]).astype(BF16)
    h2_ref[...] = h2
    cq_ref[...] = dot_nn(h2, cross_query_ref[...]).astype(BF16)


def cross_forward_kernel(
    length,
    head_size,
    cq_ref,
    mem_ref,
    y1_ref,
    column_ref,
    line_ref,
    key_ref,
    value_ref,
    output_ref,
    ck_ref,
    cv_ref,
    p_ref,
    o_ref,
    y2_ref,
):
    masks = head_masks(head_size, BF16)
    masks_f = head_masks(head_size, F32)
    mem = mem_ref[...].reshape(ck_ref.shape[1], -1)
    ck_ref[0] = dot_nn(mem, key_ref[...]).astype(BF16)
    cv_ref[0] = dot_nn(mem, value_ref[...]).astype(BF16)
    shift = jnp.where(column_ref[0] == line_ref[0], 0.0, MASKED)
    for g in range(cq_ref.shape[2] // GROUP):
        lanes = slice(g * GROUP, (g + 1) * GROUP)
        scores = dot_nt(stack_heads(cq_ref[0, :, lanes], masks), ck_ref[0, :, lanes])
        probs = []
        for h in range(len(masks)):
            one = scores[h * length : (h + 1) * length] + shift
            probs.append(softmax_rows(one).astype(BF16))
        stacked = jnp.concatenate(probs, axis=0)
        size = stacked.shape[0]
        p_ref[0, g * size : (g + 1) * size, :] = stacked
        mixed = merge_heads(dot_nn(stacked, cv_ref[0, :, lanes]), masks_f, length)
        o_ref[0, :, lanes] = mixed.astype(BF16)
    y2_ref[0] = y1_ref[0] + dot_nn(o_ref[0], output_ref[...])


def ffn_kernel(
    chunks,
    core_ref,
    y2_ref,
    cot_ref,
    gain_ref,
    in_ref,
    out_ref,
    layer_ref,
    dy2_ref,
    gain_grad_ref,
    keep_ref,
    send_ref,
    h3_ref,
    total_ref,
    back_ref,
    grad_ref,
):
    step = pl.program_id(0)

    @pl.when(step == 0)
    def _():
        y2 = y2_ref[...]
        h3_ref[...] = (y2 * norm_factor(y2) * gain_ref[...]).astype(BF16)
        total_ref[...] = y2
        back_ref[...] = jnp.zeros_like(back_ref)

    h3 = h3_ref[...]
    cot = cot_ref[...]
    act = dot_nn(h3, in_ref[...])
    square = act * act
    root = float(np.sqrt(2.0 / np.pi))
    tanh = jnp.tanh(root * act * (1.0 + 0.044715 * square))
    gate = 0.5 + 0.5 * tanh
    hidden = (act * gate).astype(BF16)
    slope = gate + (0.5 * root) * act * (1.0 - tanh * tanh) * (1.0 + 3 * 0.044715 * square)
    act_grad = (slope * dot_nt(cot, out_ref[...])).astype(BF16)
    total_ref[...] += dot_nn(hidden, out_ref[...])
    back_ref[...] += dot_nt(act_grad, in_ref[...])
    half = keep_ref.shape[2]
    mine = row_parts(half, core_ref[0])
    other = row_parts(half, 1 - core_ref[0])
    grad_ref[0] = dot_tn(h3, act_grad)
    grad_ref[1] = dot_tn(hidden, cot)
    for part in range(2):
        keep_ref[part, 0] = grad_ref[part, mine, :].astype(BF16)
        send_ref[part, 0] = grad_ref[part, other, :].astype(BF16)

    @pl.when(step == chunks - 1)
    def _():
        layer_ref[...] = total_ref[...].astype(BF16)
        grad, gain_grad = norm_backward(y2_ref[...], gain_ref[...], back_ref[...])
        dy2_ref[...] = cot_ref[...].astype(F32) + grad
        gain_grad_ref[...] = jnp.sum(gain_grad, axis=0, keepdims=True)


def cross_backward_kernel(
    length,
    head_size,
    dy2_ref,
    cq_ref,
    ck_ref,
    cv_ref,
    p_ref,
    y1_ref,
    gain_ref,
    query_ref,
    key_ref,
    value_ref,
    output_ref,
    dy1_ref,
    gain_grad_ref,
    mem_grad_ref,
    dq_ref,
    dk_ref,
    dv_ref,
):
    masks = head_masks(head_size, BF16)
    masks_f = head_masks(head_size, F32)

    @pl.when(pl.program_id(0) == 0)
    def _():
        gain_grad_ref[...] = jnp.zeros_like(gain_grad_ref)

    c2 = dy2_ref[0].astype(BF16)
    do = dot_nt(c2, output_ref[...]).astype(BF16)
    for g in range(cq_ref.shape[2] // GROUP):
        lanes = slice(g * GROUP, (g + 1) * GROUP)
        queries = stack_heads(cq_ref[0, :, lanes], masks)
        outs = stack_heads(do[:, lanes], masks)
        upstream = dot_nt(outs, cv_ref[0, :, lanes])
        size = upstream.shape[0]
        probs = p_ref[0, g * size : (g + 1) * size, :]
        dv_ref[0, :, lanes] = dot_tn(probs, outs).astype(BF16)
        pieces = []
        for h in range(len(masks)):
            prob = probs[h * length : (h + 1) * length].astype(F32)
            up = upstream[h * length : (h + 1) * length]
            pieces.append((prob * (up - jnp.sum(prob * up, axis=-1, keepdims=True))).astype(BF16))
        ds = jnp.concatenate(pieces, axis=0)
        dk_ref[0, :, lanes] = dot_tn(ds, queries).astype(BF16)
        mixed = merge_heads(dot_nn(ds, ck_ref[0, :, lanes]), masks_f, length)
        dq_ref[0, :, lanes] = mixed.astype(BF16)
    mem_grad = dot_nt(dk_ref[0], key_ref[...]) + dot_nt(dv_ref[0], value_ref[...])
    mem_grad_ref[...] = mem_grad.astype(BF16).reshape(mem_grad_ref.shape)
    back = dot_nt(dq_ref[0], query_ref[...])
    grad, gain_grad = norm_backward(y1_ref[0], gain_ref[...], back)
    dy1_ref[0] = dy2_ref[0] + grad
    gain_grad_ref[...] += jnp.sum(gain_grad, axis=0, keepdims=True)


def cross_grads_kernel(
    rows,
    core_ref,
    after_ref,
    dk_ref,
    dv_ref,
    mem_ref,
    dq_ref,
    h2_ref,
    o_ref,
    dy2_ref,
    keep_ref,
    send_ref,
    grad_ref,
):
    step = pl.program_id(0)
    mem = mem_ref[...].reshape(dk_ref.shape[1], -1)

    @pl.when(step == 0)
    def _():
        grad_ref[0] = dot_tn(o_ref[...], dy2_ref[...].astype(BF16))
        grad_ref[1] = dot_tn(h2_ref[...], dq_ref[...])
        grad_ref[2] = dot_tn(mem, dk_ref[0])
        grad_ref[3] = dot_tn(mem, dv_ref[0])

    @pl.when(step > 0)
    def _():
        grad_ref[2] += dot_tn(mem, dk_ref[0])
        grad_ref[3] += dot_tn(mem, dv_ref[0])

    @pl.when(step == rows - 1)
    def _():
        write_grads(core_ref, grad_ref, keep_ref, send_ref)


def write_grads(core_ref, grad_ref, keep_ref, send_ref):
    half = grad_ref.shape[1] // 2
    mine = row_parts(half, core_ref[0])
    other = row_parts(half, 1 - core_ref[0])
    for part in range(grad_ref.shape[0]):
        here = slice(part * half, (part + 1) * half)
        keep_ref[here, :] = grad_ref[part, mine, :].astype(BF16)
        send_ref[here, :] = grad_ref[part, other, :].astype(BF16)


def self_backward_kernel(
    rows,
    length,
    head_size,
    core_ref,
    after_ref,
    dy1_ref,
    q_ref,
    k_ref,
    v_ref,
    p_ref,
    o_ref,
    h1_ref,
    x_ref,
    gain_ref,
    query_ref,
    key_ref,
    value_ref,
    output_ref,
    cross_gain_ref,
    ffn_gain_ref,
    buckets_ref,
    dx_ref,
    keep_ref,
    send_ref,
    grad_ref,
    c1_ref,
    dq_ref,
    dk_ref,
    dv_ref,
    gain_total_ref,
    bias_grad_ref,
):
    step = pl.program_id(0)
    masks = head_masks(head_size, BF16)
    masks_f = head_masks(head_size, F32)
    here = pl.ds(pl.multiple_of(step * length, 16), length)

    @pl.when(step == 0)
    def _():
        gain_total_ref[...] = jnp.zeros_like(gain_total_ref)
        bias_grad_ref[...] = jnp.zeros_like(bias_grad_ref)

    c1 = dy1_ref[0].astype(BF16)
    c1_ref[here, :] = c1
    do = dot_nt(c1, output_ref[...]).astype(BF16)
    for g in range(q_ref.shape[2] // GROUP):
        lanes = slice(g * GROUP, (g + 1) * GROUP)
        queries = stack_heads(q_ref[0, :, lanes], masks)
        outs = stack_heads(do[:, lanes], masks)
        upstream = dot_nt(outs, v_ref[0, :, lanes])
        size = upstream.shape[0]
        probs = p_ref[0, g * size : (g + 1) * size, :]
        dv_ref[here, lanes] = dot_tn(probs, outs).astype(BF16)
        pieces = []
        for h in range(len(masks)):
            prob = probs[h * length : (h + 1) * length].astype(F32)
            up = upstream[h * length : (h + 1) * length]
            one = (prob * (up - jnp.sum(prob * up, axis=-1, keepdims=True))).astype(BF16)
            bias_grad_ref[g * len(masks) + h] += one.astype(F32)
            pieces.append(one)
        ds = jnp.concatenate(pieces, axis=0)
        dk_ref[here, lanes] = dot_tn(ds, queries).astype(BF16)
        mixed = merge_heads(dot_nn(ds, k_ref[0, :, lanes]), masks_f, length)
        dq_ref[here, lanes] = mixed.astype(BF16)
    back = dot_nt(dq_ref[here, :], query_ref[...])
    back = back + dot_nt(dk_ref[here, :], key_ref[...])
    back = back + dot_nt(dv_ref[here, :], value_ref[...])
    grad, gain_grad = norm_backward(x_ref[0].astype(F32), gain_ref[...], back)
    dx_ref[0] = (dy1_ref[0] + grad).astype(BF16)
    gain_total_ref[...] += jnp.sum(gain_grad, axis=0, keepdims=True)

    @pl.when(step == rows - 1)
    def _():
        h1 = h1_ref[...]
        grad_ref[0] = dot_tn(o_ref[...], c1_ref[...])
        grad_ref[1] = dot_tn(h1, dq_ref[...])
        grad_ref[2] = dot_tn(h1, dk_ref[...])
        grad_ref[3] = dot_tn(h1, dv_ref[...])
        write_grads(core_ref, grad_ref, keep_ref, send_ref)
        heads = bias_grad_ref.shape[0]
        lanes = buckets_ref.shape[0]
        flip = jnp.where(
            lax.broadcasted_iota(jnp.int32, (length, length), 0)
            + lax.broadcasted_iota(jnp.int32, (length, length), 1)
            == length - 1,
            1.0,
            0.0,
        ).astype(BF16)
        diagonals = []
        for h in range(heads):
            flipped = dot_nn(flip, bias_grad_ref[h].astype(BF16))
            padded = jnp.concatenate([flipped, jnp.zeros((length, lanes - length), F32)], axis=1)
            skewed = pltpu.roll(padded, 0, 1, stride=1, stride_axis=0)
            diagonals.append(jnp.sum(skewed, axis=0, keepdims=True))
        sums = dot_nn(jnp.concatenate(diagonals, axis=0), buckets_ref[...])
        small = jnp.concatenate(
            [
                gain_total_ref[...],
                cross_gain_ref[...],
                ffn_gain_ref[...],
                sums,
                jnp.zeros((CARRIED - 3 - heads, sums.shape[1]), F32),
            ],
            axis=0,
        ).astype(BF16)
        for result in (keep_ref, send_ref):
            result[result.shape[0] - CARRIED :, :] = small


def factors_of(n):
    factors = []
    while n > 1:
        factor = next(f for f in range(2, n + 1) if n % f == 0)
        factors.append(factor)
        n //= factor
    return factors


def partners(n, stride, factor, j):
    moves = []
    for i in range(n):
        digit = (i // stride) % factor
        moves.append((i, i + ((digit ^ j) - digit) * stride))
    return moves


def move_kernel(plan, operands, digits_ref, *refs):
    ins, outs = refs[:operands], refs[operands:]

    def rows_at(place, size):
        if isinstance(place, int):
            return slice(place, place + size)
        base, digit, j = place
        start = base + (digits_ref[digit] ^ j) * size
        return pl.ds(pl.multiple_of(start, 16), size)

    for out, to, sources, come, size in plan:
        if len(sources) == 1:
            rows = ins[sources[0]][rows_at(come, size), :]
        else:
            terms = [ins[source][rows_at(come, size), :].astype(F32) for source in sources]
            while len(terms) > 1:
                terms = [terms[i] + terms[i + 1] for i in range(0, len(terms), 2)]
            rows = terms[0].astype(BF16)
        outs[len(outs) - 1 - out][rows_at(to, size), :] = rows


def move_rows(plan, sizes, operands, digits, after):
    columns = operands[0].shape[1]
    vmem = pl.BlockSpec(memory_space=pltpu.VMEM)
    results = pl.pallas_call(
        functools.partial(move_kernel, plan, len(operands)),
        in_specs=[pl.BlockSpec(memory_space=pltpu.SMEM)]
        + [vmem] * len(operands)
        + [pl.BlockSpec(memory_space=pl.ANY)] * len(after),
        out_specs=[vmem] * len(sizes),
        out_shape=[struct((size, columns), BF16) for size in sizes[::-1]],
        compiler_params=params(MOVE_LIMIT),
        cost_estimate=cost(0, 4 * sum(sizes) * columns),
        name="move_rows",
    )(digits, *operands, *after)
    return results[::-1]


def unpack_kernel(layout, half, core_ref, own_ref, other_ref, *refs):
    outs = refs[-1 - max(entry[0] for entry in layout) :]
    width = own_ref.shape[1]
    start = 0
    for out, row, column, offset, size in layout:
        columns = pl.ds(column * width, width)
        for ref, core in ((own_ref, core_ref[0]), (other_ref, 1 - core_ref[0])):
            first = pl.multiple_of(row * 2 * half + core * half + offset, 16)
            rows = ref[start : start + size, :].astype(F32)
            outs[out][pl.ds(first, size), columns] = rows
        start += size


def unpack(own, other, core, layout, half, shapes, after):
    vmem = pl.BlockSpec(memory_space=pltpu.VMEM)
    return pl.pallas_call(
        functools.partial(unpack_kernel, layout, half),
        in_specs=[pl.BlockSpec(memory_space=pltpu.SMEM), vmem, vmem]
        + [pl.BlockSpec(memory_space=pl.ANY)] * len(after),
        out_specs=[vmem] * len(shapes),
        out_shape=[struct(shape, F32) for shape in shapes],
        compiler_params=params(MOVE_LIMIT),
        cost_estimate=cost(0, 12 * own.shape[0] * own.shape[1]),
        name="unpack",
    )(core, own, other, *after)


def turned(rows, first, second):
    size = first * second
    to = lax.broadcasted_iota(jnp.int32, (size, size), 0)
    come = lax.broadcasted_iota(jnp.int32, (size, size), 1)
    here = to % first * second + to // first == come
    return dot_nn(jnp.where(here, 1.0, 0.0).astype(BF16), rows).astype(BF16)


def by_row_kernel(rows, memory_ref, out_ref):
    held, count, width = memory_ref.shape
    for g in range(count // rows):
        part = memory_ref[:, g * rows : (g + 1) * rows, :].reshape(held * rows, width)
        out_ref[g * rows : (g + 1) * rows] = turned(part, held, rows).reshape(rows, held, width)


def by_row_first(memory):
    held, count, width = memory.shape
    rows = GROUP // held
    if held % 16 or rows % 16 or count % (2 * rows):
        return jnp.swapaxes(memory, 0, 1)
    return pl.pallas_call(
        functools.partial(by_row_kernel, rows),
        grid=(count // (2 * rows),),
        in_specs=[pl.BlockSpec((held, 2 * rows, width), lambda g: (0, g, 0))],
        out_specs=pl.BlockSpec((2 * rows, held, width), lambda g: (g, 0, 0)),
        out_shape=struct((count, held, width), BF16),
        compiler_params=params(MOVE_LIMIT),
        cost_estimate=cost(2 * GROUP * count * held * width, 4 * count * held * width),
        name="by_row",
    )(memory)


def by_position_kernel(rows, rows_ref, after_ref, out_ref):
    count, held, width = rows_ref.shape
    for g in range(count // rows):
        part = rows_ref[g * rows : (g + 1) * rows].reshape(rows * held, width)
        part = turned(part, rows, held).reshape(held, rows, width)
        out_ref[:, g * rows : (g + 1) * rows, :] = part


def by_position(returned, after):
    held, width = returned.shape[2:]
    returned = returned.reshape(-1, held, width)
    count = returned.shape[0]
    rows = GROUP // held
    if held % 16 or rows % 16 or count % (2 * rows):
        return jnp.swapaxes(returned, 0, 1)
    return pl.pallas_call(
        functools.partial(by_position_kernel, rows),
        grid=(count // (2 * rows),),
        in_specs=[
            pl.BlockSpec((2 * rows, held, width), lambda g: (g, 0, 0)),
            pl.BlockSpec(memory_space=pl.ANY),
        ],
        out_specs=pl.BlockSpec((held, 2 * rows, width), lambda g: (0, g, 0)),
        out_shape=struct((held, count, width), BF16),
        compiler_params=params(MOVE_LIMIT),
        cost_estimate=cost(2 * GROUP * count * held * width, 4 * count * held * width),
        name="by_position",
    )(returned, after)


def tied(rows, *after):
    return lax.optimization_barrier((rows, *after))[0]


def swap_cores(rows):
    n = lax.axis_size("dp")
    return lax.ppermute(rows, "dp", [(i, i ^ 1) for i in range(n)])


class Bucket:
    def __init__(self, lanes, carried=0):
        n, me = lax.axis_size("dp"), lax.axis_index("dp")
        self.carried = carried
        self.factors = factors_of(n)
        self.moves, digits, stride = [], [], 1
        for factor in self.factors:
            digits.append((me // stride) % factor)
            self.moves.append([partners(n, stride, factor, j) for j in range(factor)])
            stride *= factor
        self.digits = jnp.stack(digits).astype(jnp.int32)
        self.lanes = lanes

    def send(self, rows, phase, j):
        return lax.ppermute(rows, "dp", self.moves[phase][j])

    def first(self, *after):
        operands, plan, sizes = [], [], []
        for lane, chunks in enumerate(self.lanes):
            start = 0
            for mine, theirs, base, rows in chunks:
                at = []
                for operand in (mine, theirs):
                    if not any(operand is other for other in operands):
                        operands.append(operand)
                    at += [k for k, other in enumerate(operands) if other is operand]
                for j in range(2):
                    plan.append((2 * lane + j, start, at, (base, 1 + lane, j), rows // 2))
                start += rows // 2
            sizes += [start, start]
        if self.carried:
            plan += [(2 + j, sizes[2], at, base + rows, self.carried) for j in range(2)]
            sizes[2] += self.carried
            sizes[3] += self.carried
        own, out, own_too, out_too = move_rows(plan, sizes, operands, self.digits, after)
        self.size = sizes[0]
        self.terms = [[own, self.send(out, 1, 1)], [own_too, self.send(out_too, 2, 1)]]
        return own

    def second(self, *after):
        size = self.size = self.size // 2
        operands = self.terms[0] + self.terms[1]
        plan = []
        for lane in range(2):
            at = [2 * lane, 2 * lane + 1]
            for j in range(2):
                plan.append((2 * lane + j, 0, at, (0, 2 - lane, j), size))
        sizes = [size] * 2 + [size + self.carried] * 2
        if self.carried:
            plan += [(2 + j, size, [2, 3], 2 * size, self.carried) for j in range(2)]
        own, out, own_too, out_too = move_rows(plan, sizes, operands, self.digits, after)
        self.terms = [[own, self.send(out, 2, 1)], [own_too, self.send(out_too, 1, 1)]]
        self.joined = False
        return own

    def third(self, phase, *after):
        parts = self.factors[phase] if phase < len(self.factors) else 1
        size = self.size // parts
        plan = []
        for j in range(parts):
            for lane in range(2):
                if self.joined:
                    at, base = list(range(len(self.terms))), lane * self.size
                else:
                    at, base = [2 * lane, 2 * lane + 1], 0
                come = (base, phase, j) if parts > 1 else base
                plan.append((j, lane * size, at, come, size))
            if self.carried:
                base = 2 * self.size if self.joined else self.size
                plan.append((j, 2 * size, at, base, self.carried))
        operands = self.terms if self.joined else self.terms[0] + self.terms[1]
        total = 2 * size + self.carried
        own, *others = move_rows(plan, [total] * parts, operands, self.digits, after)
        self.size, self.joined = size, True
        if parts > 1:
            self.terms = [own] + [self.send(o, phase, j + 1) for j, o in enumerate(others)]
        else:
            self.sums = own[2 * size :].astype(F32)
            self.pieces = [own[: 2 * size] if self.carried else own]
            self.spread(phase - 1)
        return own

    def spread(self, phase):
        held = self.pieces[0]
        self.pieces += [self.send(held, phase, j) for j in range(1, self.factors[phase])]

    def back(self, phase, *after):
        parts, size = self.factors[phase], self.size
        plan = []
        for j in range(parts):
            for lane in range(2):
                out = 0 if phase > 3 else lane
                base = lane * size * parts if phase > 3 else 0
                plan.append((out, (base, phase, j), [j], lane * size, size))
        self.size = size * parts
        sizes = [2 * self.size] if phase > 3 else [self.size] * 2
        held = move_rows(plan, sizes, self.pieces, self.digits, after)
        if phase > 3:
            self.pieces = list(held)
            self.spread(phase - 1)
        else:
            self.pieces = [held[0], self.send(held[0], 2, 1), held[1], self.send(held[1], 1, 1)]
        return held[0]

    def back_second(self, *after):
        size = self.size
        plan = [
            (lane, (0, 2 - lane, j), [2 * lane + j], 0, size) for lane in range(2) for j in range(2)
        ]
        self.size = 2 * size
        held = move_rows(plan, [self.size] * 2, self.pieces, self.digits, after)
        self.pieces = [held[0], self.send(held[0], 1, 1), held[1], self.send(held[1], 2, 1)]
        return held[0]

    def back_first(self, *after):
        size = self.size
        plan = [
            (0, (2 * lane * size, 1 + lane, j), [2 * lane + j], 0, size)
            for lane in range(2)
            for j in range(2)
        ]
        (held,) = move_rows(plan, [4 * size], self.pieces, self.digits, after)
        self.pieces = [held, self.send(held, 0, 1)]
        return held

    def finish(self, core, layout, half, shapes, *after):
        return unpack(*self.pieces, core, layout, half, shapes, after)


def cost(flops, nbytes, transcendentals=0):
    return pl.CostEstimate(
        flops=int(flops), bytes_accessed=int(nbytes), transcendentals=int(transcendentals)
    )


def whole(*shape):
    return pl.BlockSpec(shape, lambda *_: (0,) * len(shape))


def per_row(*shape):
    return pl.BlockSpec((1, *shape), lambda r, *_: (r,) + (0,) * len(shape))


def struct(shape, dtype):
    return jax.ShapeDtypeStruct(shape, dtype)


def params(limit=VMEM_LIMIT):
    return pltpu.CompilerParams(vmem_limit_bytes=limit)


def body(
    target,
    memory,
    target_segments,
    memory_segments,
    cotangent,
    self_query,
    self_key,
    self_value,
    self_output,
    relative_bias,
    self_gain,
    cross_query,
    cross_key,
    cross_value,
    cross_output,
    cross_gain,
    ffn_gain,
    ffn_in,
    ffn_out,
):
    devices = lax.axis_size("dp")
    rows, length, width = target.shape
    held = memory.shape[0]
    span = held * devices
    heads = relative_bias.shape[1]
    inner = self_query.shape[1]
    head_size = inner // heads
    hidden_width = ffn_in.shape[1]
    chunks = hidden_width // width
    count = rows * length
    stacked = heads * length
    core = (lax.axis_index("dp") % 2).astype(jnp.int32).reshape(1)
    smem = pl.BlockSpec(memory_space=pltpu.SMEM)

    outgoing = by_row_first(memory).reshape(devices, rows, held, width)
    mem = lax.all_to_all(outgoing, "dp", split_axis=0, concat_axis=0, tiled=True)

    gain_one = self_gain.astype(F32).reshape(1, width)
    gain_two = cross_gain.astype(F32).reshape(1, width)
    gain_three = ffn_gain.astype(F32).reshape(1, width)
    table = bucket_table(length)
    onehot = jnp.asarray(table[None, :, :] == np.arange(NB)[:, None, None], dtype=BF16)
    bias = jnp.einsum("bh,bij->hij", relative_bias, onehot, preferred_element_type=F32)
    column = target_segments.reshape(rows, length, 1)
    line = target_segments.reshape(rows, 1, length)
    mem_line = memory_segments.reshape(rows, 1, span)

    tokens = struct((count, inner), BF16)
    h1, q, k, v, p1, o1, y1, h2, cq = pl.pallas_call(
        functools.partial(self_forward_kernel, rows, length, head_size),
        out_shape=[
            tokens,
            tokens,
            tokens,
            tokens,
            struct((rows, stacked, length), BF16),
            tokens,
            struct((count, width), F32),
            tokens,
            tokens,
        ],
        compiler_params=params(),
        cost_estimate=cost(2 * count * width * inner * 5, 12 * count * width),
        name="self_forward",
    )(
        target.reshape(count, width),
        column,
        line,
        bias,
        self_query,
        self_key,
        self_value,
        self_output,
        cross_query,
        gain_one,
        gain_two,
    )
    by_row = (rows, length, width)
    y1 = y1.reshape(by_row)
    cq = cq.reshape(by_row)
    h2 = h2.reshape(by_row)
    h1, q, k, v, o1 = (a.reshape(by_row) for a in (h1, q, k, v, o1))
    half = width // 2
    square = whole(width, inner)
    line_spec = whole(1, width)
    any_spec = pl.BlockSpec(memory_space=pl.ANY)
    here = per_row(length, width)
    mem_spec = pl.BlockSpec((devices, 1, held, width), lambda r: (0, r, 0, 0))
    keys_spec = per_row(span, inner)
    keys = struct((rows, span, inner), BF16)
    ck, cv, p2, o2, y2 = pl.pallas_call(
        functools.partial(cross_forward_kernel, length, head_size),
        grid=(rows,),
        in_specs=[
            here,
            mem_spec,
            here,
            per_row(length, 1),
            per_row(1, span),
            square,
            square,
            square,
        ],
        out_specs=[keys_spec, keys_spec, per_row(stacked, span), here, here],
        out_shape=[
            keys,
            keys,
            struct((rows, stacked, span), BF16),
            struct(by_row, BF16),
            struct(by_row, F32),
        ],
        compiler_params=params(),
        cost_estimate=cost(4 * rows * span * width * inner, 10 * rows * span * width),
        name="cross_forward",
    )(cq, mem, y1, column, mem_line, cross_key, cross_value, cross_output)

    full = whole(count, width)
    part_spec = pl.BlockSpec((2, 1, half, width), lambda c: (0, c, 0, 0))
    part = struct((2, chunks, half, width), BF16)
    layer_out, dy2, ffn_gain_grad, ffn_keep, ffn_send = pl.pallas_call(
        functools.partial(ffn_kernel, chunks),
        grid=(chunks,),
        in_specs=[
            smem,
            full,
            full,
            line_spec,
            pl.BlockSpec((width, width), lambda c: (0, c)),
            pl.BlockSpec((width, width), lambda c: (c, 0)),
        ],
        out_specs=[full, full, line_spec, part_spec, part_spec],
        out_shape=[
            struct((count, width), BF16),
            struct((count, width), F32),
            struct((1, width), F32),
            part,
            part,
        ],
        scratch_shapes=[
            pltpu.VMEM((count, width), BF16),
            pltpu.VMEM((count, width), F32),
            pltpu.VMEM((count, width), F32),
            pltpu.VMEM((2, width, width), F32),
        ],
        compiler_params=params(),
        cost_estimate=cost(12 * count * width * hidden_width, 10 * width * hidden_width),
        name="ffn",
    )(core, y2.reshape(count, width), cotangent.reshape(count, width), gain_three, ffn_in, ffn_out)

    ffn_keep = ffn_keep.reshape(-1, width)
    ffn_other = swap_cores(ffn_send.reshape(-1, width))
    rows_each = chunks * half
    ffn_sum = Bucket([[(ffn_keep, ffn_other, lane * rows_each, rows_each)] for lane in range(2)])

    dy1, cross_gain_grad, mem_grad, dq, dk, dv = pl.pallas_call(
        functools.partial(cross_backward_kernel, length, head_size),
        grid=(rows,),
        in_specs=[
            here,
            here,
            keys_spec,
            keys_spec,
            per_row(stacked, span),
            here,
            line_spec,
            square,
            square,
            square,
            square,
        ],
        out_specs=[here, line_spec, mem_spec, here, keys_spec, keys_spec],
        out_shape=[
            struct(by_row, F32),
            struct((1, width), F32),
            struct(mem.shape, BF16),
            struct(by_row, BF16),
            keys,
            keys,
        ],
        compiler_params=params(),
        cost_estimate=cost(6 * rows * span * width * inner, 10 * rows * span * width),
        name="cross_backward",
    )(
        dy2.reshape(by_row),
        cq,
        ck,
        cv,
        p2,
        y1,
        gain_two,
        cross_query,
        cross_key,
        cross_value,
        cross_output,
    )
    passed = ffn_sum.first(dy1)
    returned = lax.all_to_all(
        tied(mem_grad, passed), "dp", split_axis=0, concat_axis=0, tiled=True
    )

    halves = struct((4 * half, width), BF16)
    halves_spec = whole(4 * half, width)
    cross_keep, cross_send = pl.pallas_call(
        functools.partial(cross_grads_kernel, rows),
        grid=(rows,),
        in_specs=[smem, any_spec, keys_spec, keys_spec, mem_spec, full, full, full, full],
        out_specs=[halves_spec, halves_spec],
        out_shape=[halves, halves],
        scratch_shapes=[pltpu.VMEM((4, width, inner), F32)],
        compiler_params=params(),
        cost_estimate=cost(4 * rows * span * width * inner, 10 * rows * span * width),
        name="cross_grads",
    )(
        core,
        passed,
        dk,
        dv,
        mem,
        dq.reshape(count, inner),
        h2.reshape(count, width),
        o2.reshape(count, inner),
        dy2,
    )

    lanes = 256
    buckets = np.zeros((lanes, width), np.float32)
    for n in range(length):
        buckets[length - 1 - n, table[n, 0]] = 1.0
    packed = [struct((4 * half + CARRIED, width), BF16)] * 2
    target_grad, self_keep, self_send = pl.pallas_call(
        functools.partial(self_backward_kernel, rows, length, head_size),
        grid=(rows,),
        in_specs=[
            smem,
            any_spec,
            here,
            here,
            here,
            here,
            per_row(stacked, length),
            full,
            full,
            here,
            line_spec,
            square,
            square,
            square,
            square,
            line_spec,
            line_spec,
            whole(lanes, width),
        ],
        out_specs=[here] + [whole(*one.shape) for one in packed],
        out_shape=[struct(by_row, BF16)] + packed,
        scratch_shapes=[
            pltpu.VMEM((4, width, inner), F32),
            pltpu.VMEM((count, width), BF16),
            pltpu.VMEM((count, inner), BF16),
            pltpu.VMEM((count, inner), BF16),
            pltpu.VMEM((count, inner), BF16),
            pltpu.VMEM((1, width), F32),
            pltpu.VMEM((heads, length, length), F32),
        ],
        compiler_params=params(),
        cost_estimate=cost(2 * count * width * inner * 12, 12 * count * width),
        name="self_backward",
    )(
        core,
        cross_keep,
        dy1,
        q,
        k,
        v,
        p1,
        o1.reshape(count, inner),
        h1.reshape(count, width),
        target,
        gain_one,
        self_query,
        self_key,
        self_value,
        self_output,
        cross_gain_grad,
        ffn_gain_grad,
        jnp.asarray(buckets),
    )
    passed = ffn_sum.second(target_grad)
    self_other = swap_cores(tied(self_send, passed))
    cross_other = swap_cores(tied(cross_send, passed))
    attention_sum = Bucket(
        [[(cross_keep, cross_other, 0, 4 * half)], [(self_keep, self_other, 0, 4 * half)]], CARRIED
    )
    phases = len(ffn_sum.factors)
    ahead = [functools.partial(ffn_sum.third, phase) for phase in range(3, phases + 1)]
    ahead += [functools.partial(ffn_sum.back, phase) for phase in range(phases - 1, 2, -1)]
    ahead += [ffn_sum.back_second, ffn_sum.back_first]
    behind = [attention_sum.first, attention_sum.second]
    behind += [functools.partial(attention_sum.third, phase) for phase in range(3, phases + 1)]
    behind += [functools.partial(attention_sum.back, phase) for phase in range(phases - 1, 2, -1)]
    for k, (one, other) in enumerate(zip(ahead, behind)):
        passed = one(other(passed))
        if k == len(ahead) - 3:
            memory_grad = by_position(returned, passed)
            passed = memory_grad
    ffn_layout = [(0, 0, c, 0, half) for c in range(chunks)]
    ffn_layout += [(1, c, 0, 0, half) for c in range(chunks)]
    small = attention_sum.sums
    ffn_in_grad, ffn_out_grad = ffn_sum.finish(
        core, ffn_layout, half, [(width, hidden_width), (hidden_width, width)], passed
    )
    passed = attention_sum.back_second(ffn_in_grad, small)
    passed = attention_sum.back_first(passed)
    attention_layout = [(part, 0, 0, 0, half) for part in range(8)]
    (
        cross_output_grad,
        cross_query_grad,
        cross_key_grad,
        cross_value_grad,
        self_output_grad,
        self_query_grad,
        self_key_grad,
        self_value_grad,
    ) = attention_sum.finish(core, attention_layout, half, [(width, inner)] * 8)
    return (
        layer_out.reshape(by_row),
        target_grad,
        memory_grad,
        self_query_grad,
        self_key_grad,
        self_value_grad,
        self_output_grad,
        small[3 : 3 + heads, :NB].T,
        small[0],
        cross_query_grad,
        cross_key_grad,
        cross_value_grad,
        cross_output_grad,
        small[1],
        small[2],
        ffn_in_grad,
        ffn_out_grad,
    )


def solution(mesh):
    rows3 = P("dp", None, None)
    rows2 = P("dp", None)
    in_specs = (rows3, rows3, rows2, rows2, rows3) + (P(),) * 14
    out_specs = (rows3, rows3, rows3) + (P(),) * 14
    return jax.shard_map(body, mesh=mesh, in_specs=in_specs, out_specs=out_specs, check_vma=False)
```

```python
import functools

import jax
import jax.numpy as jnp
import numpy as np
from jax import lax
from jax.experimental import pallas as pl
from jax.experimental.pallas import tpu as pltpu
from jax.sharding import PartitionSpec as P

NB = 32
MAXDIST = 128
EPS = 1e-06
GROUP = 256
CARRIED = 16
MASKED = -1000000000.0
LIMITS = {
    "by_row": 16,
    "self_forward": 36,
    "cross_forward": 56,
    "ffn": 56,
    "cross_backward": 56,
    "cross_grads": 56,
    "self_backward": 56,
    "by_position": 16,
    "move_rows": 16,
    "unpack": 16,
}
BF16 = jnp.bfloat16
F32 = jnp.float32


def bucket_table(length):
    exact = NB // 2
    offsets = np.arange(length)[:, None] - np.arange(length)[None, :]
    distance = np.maximum(offsets, 0)
    scaled = np.log(np.maximum(distance, exact) / exact) / np.log(MAXDIST / exact) * (NB - exact)
    farther = np.minimum(exact + scaled.astype(np.int32), NB - 1)
    return np.where(distance < exact, distance, farther).astype(np.int32)


def dot_nn(left, right):
    return lax.dot_general(left, right, (((1,), (0,)), ((), ())), preferred_element_type=F32)


def dot_nt(left, right):
    return lax.dot_general(left, right, (((1,), (1,)), ((), ())), preferred_element_type=F32)


def dot_tn(left, right):
    return lax.dot_general(left, right, (((0,), (0,)), ((), ())), preferred_element_type=F32)


def norm_factor(tensor):
    return lax.rsqrt(jnp.mean(tensor * tensor, axis=-1, keepdims=True) + EPS)


def norm_backward(tensor, gain, incoming):
    factor = norm_factor(tensor)
    scaled = tensor * factor
    shaped = incoming * gain
    inner = jnp.mean(scaled * shaped, axis=-1, keepdims=True)
    return factor * (shaped - scaled * inner), incoming * scaled


def head_masks(head_size, dtype):
    lane = lax.broadcasted_iota(jnp.int32, (1, GROUP), 1)
    return [
        jnp.where(lane // head_size == h, 1.0, 0.0).astype(dtype)
        for h in range(GROUP // head_size)
    ]


def stack_heads(tensor, masks):
    return jnp.concatenate([tensor * mask for mask in masks], axis=0)


def merge_heads(stacked, masks, length):
    out = stacked[:length] * masks[0]
    for h in range(1, len(masks)):
        out = out + stacked[h * length : (h + 1) * length] * masks[h]
    return out


def flat(ref):
    return ref[...].reshape(-1, ref.shape[-1])


def row_parts(size, index):
    return pl.ds(pl.multiple_of(index * size, 16), size)


def softmax_rows(scores):
    top = jnp.max(scores, axis=-1, keepdims=True)
    grown = jnp.exp(scores - top)
    return grown * (1.0 / jnp.sum(grown, axis=-1, keepdims=True))


def self_forward_kernel(
    rows,
    length,
    head_size,
    x_ref,
    column_ref,
    line_ref,
    bias_ref,
    query_ref,
    key_ref,
    value_ref,
    output_ref,
    cross_query_ref,
    gain_one_ref,
    gain_two_ref,
    h1_ref,
    q_ref,
    k_ref,
    v_ref,
    p_ref,
    o_ref,
    y1_ref,
    h2_ref,
    cq_ref,
):
    masks = head_masks(head_size, BF16)
    masks_f = head_masks(head_size, F32)
    x = x_ref[...].astype(F32)
    h1 = (x * norm_factor(x) * gain_one_ref[...]).astype(BF16)
    h1_ref[...] = h1
    q_ref[...] = dot_nn(h1, query_ref[...]).astype(BF16)
    k_ref[...] = dot_nn(h1, key_ref[...]).astype(BF16)
    v_ref[...] = dot_nn(h1, value_ref[...]).astype(BF16)
    i = lax.broadcasted_iota(jnp.int32, (length, length), 0)
    j = lax.broadcasted_iota(jnp.int32, (length, length), 1)

    def row(r, carry):
        here = pl.ds(pl.multiple_of(r * length, 16), length)
        allowed = jnp.logical_and(j <= i, column_ref[r] == line_ref[r])
        shift = jnp.where(allowed, 0.0, MASKED)
        for g in range(q_ref.shape[1] // GROUP):
            lanes = pl.ds(g * GROUP, GROUP)
            scores = dot_nt(stack_heads(q_ref[here, lanes], masks), k_ref[here, lanes])
            probs = []
            for h in range(len(masks)):
                one = scores[h * length : (h + 1) * length]
                one = one + bias_ref[g * len(masks) + h] + shift
                probs.append(softmax_rows(one).astype(BF16))
            stacked = jnp.concatenate(probs, axis=0)
            size = stacked.shape[0]
            p_ref[r, g * size : (g + 1) * size, :] = stacked
            mixed = merge_heads(dot_nn(stacked, v_ref[here, lanes]), masks_f, length)
            o_ref[here, lanes] = mixed.astype(BF16)
        return carry

    lax.fori_loop(0, rows, row, 0)
    y1 = x + dot_nn(o_ref[...], output_ref[...])
    y1_ref[...] = y1
    h2 = (y1 * norm_factor(y1) * gain_two_ref[...]).astype(BF16)
    h2_ref[...] = h2
    cq_ref[...] = dot_nn(h2, cross_query_ref[...]).astype(BF16)


def cross_forward_kernel(
    length,
    head_size,
    cq_ref,
    mem_ref,
    y1_ref,
    column_ref,
    line_ref,
    key_ref,
    value_ref,
    output_ref,
    ck_ref,
    cv_ref,
    p_ref,
    o_ref,
    y2_ref,
):
    masks = head_masks(head_size, BF16)
    masks_f = head_masks(head_size, F32)
    pair, span, inner = ck_ref.shape
    for r in range(pair):
        mem = mem_ref[:, r].reshape(span, -1)
        ck_ref[r] = dot_nn(mem, key_ref[...]).astype(BF16)
        cv_ref[r] = dot_nn(mem, value_ref[...]).astype(BF16)
    jobs = [(r, g) for r in range(pair) for g in range(inner // GROUP)]
    shift = [jnp.where(column_ref[r] == line_ref[r], 0.0, MASKED) for r in range(pair)]
    scores = {}
    for r, g in jobs:
        lanes = slice(g * GROUP, (g + 1) * GROUP)
        scores[r, g] = dot_nt(stack_heads(cq_ref[r, :, lanes], masks), ck_ref[r, :, lanes])
    for r, g in jobs:
        lanes = slice(g * GROUP, (g + 1) * GROUP)
        probs = []
        for h in range(len(masks)):
            one = scores[r, g][h * length : (h + 1) * length] + shift[r]
            probs.append(softmax_rows(one).astype(BF16))
        stacked = jnp.concatenate(probs, axis=0)
        size = stacked.shape[0]
        p_ref[r, g * size : (g + 1) * size, :] = stacked
        mixed = merge_heads(dot_nn(stacked, cv_ref[r, :, lanes]), masks_f, length)
        o_ref[r, :, lanes] = mixed.astype(BF16)
    y2 = flat(y1_ref) + dot_nn(flat(o_ref), output_ref[...])
    y2_ref[...] = y2.reshape(y2_ref.shape)


def ffn_kernel(
    chunks,
    core_ref,
    y2_ref,
    cot_ref,
    gain_ref,
    in_ref,
    out_ref,
    layer_ref,
    dy2_ref,
    gain_grad_ref,
    keep_ref,
    send_ref,
    h3_ref,
    total_ref,
    back_ref,
    grad_ref,
):
    step = pl.program_id(0)

    @pl.when(step == 0)
    def _():
        y2 = y2_ref[...]
        h3_ref[...] = (y2 * norm_factor(y2) * gain_ref[...]).astype(BF16)
        total_ref[...] = y2
        back_ref[...] = jnp.zeros_like(back_ref)

    h3 = h3_ref[...]
    cot = cot_ref[...]
    act = dot_nn(h3, in_ref[...])
    square = act * act
    root = float(np.sqrt(2.0 / np.pi))
    tanh = jnp.tanh(root * act * (1.0 + 0.044715 * square))
    gate = 0.5 + 0.5 * tanh
    hidden = (act * gate).astype(BF16)
    slope = gate + (0.5 * root) * act * (1.0 - tanh * tanh) * (1.0 + 3 * 0.044715 * square)
    act_grad = (slope * dot_nt(cot, out_ref[...])).astype(BF16)
    total_ref[...] += dot_nn(hidden, out_ref[...])
    back_ref[...] += dot_nt(act_grad, in_ref[...])
    half = keep_ref.shape[2]
    mine = row_parts(half, core_ref[0])
    other = row_parts(half, 1 - core_ref[0])
    grad_ref[0] = dot_tn(h3, act_grad)
    grad_ref[1] = dot_tn(hidden, cot)
    for part in range(2):
        keep_ref[part, 0] = grad_ref[part, mine, :].astype(BF16)
        send_ref[part, 0] = grad_ref[part, other, :].astype(BF16)

    @pl.when(step == chunks - 1)
    def _():
        layer_ref[...] = total_ref[...].astype(BF16)
        grad, gain_grad = norm_backward(y2_ref[...], gain_ref[...], back_ref[...])
        dy2_ref[...] = cot_ref[...].astype(F32) + grad
        gain_grad_ref[...] = jnp.sum(gain_grad, axis=0, keepdims=True)


def cross_backward_kernel(
    length,
    head_size,
    dy2_ref,
    cq_ref,
    ck_ref,
    cv_ref,
    p_ref,
    y1_ref,
    gain_ref,
    query_ref,
    key_ref,
    value_ref,
    output_ref,
    dy1_ref,
    gain_grad_ref,
    mem_grad_ref,
    dq_ref,
    dk_ref,
    dv_ref,
):
    masks = head_masks(head_size, BF16)
    masks_f = head_masks(head_size, F32)

    @pl.when(pl.program_id(0) == 0)
    def _():
        gain_grad_ref[...] = jnp.zeros_like(gain_grad_ref)

    pair = dy2_ref.shape[0]
    c2 = flat(dy2_ref).astype(BF16)
    do = dot_nt(c2, output_ref[...]).astype(BF16)
    jobs = [(r, g) for r in range(pair) for g in range(cq_ref.shape[2] // GROUP)]
    outs, upstream = {}, {}
    for r, g in jobs:
        lanes = slice(g * GROUP, (g + 1) * GROUP)
        outs[r, g] = stack_heads(do[r * length : (r + 1) * length, lanes], masks)
        upstream[r, g] = dot_nt(outs[r, g], cv_ref[r, :, lanes])
    for r, g in jobs:
        lanes = slice(g * GROUP, (g + 1) * GROUP)
        size = len(masks) * length
        probs = p_ref[r, g * size : (g + 1) * size, :]
        dv_ref[r, :, lanes] = dot_tn(probs, outs[r, g]).astype(BF16)
        pieces = []
        for h in range(len(masks)):
            prob = probs[h * length : (h + 1) * length].astype(F32)
            up = upstream[r, g][h * length : (h + 1) * length]
            pieces.append((prob * (up - jnp.sum(prob * up, axis=-1, keepdims=True))).astype(BF16))
        ds = jnp.concatenate(pieces, axis=0)
        queries = stack_heads(cq_ref[r, :, lanes], masks)
        dk_ref[r, :, lanes] = dot_tn(ds, queries).astype(BF16)
        mixed = merge_heads(dot_nn(ds, ck_ref[r, :, lanes]), masks_f, length)
        dq_ref[r, :, lanes] = mixed.astype(BF16)
    for r in range(pair):
        mem_grad = dot_nt(dk_ref[r], key_ref[...]) + dot_nt(dv_ref[r], value_ref[...])
        shape = (mem_grad_ref.shape[0], *mem_grad_ref.shape[2:])
        mem_grad_ref[:, r] = mem_grad.astype(BF16).reshape(shape)
    back = dot_nt(flat(dq_ref), query_ref[...])
    grad, gain_grad = norm_backward(flat(y1_ref), gain_ref[...], back)
    dy1_ref[...] = (flat(dy2_ref) + grad).reshape(dy1_ref.shape)
    gain_grad_ref[...] += jnp.sum(gain_grad, axis=0, keepdims=True)


def cross_grads_kernel(
    rows,
    core_ref,
    after_ref,
    dk_ref,
    dv_ref,
    mem_ref,
    dq_ref,
    h2_ref,
    o_ref,
    dy2_ref,
    keep_ref,
    send_ref,
    grad_ref,
):
    step = pl.program_id(0)
    mem = mem_ref[...].reshape(dk_ref.shape[1], -1)

    @pl.when(step == 0)
    def _():
        grad_ref[0] = dot_tn(o_ref[...], dy2_ref[...].astype(BF16))
        grad_ref[1] = dot_tn(h2_ref[...], dq_ref[...])
        grad_ref[2] = dot_tn(mem, dk_ref[0])
        grad_ref[3] = dot_tn(mem, dv_ref[0])

    @pl.when(step > 0)
    def _():
        grad_ref[2] += dot_tn(mem, dk_ref[0])
        grad_ref[3] += dot_tn(mem, dv_ref[0])

    @pl.when(step == rows - 1)
    def _():
        write_grads(core_ref, grad_ref, [keep_ref], [send_ref])


def write_grads(core_ref, grad_ref, keeps, sends):
    half = grad_ref.shape[1] // 2
    mine = row_parts(half, core_ref[0])
    other = row_parts(half, 1 - core_ref[0])
    part = 0
    for keep_ref, send_ref in zip(keeps, sends):
        for block in range(keep_ref.shape[0] // half):
            here = slice(block * half, (block + 1) * half)
            keep_ref[here, :] = grad_ref[part, mine, :].astype(BF16)
            send_ref[here, :] = grad_ref[part, other, :].astype(BF16)
            part += 1


def self_backward_kernel(
    rows,
    length,
    head_size,
    core_ref,
    after_ref,
    dy1_ref,
    q_ref,
    k_ref,
    v_ref,
    p_ref,
    o_ref,
    h1_ref,
    x_ref,
    gain_ref,
    query_ref,
    key_ref,
    value_ref,
    output_ref,
    cross_gain_ref,
    ffn_gain_ref,
    buckets_ref,
    dx_ref,
    keep_ref,
    next_keep_ref,
    last_keep_ref,
    send_ref,
    next_send_ref,
    last_send_ref,
    grad_ref,
    c1_ref,
    dq_ref,
    dk_ref,
    dv_ref,
    gain_total_ref,
    bias_grad_ref,
):
    step = pl.program_id(0)
    masks = head_masks(head_size, BF16)
    masks_f = head_masks(head_size, F32)
    pair = dy1_ref.shape[0]
    here = pl.ds(pl.multiple_of(step * pair * length, 16), pair * length)

    @pl.when(step == 0)
    def _():
        gain_total_ref[...] = jnp.zeros_like(gain_total_ref)
        bias_grad_ref[...] = jnp.zeros_like(bias_grad_ref)

    c1 = flat(dy1_ref).astype(BF16)
    c1_ref[here, :] = c1
    do = dot_nt(c1, output_ref[...]).astype(BF16)
    jobs = [(r, g) for r in range(pair) for g in range(q_ref.shape[2] // GROUP)]
    outs, upstream, total = {}, {}, {}
    for r, g in jobs:
        lanes = slice(g * GROUP, (g + 1) * GROUP)
        outs[r, g] = stack_heads(do[r * length : (r + 1) * length, lanes], masks)
        upstream[r, g] = dot_nt(outs[r, g], v_ref[r, :, lanes])
    for r, g in jobs:
        lanes = slice(g * GROUP, (g + 1) * GROUP)
        there = pl.ds(pl.multiple_of((step * pair + r) * length, 16), length)
        size = len(masks) * length
        probs = p_ref[r, g * size : (g + 1) * size, :]
        dv_ref[there, lanes] = dot_tn(probs, outs[r, g]).astype(BF16)
        pieces = []
        for h in range(len(masks)):
            prob = probs[h * length : (h + 1) * length].astype(F32)
            up = upstream[r, g][h * length : (h + 1) * length]
            one = (prob * (up - jnp.sum(prob * up, axis=-1, keepdims=True))).astype(BF16)
            pieces.append(one)
            total[g, h] = one.astype(F32) + total[g, h] if r else one.astype(F32)
        ds = jnp.concatenate(pieces, axis=0)
        queries = stack_heads(q_ref[r, :, lanes], masks)
        dk_ref[there, lanes] = dot_tn(ds, queries).astype(BF16)
        mixed = merge_heads(dot_nn(ds, k_ref[r, :, lanes]), masks_f, length)
        dq_ref[there, lanes] = mixed.astype(BF16)
    for (g, h), one in total.items():
        bias_grad_ref[g * len(masks) + h] += one
    back = dot_nt(dq_ref[here, :], query_ref[...])
    back = back + dot_nt(dk_ref[here, :], key_ref[...])
    back = back + dot_nt(dv_ref[here, :], value_ref[...])
    grad, gain_grad = norm_backward(flat(x_ref).astype(F32), gain_ref[...], back)
    dx_ref[...] = (flat(dy1_ref) + grad).astype(BF16).reshape(dx_ref.shape)
    gain_total_ref[...] += jnp.sum(gain_grad, axis=0, keepdims=True)

    @pl.when(step == rows // pair - 1)
    def _():
        h1 = h1_ref[...]
        grad_ref[0] = dot_tn(o_ref[...], c1_ref[...])
        grad_ref[1] = dot_tn(h1, dq_ref[...])
        grad_ref[2] = dot_tn(h1, dk_ref[...])
        grad_ref[3] = dot_tn(h1, dv_ref[...])
        keeps = [keep_ref, next_keep_ref, last_keep_ref]
        sends = [send_ref, next_send_ref, last_send_ref]
        write_grads(core_ref, grad_ref, keeps, sends)
        heads = bias_grad_ref.shape[0]
        lanes = buckets_ref.shape[0]
        flip = jnp.where(
            lax.broadcasted_iota(jnp.int32, (length, length), 0)
            + lax.broadcasted_iota(jnp.int32, (length, length), 1)
            == length - 1,
            1.0,
            0.0,
        ).astype(BF16)
        diagonals = []
        for h in range(heads):
            flipped = dot_nn(flip, bias_grad_ref[h].astype(BF16))
            padded = jnp.concatenate([flipped, jnp.zeros((length, lanes - length), F32)], axis=1)
            skewed = pltpu.roll(padded, 0, 1, stride=1, stride_axis=0)
            diagonals.append(jnp.sum(skewed, axis=0, keepdims=True))
        sums = dot_nn(jnp.concatenate(diagonals, axis=0), buckets_ref[...])
        small = jnp.concatenate(
            [
                gain_total_ref[...],
                cross_gain_ref[...],
                ffn_gain_ref[...],
                sums,
                jnp.zeros((CARRIED - 3 - heads, sums.shape[1]), F32),
            ],
            axis=0,
        ).astype(BF16)
        for result in (last_keep_ref, last_send_ref):
            result[result.shape[0] - CARRIED :, :] = small


def factors_of(n):
    factors = []
    while n > 1:
        factor = next(f for f in range(2, n + 1) if n % f == 0)
        factors.append(factor)
        n //= factor
    return factors


def partners(n, stride, factor, j):
    moves = []
    for i in range(n):
        digit = (i // stride) % factor
        moves.append((i, i + ((digit ^ j) - digit) * stride))
    return moves


def move_kernel(plan, operands, digits_ref, *refs):
    ins, outs = refs[:operands], refs[operands:]

    def rows_at(place, size):
        if isinstance(place, int):
            return slice(place, place + size)
        base, digit, j = place
        start = base + (digits_ref[digit] ^ j) * size
        return pl.ds(pl.multiple_of(start, 16), size)

    for out, to, sources, come, size in plan:
        if len(sources) == 1:
            rows = ins[sources[0]][rows_at(come, size), :]
        else:
            terms = [ins[source][rows_at(come, size), :].astype(F32) for source in sources]
            while len(terms) > 1:
                terms = [terms[i] + terms[i + 1] for i in range(0, len(terms), 2)]
            rows = terms[0].astype(BF16)
        outs[len(outs) - 1 - out][rows_at(to, size), :] = rows


def move_rows(plan, sizes, operands, digits, after):
    columns = operands[0].shape[1]
    vmem = pl.BlockSpec(memory_space=pltpu.VMEM)
    results = pl.pallas_call(
        functools.partial(move_kernel, plan, len(operands)),
        in_specs=[pl.BlockSpec(memory_space=pltpu.SMEM)]
        + [vmem] * len(operands)
        + [pl.BlockSpec(memory_space=pl.ANY)] * len(after),
        out_specs=[vmem] * len(sizes),
        out_shape=[struct((size, columns), BF16) for size in sizes[::-1]],
        compiler_params=params(LIMITS["move_rows"]),
        cost_estimate=cost(0, 4 * sum(sizes) * columns),
        name="move_rows",
    )(digits, *operands, *after)
    return results[::-1]


def unpack_kernel(layout, half, core_ref, own_ref, other_ref, *refs):
    outs = refs[-1 - max(entry[0] for entry in layout) :]
    width = own_ref.shape[1]
    start = 0
    for out, row, column, offset, size in layout:
        columns = pl.ds(column * width, width)
        for ref, core in ((own_ref, core_ref[0]), (other_ref, 1 - core_ref[0])):
            first = pl.multiple_of(row * 2 * half + core * half + offset, 16)
            rows = ref[start : start + size, :].astype(F32)
            outs[out][pl.ds(first, size), columns] = rows
        start += size


def unpack(own, other, core, layout, half, shapes, after):
    vmem = pl.BlockSpec(memory_space=pltpu.VMEM)
    return pl.pallas_call(
        functools.partial(unpack_kernel, layout, half),
        in_specs=[pl.BlockSpec(memory_space=pltpu.SMEM), vmem, vmem]
        + [pl.BlockSpec(memory_space=pl.ANY)] * len(after),
        out_specs=[vmem] * len(shapes),
        out_shape=[struct(shape, F32) for shape in shapes],
        compiler_params=params(LIMITS["unpack"]),
        cost_estimate=cost(0, 12 * own.shape[0] * own.shape[1]),
        name="unpack",
    )(core, own, other, *after)


def turned(rows, first, second):
    size = first * second
    to = lax.broadcasted_iota(jnp.int32, (size, size), 0)
    come = lax.broadcasted_iota(jnp.int32, (size, size), 1)
    here = to % first * second + to // first == come
    return dot_nn(jnp.where(here, 1.0, 0.0).astype(BF16), rows).astype(BF16)


def by_row_kernel(rows, memory_ref, out_ref):
    held, count, width = memory_ref.shape
    for g in range(count // rows):
        part = memory_ref[:, g * rows : (g + 1) * rows, :].reshape(held * rows, width)
        out_ref[g * rows : (g + 1) * rows] = turned(part, held, rows).reshape(rows, held, width)


def by_row_first(memory):
    held, count, width = memory.shape
    rows = GROUP // held
    if held % 16 or rows % 16 or count % (4 * rows):
        return jnp.swapaxes(memory, 0, 1)
    return pl.pallas_call(
        functools.partial(by_row_kernel, rows),
        grid=(count // (4 * rows),),
        in_specs=[pl.BlockSpec((held, 4 * rows, width), lambda g: (0, g, 0))],
        out_specs=pl.BlockSpec((4 * rows, held, width), lambda g: (g, 0, 0)),
        out_shape=struct((count, held, width), BF16),
        compiler_params=params(LIMITS["by_row"]),
        cost_estimate=cost(2 * GROUP * count * held * width, 4 * count * held * width),
        name="by_row",
    )(memory)


def by_position_kernel(rows, rows_ref, after_ref, out_ref):
    count, held, width = rows_ref.shape
    for g in range(count // rows):
        part = rows_ref[g * rows : (g + 1) * rows].reshape(rows * held, width)
        part = turned(part, rows, held).reshape(held, rows, width)
        out_ref[:, g * rows : (g + 1) * rows, :] = part


def by_position(returned, after):
    held, width = returned.shape[2:]
    returned = returned.reshape(-1, held, width)
    count = returned.shape[0]
    rows = GROUP // held
    if held % 16 or rows % 16 or count % (2 * rows):
        return jnp.swapaxes(returned, 0, 1)
    return pl.pallas_call(
        functools.partial(by_position_kernel, rows),
        grid=(count // (2 * rows),),
        in_specs=[
            pl.BlockSpec((2 * rows, held, width), lambda g: (g, 0, 0)),
            pl.BlockSpec(memory_space=pl.ANY),
        ],
        out_specs=pl.BlockSpec((held, 2 * rows, width), lambda g: (0, g, 0)),
        out_shape=struct((held, count, width), BF16),
        compiler_params=params(LIMITS["by_position"]),
        cost_estimate=cost(2 * GROUP * count * held * width, 4 * count * held * width),
        name="by_position",
    )(returned, after)


def tied(rows, *after):
    return lax.optimization_barrier((rows, *after))[0]


def swap_cores(rows):
    n = lax.axis_size("dp")
    return lax.ppermute(rows, "dp", [(i, i ^ 1) for i in range(n)])


class Bucket:
    def __init__(self, lanes, carried=0):
        n, me = lax.axis_size("dp"), lax.axis_index("dp")
        self.carried = carried
        self.factors = factors_of(n)
        self.moves, digits, stride = [], [], 1
        for factor in self.factors:
            digits.append((me // stride) % factor)
            self.moves.append([partners(n, stride, factor, j) for j in range(factor)])
            stride *= factor
        self.digits = jnp.stack(digits).astype(jnp.int32)
        self.lanes = lanes

    def send(self, rows, phase, j):
        return lax.ppermute(rows, "dp", self.moves[phase][j])

    def first(self, *after):
        operands, plan, sizes = [], [], []
        for lane, chunks in enumerate(self.lanes):
            start = 0
            for mine, theirs, base, rows in chunks:
                at = []
                for operand in (mine, theirs):
                    if not any(operand is other for other in operands):
                        operands.append(operand)
                    at += [k for k, other in enumerate(operands) if other is operand]
                for j in range(2):
                    plan.append((2 * lane + j, start, at, (base, 1 + lane, j), rows // 2))
                start += rows // 2
            sizes += [start, start]
        if self.carried:
            plan += [(2 + j, sizes[2], at, base + rows, self.carried) for j in range(2)]
            sizes[2] += self.carried
            sizes[3] += self.carried
        own, out, own_too, out_too = move_rows(plan, sizes, operands, self.digits, after)
        self.size = sizes[0]
        self.terms = [[own, self.send(out, 1, 1)], [own_too, self.send(out_too, 2, 1)]]
        return own

    def second(self, *after):
        size = self.size = self.size // 2
        operands = self.terms[0] + self.terms[1]
        plan = []
        for lane in range(2):
            at = [2 * lane, 2 * lane + 1]
            for j in range(2):
                plan.append((2 * lane + j, 0, at, (0, 2 - lane, j), size))
        sizes = [size] * 2 + [size + self.carried] * 2
        if self.carried:
            plan += [(2 + j, size, [2, 3], 2 * size, self.carried) for j in range(2)]
        own, out, own_too, out_too = move_rows(plan, sizes, operands, self.digits, after)
        self.terms = [[own, self.send(out, 2, 1)], [own_too, self.send(out_too, 1, 1)]]
        self.joined = False
        return own

    def third(self, phase, *after):
        parts = self.factors[phase] if phase < len(self.factors) else 1
        size = self.size // parts
        plan = []
        for j in range(parts):
            for lane in range(2):
                if self.joined:
                    at, base = list(range(len(self.terms))), lane * self.size
                else:
                    at, base = [2 * lane, 2 * lane + 1], 0
                come = (base, phase, j) if parts > 1 else base
                plan.append((j, lane * size, at, come, size))
            if self.carried:
                base = 2 * self.size if self.joined else self.size
                plan.append((j, 2 * size, at, base, self.carried))
        operands = self.terms if self.joined else self.terms[0] + self.terms[1]
        total = 2 * size + self.carried
        own, *others = move_rows(plan, [total] * parts, operands, self.digits, after)
        self.size, self.joined = size, True
        if parts > 1:
            self.terms = [own] + [self.send(o, phase, j + 1) for j, o in enumerate(others)]
        else:
            self.sums = own[2 * size :].astype(F32)
            self.pieces = [own[: 2 * size] if self.carried else own]
            self.spread(phase - 1)
        return own

    def spread(self, phase):
        held = self.pieces[0]
        self.pieces += [self.send(held, phase, j) for j in range(1, self.factors[phase])]

    def back(self, phase, *after):
        parts, size = self.factors[phase], self.size
        plan = []
        for j in range(parts):
            for lane in range(2):
                out = 0 if phase > 3 else lane
                base = lane * size * parts if phase > 3 else 0
                plan.append((out, (base, phase, j), [j], lane * size, size))
        self.size = size * parts
        sizes = [2 * self.size] if phase > 3 else [self.size] * 2
        held = move_rows(plan, sizes, self.pieces, self.digits, after)
        if phase > 3:
            self.pieces = list(held)
            self.spread(phase - 1)
        else:
            self.pieces = [held[0], self.send(held[0], 2, 1), held[1], self.send(held[1], 1, 1)]
        return held[0]

    def back_second(self, *after):
        size = self.size
        plan = [
            (lane, (0, 2 - lane, j), [2 * lane + j], 0, size) for lane in range(2) for j in range(2)
        ]
        self.size = 2 * size
        held = move_rows(plan, [self.size] * 2, self.pieces, self.digits, after)
        self.pieces = [held[0], self.send(held[0], 1, 1), held[1], self.send(held[1], 2, 1)]
        return held[0]

    def back_first(self, *after):
        size = self.size
        plan = [
            (0, (2 * lane * size, 1 + lane, j), [2 * lane + j], 0, size)
            for lane in range(2)
            for j in range(2)
        ]
        (held,) = move_rows(plan, [4 * size], self.pieces, self.digits, after)
        self.pieces = [held, self.send(held, 0, 1)]
        return held

    def finish(self, core, layout, half, shapes, *after):
        return unpack(*self.pieces, core, layout, half, shapes, after)


def cost(flops, nbytes, transcendentals=0):
    return pl.CostEstimate(
        flops=int(flops), bytes_accessed=int(nbytes), transcendentals=int(transcendentals)
    )


def whole(*shape):
    return pl.BlockSpec(shape, lambda *_: (0,) * len(shape))


def per_rows(pair, *shape):
    return pl.BlockSpec((pair, *shape), lambda r, *_: (r,) + (0,) * len(shape))


def struct(shape, dtype):
    return jax.ShapeDtypeStruct(shape, dtype)


def params(limit):
    return pltpu.CompilerParams(vmem_limit_bytes=limit * 1024 * 1024)


def body(
    target,
    memory,
    target_segments,
    memory_segments,
    cotangent,
    self_query,
    self_key,
    self_value,
    self_output,
    relative_bias,
    self_gain,
    cross_query,
    cross_key,
    cross_value,
    cross_output,
    cross_gain,
    ffn_gain,
    ffn_in,
    ffn_out,
):
    devices = lax.axis_size("dp")
    rows, length, width = target.shape
    held = memory.shape[0]
    span = held * devices
    heads = relative_bias.shape[1]
    inner = self_query.shape[1]
    head_size = inner // heads
    hidden_width = ffn_in.shape[1]
    chunks = hidden_width // width
    count = rows * length
    stacked = heads * length
    core = (lax.axis_index("dp") % 2).astype(jnp.int32).reshape(1)
    smem = pl.BlockSpec(memory_space=pltpu.SMEM)

    outgoing = by_row_first(memory).reshape(devices, rows, held, width)
    mem = lax.all_to_all(outgoing, "dp", split_axis=0, concat_axis=0, tiled=True)

    gain_one = self_gain.astype(F32).reshape(1, width)
    gain_two = cross_gain.astype(F32).reshape(1, width)
    gain_three = ffn_gain.astype(F32).reshape(1, width)
    table = bucket_table(length)
    onehot = jnp.asarray(table[None, :, :] == np.arange(NB)[:, None, None], dtype=BF16)
    bias = jnp.einsum("bh,bij->hij", relative_bias, onehot, preferred_element_type=F32)
    column = target_segments.reshape(rows, length, 1)
    line = target_segments.reshape(rows, 1, length)
    mem_line = memory_segments.reshape(rows, 1, span)

    tokens = struct((count, inner), BF16)
    h1, q, k, v, p1, o1, y1, h2, cq = pl.pallas_call(
        functools.partial(self_forward_kernel, rows, length, head_size),
        out_shape=[
            tokens,
            tokens,
            tokens,
            tokens,
            struct((rows, stacked, length), BF16),
            tokens,
            struct((count, width), F32),
            tokens,
            tokens,
        ],
        compiler_params=params(LIMITS["self_forward"]),
        cost_estimate=cost(2 * count * width * inner * 5, 12 * count * width),
        name="self_forward",
    )(
        target.reshape(count, width),
        column,
        line,
        bias,
        self_query,
        self_key,
        self_value,
        self_output,
        cross_query,
        gain_one,
        gain_two,
    )
    by_row = (rows, length, width)
    y1 = y1.reshape(by_row)
    cq = cq.reshape(by_row)
    h2 = h2.reshape(by_row)
    h1, q, k, v, o1 = (a.reshape(by_row) for a in (h1, q, k, v, o1))
    half = width // 2
    square = whole(width, inner)
    line_spec = whole(1, width)
    any_spec = pl.BlockSpec(memory_space=pl.ANY)
    pair = 2 if rows % 2 == 0 else 1
    per_row = functools.partial(per_rows, pair)
    here = per_row(length, width)
    mem_spec = pl.BlockSpec((devices, pair, held, width), lambda r: (0, r, 0, 0))
    one_mem_spec = pl.BlockSpec((devices, 1, held, width), lambda r: (0, r, 0, 0))
    one_keys_spec = per_rows(1, span, inner)
    keys_spec = per_row(span, inner)
    keys = struct((rows, span, inner), BF16)
    ck, cv, p2, o2, y2 = pl.pallas_call(
        functools.partial(cross_forward_kernel, length, head_size),
        grid=(rows // pair,),
        in_specs=[
            here,
            mem_spec,
            here,
            per_row(length, 1),
            per_row(1, span),
            square,
            square,
            square,
        ],
        out_specs=[keys_spec, keys_spec, per_row(stacked, span), here, here],
        out_shape=[
            keys,
            keys,
            struct((rows, stacked, span), BF16),
            struct(by_row, BF16),
            struct(by_row, F32),
        ],
        compiler_params=params(LIMITS["cross_forward"]),
        cost_estimate=cost(4 * rows * span * width * inner, 10 * rows * span * width),
        name="cross_forward",
    )(cq, mem, y1, column, mem_line, cross_key, cross_value, cross_output)

    full = whole(count, width)
    part_spec = pl.BlockSpec((2, 1, half, width), lambda c: (0, c, 0, 0))
    part = struct((2, chunks, half, width), BF16)
    layer_out, dy2, ffn_gain_grad, ffn_keep, ffn_send = pl.pallas_call(
        functools.partial(ffn_kernel, chunks),
        grid=(chunks,),
        in_specs=[
            smem,
            full,
            full,
            line_spec,
            pl.BlockSpec((width, width), lambda c: (0, c)),
            pl.BlockSpec((width, width), lambda c: (c, 0)),
        ],
        out_specs=[full, full, line_spec, part_spec, part_spec],
        out_shape=[
            struct((count, width), BF16),
            struct((count, width), F32),
            struct((1, width), F32),
            part,
            part,
        ],
        scratch_shapes=[
            pltpu.VMEM((count, width), BF16),
            pltpu.VMEM((count, width), F32),
            pltpu.VMEM((count, width), F32),
            pltpu.VMEM((2, width, width), F32),
        ],
        compiler_params=params(LIMITS["ffn"]),
        cost_estimate=cost(12 * count * width * hidden_width, 10 * width * hidden_width),
        name="ffn",
    )(core, y2.reshape(count, width), cotangent.reshape(count, width), gain_three, ffn_in, ffn_out)

    ffn_keep = ffn_keep.reshape(-1, width)
    ffn_other = swap_cores(ffn_send.reshape(-1, width))
    rows_each = chunks * half
    ffn_sum = Bucket([[(ffn_keep, ffn_other, lane * rows_each, rows_each)] for lane in range(2)])

    dy1, cross_gain_grad, mem_grad, dq, dk, dv = pl.pallas_call(
        functools.partial(cross_backward_kernel, length, head_size),
        grid=(rows // pair,),
        in_specs=[
            here,
            here,
            keys_spec,
            keys_spec,
            per_row(stacked, span),
            here,
            line_spec,
            square,
            square,
            square,
            square,
        ],
        out_specs=[here, line_spec, mem_spec, here, keys_spec, keys_spec],
        out_shape=[
            struct(by_row, F32),
            struct((1, width), F32),
            struct(mem.shape, BF16),
            struct(by_row, BF16),
            keys,
            keys,
        ],
        compiler_params=params(LIMITS["cross_backward"]),
        cost_estimate=cost(6 * rows * span * width * inner, 10 * rows * span * width),
        name="cross_backward",
    )(
        dy2.reshape(by_row),
        cq,
        ck,
        cv,
        p2,
        y1,
        gain_two,
        cross_query,
        cross_key,
        cross_value,
        cross_output,
    )
    passed = ffn_sum.first(dy1)
    returned = lax.all_to_all(
        tied(mem_grad, passed), "dp", split_axis=0, concat_axis=0, tiled=True
    )

    halves = struct((4 * half, width), BF16)
    halves_spec = whole(4 * half, width)
    cross_keep, cross_send = pl.pallas_call(
        functools.partial(cross_grads_kernel, rows),
        grid=(rows,),
        in_specs=[smem, any_spec, one_keys_spec, one_keys_spec, one_mem_spec]
        + [full] * 4,
        out_specs=[halves_spec, halves_spec],
        out_shape=[halves, halves],
        scratch_shapes=[pltpu.VMEM((4, width, inner), F32)],
        compiler_params=params(LIMITS["cross_grads"]),
        cost_estimate=cost(4 * rows * span * width * inner, 10 * rows * span * width),
        name="cross_grads",
    )(
        core,
        passed,
        dk,
        dv,
        mem,
        dq.reshape(count, inner),
        h2.reshape(count, width),
        o2.reshape(count, inner),
        dy2,
    )

    lanes = 256
    buckets = np.zeros((lanes, width), np.float32)
    for n in range(length):
        buckets[length - 1 - n, table[n, 0]] = 1.0
    packed = [struct((size, width), BF16) for size in (2 * half, half, half + CARRIED)] * 2
    target_grad, *self_halves = pl.pallas_call(
        functools.partial(self_backward_kernel, rows, length, head_size),
        grid=(rows // pair,),
        in_specs=[
            smem,
            any_spec,
            here,
            here,
            here,
            here,
            per_row(stacked, length),
            full,
            full,
            here,
            line_spec,
            square,
            square,
            square,
            square,
            line_spec,
            line_spec,
            whole(lanes, width),
        ],
        out_specs=[here] + [whole(*one.shape) for one in packed],
        out_shape=[struct(by_row, BF16)] + packed,
        scratch_shapes=[
            pltpu.VMEM((4, width, inner), F32),
            pltpu.VMEM((count, width), BF16),
            pltpu.VMEM((count, inner), BF16),
            pltpu.VMEM((count, inner), BF16),
            pltpu.VMEM((count, inner), BF16),
            pltpu.VMEM((1, width), F32),
            pltpu.VMEM((heads, length, length), F32),
        ],
        compiler_params=params(LIMITS["self_backward"]),
        cost_estimate=cost(2 * count * width * inner * 12, 12 * count * width),
        name="self_backward",
    )(
        core,
        cross_keep,
        dy1,
        q,
        k,
        v,
        p1,
        o1.reshape(count, inner),
        h1.reshape(count, width),
        target,
        gain_one,
        self_query,
        self_key,
        self_value,
        self_output,
        cross_gain_grad,
        ffn_gain_grad,
        jnp.asarray(buckets),
    )
    passed = ffn_sum.second(target_grad)
    cross_other = swap_cores(tied(cross_send, cross_keep))
    self_chunks = [
        (keep, swap_cores(send), 0, blocks * half)
        for blocks, keep, send in zip((2, 1, 1), self_halves[:3], self_halves[3:])
    ]
    attention_sum = Bucket([[(cross_keep, cross_other, 0, 4 * half)], self_chunks], CARRIED)
    phases = len(ffn_sum.factors)
    ahead = [functools.partial(ffn_sum.third, phase) for phase in range(3, phases + 1)]
    ahead += [functools.partial(ffn_sum.back, phase) for phase in range(phases - 1, 2, -1)]
    ahead += [ffn_sum.back_second, ffn_sum.back_first]
    behind = [attention_sum.first, attention_sum.second]
    behind += [functools.partial(attention_sum.third, phase) for phase in range(3, phases + 1)]
    behind += [functools.partial(attention_sum.back, phase) for phase in range(phases - 1, 2, -1)]
    for k, (one, other) in enumerate(zip(ahead, behind)):
        passed = one(other(passed))
        if k == len(ahead) - 3:
            memory_grad = by_position(returned, passed)
            passed = memory_grad
    ffn_layout = [(0, 0, c, 0, half) for c in range(chunks)]
    ffn_layout += [(1, c, 0, 0, half) for c in range(chunks)]
    small = attention_sum.sums
    ffn_in_grad, ffn_out_grad = ffn_sum.finish(
        core, ffn_layout, half, [(width, hidden_width), (hidden_width, width)], passed
    )
    passed = attention_sum.back_second(ffn_in_grad, small)
    passed = attention_sum.back_first(passed)
    attention_layout = [(part, 0, 0, 0, half) for part in range(4)]
    for part in range(2):
        attention_layout += [(4 + part, 0, 0, 0, half)]
        attention_layout += [(out, 0, 0, part * half // 2, half // 2) for out in (6, 7)]
    (
        cross_output_grad,
        cross_query_grad,
        cross_key_grad,
        cross_value_grad,
        self_output_grad,
        self_query_grad,
        self_key_grad,
        self_value_grad,
    ) = attention_sum.finish(core, attention_layout, half, [(width, inner)] * 8)
    return (
        layer_out.reshape(by_row),
        target_grad,
        memory_grad,
        self_query_grad,
        self_key_grad,
        self_value_grad,
        self_output_grad,
        small[3 : 3 + heads, :NB].T,
        small[0],
        cross_query_grad,
        cross_key_grad,
        cross_value_grad,
        cross_output_grad,
        small[1],
        small[2],
        ffn_in_grad,
        ffn_out_grad,
    )


def solution(mesh):
    rows3 = P("dp", None, None)
    rows2 = P("dp", None)
    in_specs = (rows3, rows3, rows2, rows2, rows3) + (P(),) * 14
    out_specs = (rows3, rows3, rows3) + (P(),) * 14
    return jax.shard_map(body, mesh=mesh, in_specs=in_specs, out_specs=out_specs, check_vma=False)
```

```python
import functools

import jax
import jax.numpy as jnp
import numpy as np
from jax import lax
from jax.experimental import pallas as pl
from jax.experimental.pallas import tpu as pltpu
from jax.sharding import PartitionSpec as P

NB = 32
MAXDIST = 128
EPS = 1e-06
GROUP = 256
CARRIED = 16
SECOND_HALF = 2
MASKED = -1000000000.0
LIMITS = {
    "by_row": 16,
    "self_forward": 36,
    "cross_forward": 56,
    "ffn": 56,
    "cross_backward": 56,
    "cross_grads": 56,
    "self_backward": 56,
    "by_position": 16,
    "move_rows": 16,
    "unpack": 16,
}
BF16 = jnp.bfloat16
F32 = jnp.float32


def bucket_table(length):
    exact = NB // 2
    offsets = np.arange(length)[:, None] - np.arange(length)[None, :]
    distance = np.maximum(offsets, 0)
    scaled = np.log(np.maximum(distance, exact) / exact) / np.log(MAXDIST / exact) * (NB - exact)
    farther = np.minimum(exact + scaled.astype(np.int32), NB - 1)
    return np.where(distance < exact, distance, farther).astype(np.int32)


def dot_nn(left, right):
    return lax.dot_general(left, right, (((1,), (0,)), ((), ())), preferred_element_type=F32)


def dot_nt(left, right):
    return lax.dot_general(left, right, (((1,), (1,)), ((), ())), preferred_element_type=F32)


def dot_tn(left, right):
    return lax.dot_general(left, right, (((0,), (0,)), ((), ())), preferred_element_type=F32)


def norm_factor(tensor):
    return lax.rsqrt(jnp.mean(tensor * tensor, axis=-1, keepdims=True) + EPS)


def norm_backward(tensor, gain, incoming):
    factor = norm_factor(tensor)
    scaled = tensor * factor
    shaped = incoming * gain
    inner = jnp.mean(scaled * shaped, axis=-1, keepdims=True)
    return factor * (shaped - scaled * inner), incoming * scaled


def head_masks(head_size, dtype):
    lane = lax.broadcasted_iota(jnp.int32, (1, GROUP), 1)
    return [
        jnp.where(lane // head_size == h, 1.0, 0.0).astype(dtype)
        for h in range(GROUP // head_size)
    ]


def stack_heads(tensor, masks):
    return jnp.concatenate([tensor * mask for mask in masks], axis=0)


def merge_heads(stacked, masks, length):
    out = stacked[:length] * masks[0]
    for h in range(1, len(masks)):
        out = out + stacked[h * length : (h + 1) * length] * masks[h]
    return out


def flat(ref):
    return ref[...].reshape(-1, ref.shape[-1])


def row_parts(size, index):
    return pl.ds(pl.multiple_of(index * size, 16), size)


def softmax_rows(scores):
    top = jnp.max(scores, axis=-1, keepdims=True)
    grown = jnp.exp(scores - top)
    return grown * (1.0 / jnp.sum(grown, axis=-1, keepdims=True))


def self_forward_kernel(
    rows,
    length,
    head_size,
    x_ref,
    column_ref,
    line_ref,
    bias_ref,
    query_ref,
    key_ref,
    value_ref,
    output_ref,
    cross_query_ref,
    gain_one_ref,
    gain_two_ref,
    h1_ref,
    q_ref,
    k_ref,
    v_ref,
    p_ref,
    o_ref,
    y1_ref,
    h2_ref,
    cq_ref,
):
    masks = head_masks(head_size, BF16)
    masks_f = head_masks(head_size, F32)
    x = x_ref[...].astype(F32)
    h1 = (x * norm_factor(x) * gain_one_ref[...]).astype(BF16)
    h1_ref[...] = h1
    q_ref[...] = dot_nn(h1, query_ref[...]).astype(BF16)
    k_ref[...] = dot_nn(h1, key_ref[...]).astype(BF16)
    v_ref[...] = dot_nn(h1, value_ref[...]).astype(BF16)
    i = lax.broadcasted_iota(jnp.int32, (length, length), 0)
    j = lax.broadcasted_iota(jnp.int32, (length, length), 1)

    def row(r, carry):
        here = pl.ds(pl.multiple_of(r * length, 16), length)
        allowed = jnp.logical_and(j <= i, column_ref[r] == line_ref[r])
        shift = jnp.where(allowed, 0.0, MASKED)
        for g in range(q_ref.shape[1] // GROUP):
            lanes = pl.ds(g * GROUP, GROUP)
            scores = dot_nt(stack_heads(q_ref[here, lanes], masks), k_ref[here, lanes])
            probs = []
            for h in range(len(masks)):
                one = scores[h * length : (h + 1) * length]
                one = one + bias_ref[g * len(masks) + h] + shift
                probs.append(softmax_rows(one).astype(BF16))
            stacked = jnp.concatenate(probs, axis=0)
            size = stacked.shape[0]
            p_ref[r, g * size : (g + 1) * size, :] = stacked
            mixed = merge_heads(dot_nn(stacked, v_ref[here, lanes]), masks_f, length)
            o_ref[here, lanes] = mixed.astype(BF16)
        return carry

    lax.fori_loop(0, rows, row, 0)
    y1 = x + dot_nn(o_ref[...], output_ref[...])
    y1_ref[...] = y1
    h2 = (y1 * norm_factor(y1) * gain_two_ref[...]).astype(BF16)
    h2_ref[...] = h2
    cq_ref[...] = dot_nn(h2, cross_query_ref[...]).astype(BF16)


def cross_forward_kernel(
    length,
    head_size,
    cq_ref,
    mem_ref,
    y1_ref,
    column_ref,
    line_ref,
    key_ref,
    value_ref,
    output_ref,
    ck_ref,
    cv_ref,
    p_ref,
    o_ref,
    y2_ref,
):
    masks = head_masks(head_size, BF16)
    masks_f = head_masks(head_size, F32)
    pair, span, inner = ck_ref.shape
    for r in range(pair):
        mem = mem_ref[:, r].reshape(span, -1)
        ck_ref[r] = dot_nn(mem, key_ref[...]).astype(BF16)
        cv_ref[r] = dot_nn(mem, value_ref[...]).astype(BF16)
    jobs = [(r, g) for r in range(pair) for g in range(inner // GROUP)]
    shift = [jnp.where(column_ref[r] == line_ref[r], 0.0, MASKED) for r in range(pair)]
    scores = {}
    for r, g in jobs:
        lanes = slice(g * GROUP, (g + 1) * GROUP)
        scores[r, g] = dot_nt(stack_heads(cq_ref[r, :, lanes], masks), ck_ref[r, :, lanes])
    for r, g in jobs:
        lanes = slice(g * GROUP, (g + 1) * GROUP)
        probs = []
        for h in range(len(masks)):
            one = scores[r, g][h * length : (h + 1) * length] + shift[r]
            probs.append(softmax_rows(one).astype(BF16))
        stacked = jnp.concatenate(probs, axis=0)
        size = stacked.shape[0]
        p_ref[r, g * size : (g + 1) * size, :] = stacked
        mixed = merge_heads(dot_nn(stacked, cv_ref[r, :, lanes]), masks_f, length)
        o_ref[r, :, lanes] = mixed.astype(BF16)
    y2 = flat(y1_ref) + dot_nn(flat(o_ref), output_ref[...])
    y2_ref[...] = y2.reshape(y2_ref.shape)


def ffn_kernel(
    chunks,
    core_ref,
    y2_ref,
    cot_ref,
    gain_ref,
    in_ref,
    out_ref,
    layer_ref,
    dy2_ref,
    gain_grad_ref,
    keep_ref,
    send_ref,
    h3_ref,
    total_ref,
    back_ref,
    grad_ref,
):
    step = pl.program_id(0)

    @pl.when(step == 0)
    def _():
        y2 = y2_ref[...]
        h3_ref[...] = (y2 * norm_factor(y2) * gain_ref[...]).astype(BF16)
        total_ref[...] = y2
        back_ref[...] = jnp.zeros_like(back_ref)

    h3 = h3_ref[...]
    cot = cot_ref[...]
    act = dot_nn(h3, in_ref[...])
    square = act * act
    root = float(np.sqrt(2.0 / np.pi))
    tanh = jnp.tanh(root * act * (1.0 + 0.044715 * square))
    gate = 0.5 + 0.5 * tanh
    hidden = (act * gate).astype(BF16)
    slope = gate + (0.5 * root) * act * (1.0 - tanh * tanh) * (1.0 + 3 * 0.044715 * square)
    act_grad = (slope * dot_nt(cot, out_ref[...])).astype(BF16)
    total_ref[...] += dot_nn(hidden, out_ref[...])
    back_ref[...] += dot_nt(act_grad, in_ref[...])
    half = keep_ref.shape[2]
    mine = row_parts(half, core_ref[0])
    other = row_parts(half, 1 - core_ref[0])
    grad_ref[0] = dot_tn(h3, act_grad)
    grad_ref[1] = dot_tn(hidden, cot)
    for part in range(2):
        keep_ref[part, 0] = grad_ref[part, mine, :].astype(BF16)
        send_ref[part, 0] = grad_ref[part, other, :].astype(BF16)

    @pl.when(step == chunks - 1)
    def _():
        layer_ref[...] = total_ref[...].astype(BF16)
        grad, gain_grad = norm_backward(y2_ref[...], gain_ref[...], back_ref[...])
        dy2_ref[...] = cot_ref[...].astype(F32) + grad
        gain_grad_ref[...] = jnp.sum(gain_grad, axis=0, keepdims=True)


def cross_backward_kernel(
    length,
    head_size,
    dy2_ref,
    cq_ref,
    ck_ref,
    cv_ref,
    p_ref,
    y1_ref,
    gain_ref,
    query_ref,
    key_ref,
    value_ref,
    output_ref,
    dy1_ref,
    gain_grad_ref,
    mem_grad_ref,
    dq_ref,
    dk_ref,
    dv_ref,
):
    masks = head_masks(head_size, BF16)
    masks_f = head_masks(head_size, F32)

    @pl.when(pl.program_id(0) == 0)
    def _():
        gain_grad_ref[...] = jnp.zeros_like(gain_grad_ref)

    pair = dy2_ref.shape[0]
    c2 = flat(dy2_ref).astype(BF16)
    do = dot_nt(c2, output_ref[...]).astype(BF16)
    jobs = [(r, g) for r in range(pair) for g in range(cq_ref.shape[2] // GROUP)]
    outs, upstream = {}, {}
    for r, g in jobs:
        lanes = slice(g * GROUP, (g + 1) * GROUP)
        outs[r, g] = stack_heads(do[r * length : (r + 1) * length, lanes], masks)
        upstream[r, g] = dot_nt(outs[r, g], cv_ref[r, :, lanes])
    for r, g in jobs:
        lanes = slice(g * GROUP, (g + 1) * GROUP)
        size = len(masks) * length
        probs = p_ref[r, g * size : (g + 1) * size, :]
        dv_ref[r, :, lanes] = dot_tn(probs, outs[r, g]).astype(BF16)
        pieces = []
        for h in range(len(masks)):
            prob = probs[h * length : (h + 1) * length].astype(F32)
            up = upstream[r, g][h * length : (h + 1) * length]
            pieces.append((prob * (up - jnp.sum(prob * up, axis=-1, keepdims=True))).astype(BF16))
        ds = jnp.concatenate(pieces, axis=0)
        queries = stack_heads(cq_ref[r, :, lanes], masks)
        dk_ref[r, :, lanes] = dot_tn(ds, queries).astype(BF16)
        mixed = merge_heads(dot_nn(ds, ck_ref[r, :, lanes]), masks_f, length)
        dq_ref[r, :, lanes] = mixed.astype(BF16)
    for r in range(pair):
        mem_grad = dot_nt(dk_ref[r], key_ref[...]) + dot_nt(dv_ref[r], value_ref[...])
        shape = (mem_grad_ref.shape[0], *mem_grad_ref.shape[2:])
        mem_grad_ref[:, r] = mem_grad.astype(BF16).reshape(shape)
    back = dot_nt(flat(dq_ref), query_ref[...])
    grad, gain_grad = norm_backward(flat(y1_ref), gain_ref[...], back)
    dy1_ref[...] = (flat(dy2_ref) + grad).reshape(dy1_ref.shape)
    gain_grad_ref[...] += jnp.sum(gain_grad, axis=0, keepdims=True)


def cross_grads_kernel(
    rows,
    core_ref,
    after_ref,
    dk_ref,
    dv_ref,
    mem_ref,
    dq_ref,
    h2_ref,
    o_ref,
    dy2_ref,
    keep_ref,
    send_ref,
    grad_ref,
):
    step = pl.program_id(0)
    mem = mem_ref[...].reshape(dk_ref.shape[1], -1)

    @pl.when(step == 0)
    def _():
        grad_ref[0] = dot_tn(o_ref[...], dy2_ref[...].astype(BF16))
        grad_ref[1] = dot_tn(h2_ref[...], dq_ref[...])
        grad_ref[2] = dot_tn(mem, dk_ref[0])
        grad_ref[3] = dot_tn(mem, dv_ref[0])

    @pl.when(step > 0)
    def _():
        grad_ref[2] += dot_tn(mem, dk_ref[0])
        grad_ref[3] += dot_tn(mem, dv_ref[0])

    @pl.when(step == rows - 1)
    def _():
        write_grads(core_ref, grad_ref, [keep_ref], [send_ref])


def write_grads(core_ref, grad_ref, keeps, sends):
    half = grad_ref.shape[1] // 2
    mine = row_parts(half, core_ref[0])
    other = row_parts(half, 1 - core_ref[0])
    part = 0
    for keep_ref, send_ref in zip(keeps, sends):
        for block in range(keep_ref.shape[0] // half):
            here = slice(block * half, (block + 1) * half)
            keep_ref[here, :] = grad_ref[part, mine, :].astype(BF16)
            send_ref[here, :] = grad_ref[part, other, :].astype(BF16)
            part += 1


def self_backward_kernel(
    rows,
    length,
    head_size,
    core_ref,
    after_ref,
    dy1_ref,
    q_ref,
    k_ref,
    v_ref,
    p_ref,
    o_ref,
    h1_ref,
    x_ref,
    gain_ref,
    query_ref,
    key_ref,
    value_ref,
    output_ref,
    cross_gain_ref,
    ffn_gain_ref,
    buckets_ref,
    dx_ref,
    keep_ref,
    next_keep_ref,
    last_keep_ref,
    send_ref,
    next_send_ref,
    last_send_ref,
    grad_ref,
    c1_ref,
    dq_ref,
    dk_ref,
    dv_ref,
    gain_total_ref,
    bias_grad_ref,
):
    step = pl.program_id(0)
    masks = head_masks(head_size, BF16)
    masks_f = head_masks(head_size, F32)
    pair = dy1_ref.shape[0]
    here = pl.ds(pl.multiple_of(step * pair * length, 16), pair * length)

    @pl.when(step == 0)
    def _():
        gain_total_ref[...] = jnp.zeros_like(gain_total_ref)
        bias_grad_ref[...] = jnp.zeros_like(bias_grad_ref)

    c1 = flat(dy1_ref).astype(BF16)
    c1_ref[here, :] = c1
    do = dot_nt(c1, output_ref[...]).astype(BF16)
    jobs = [(r, g) for r in range(pair) for g in range(q_ref.shape[2] // GROUP)]
    outs, upstream, total = {}, {}, {}
    for r, g in jobs:
        lanes = slice(g * GROUP, (g + 1) * GROUP)
        outs[r, g] = stack_heads(do[r * length : (r + 1) * length, lanes], masks)
        upstream[r, g] = dot_nt(outs[r, g], v_ref[r, :, lanes])
    for r, g in jobs:
        lanes = slice(g * GROUP, (g + 1) * GROUP)
        there = pl.ds(pl.multiple_of((step * pair + r) * length, 16), length)
        size = len(masks) * length
        probs = p_ref[r, g * size : (g + 1) * size, :]
        dv_ref[there, lanes] = dot_tn(probs, outs[r, g]).astype(BF16)
        pieces = []
        for h in range(len(masks)):
            prob = probs[h * length : (h + 1) * length].astype(F32)
            up = upstream[r, g][h * length : (h + 1) * length]
            one = (prob * (up - jnp.sum(prob * up, axis=-1, keepdims=True))).astype(BF16)
            pieces.append(one)
            total[g, h] = one.astype(F32) + total[g, h] if r else one.astype(F32)
        ds = jnp.concatenate(pieces, axis=0)
        queries = stack_heads(q_ref[r, :, lanes], masks)
        dk_ref[there, lanes] = dot_tn(ds, queries).astype(BF16)
        mixed = merge_heads(dot_nn(ds, k_ref[r, :, lanes]), masks_f, length)
        dq_ref[there, lanes] = mixed.astype(BF16)
    for (g, h), one in total.items():
        bias_grad_ref[g * len(masks) + h] += one
    back = dot_nt(dq_ref[here, :], query_ref[...])
    back = back + dot_nt(dk_ref[here, :], key_ref[...])
    back = back + dot_nt(dv_ref[here, :], value_ref[...])
    grad, gain_grad = norm_backward(flat(x_ref).astype(F32), gain_ref[...], back)
    dx_ref[...] = (flat(dy1_ref) + grad).astype(BF16).reshape(dx_ref.shape)
    gain_total_ref[...] += jnp.sum(gain_grad, axis=0, keepdims=True)

    @pl.when(step == rows // pair - 1)
    def _():
        h1 = h1_ref[...]
        grad_ref[0] = dot_tn(o_ref[...], c1_ref[...])
        grad_ref[1] = dot_tn(h1, dq_ref[...])
        grad_ref[2] = dot_tn(h1, dk_ref[...])
        grad_ref[3] = dot_tn(h1, dv_ref[...])
        keeps = [keep_ref, next_keep_ref, last_keep_ref]
        sends = [send_ref, next_send_ref, last_send_ref]
        write_grads(core_ref, grad_ref, keeps, sends)
        heads = bias_grad_ref.shape[0]
        lanes = buckets_ref.shape[0]
        flip = jnp.where(
            lax.broadcasted_iota(jnp.int32, (length, length), 0)
            + lax.broadcasted_iota(jnp.int32, (length, length), 1)
            == length - 1,
            1.0,
            0.0,
        ).astype(BF16)
        diagonals = []
        for h in range(heads):
            flipped = dot_nn(flip, bias_grad_ref[h].astype(BF16))
            padded = jnp.concatenate([flipped, jnp.zeros((length, lanes - length), F32)], axis=1)
            skewed = pltpu.roll(padded, 0, 1, stride=1, stride_axis=0)
            diagonals.append(jnp.sum(skewed, axis=0, keepdims=True))
        sums = dot_nn(jnp.concatenate(diagonals, axis=0), buckets_ref[...])
        small = jnp.concatenate(
            [
                gain_total_ref[...],
                cross_gain_ref[...],
                ffn_gain_ref[...],
                sums,
                jnp.zeros((CARRIED - 3 - heads, sums.shape[1]), F32),
            ],
            axis=0,
        ).astype(BF16)
        for result in (last_keep_ref, last_send_ref):
            result[result.shape[0] - CARRIED :, :] = small


def factors_of(n):
    factors = []
    while n > 1:
        factor = next(f for f in range(2, n + 1) if n % f == 0)
        factors.append(factor)
        n //= factor
    return factors


def partners(n, stride, factor, j):
    moves = []
    for i in range(n):
        digit = (i // stride) % factor
        moves.append((i, i + ((digit ^ j) - digit) * stride))
    return moves


def move_kernel(plan, operands, digits_ref, *refs):
    ins, outs = refs[:operands], refs[operands:]

    def rows_at(place, size):
        if isinstance(place, int):
            return slice(place, place + size)
        base, digit, j = place
        start = base + (digits_ref[digit] ^ j) * size
        return pl.ds(pl.multiple_of(start, 16), size)

    for out, to, sources, come, size in plan:
        if len(sources) == 1:
            rows = ins[sources[0]][rows_at(come, size), :]
        else:
            terms = [ins[source][rows_at(come, size), :].astype(F32) for source in sources]
            while len(terms) > 1:
                terms = [terms[i] + terms[i + 1] for i in range(0, len(terms), 2)]
            rows = terms[0].astype(BF16)
        outs[len(outs) - 1 - out][rows_at(to, size), :] = rows


def move_rows(plan, sizes, operands, digits, after):
    columns = operands[0].shape[1]
    vmem = pl.BlockSpec(memory_space=pltpu.VMEM)
    results = pl.pallas_call(
        functools.partial(move_kernel, plan, len(operands)),
        in_specs=[pl.BlockSpec(memory_space=pltpu.SMEM)]
        + [vmem] * len(operands)
        + [pl.BlockSpec(memory_space=pl.ANY)] * len(after),
        out_specs=[vmem] * len(sizes),
        out_shape=[struct((size, columns), BF16) for size in sizes[::-1]],
        compiler_params=params(LIMITS["move_rows"]),
        cost_estimate=cost(0, 4 * sum(sizes) * columns),
        name="move_rows",
    )(digits, *operands, *after)
    return results[::-1]


def unpack_kernel(layout, half, core_ref, own_ref, other_ref, *refs):
    outs = refs[-1 - max(entry[0] for entry in layout) :]
    width = own_ref.shape[1]
    start = 0
    for out, row, column, offset, size in layout:
        columns = pl.ds(column * width, width)
        for ref, core in ((own_ref, core_ref[0]), (other_ref, 1 - core_ref[0])):
            first = pl.multiple_of(row * 2 * half + core * half + offset, 16)
            rows = ref[start : start + size, :].astype(F32)
            outs[out][pl.ds(first, size), columns] = rows
        start += size


def unpack(own, other, core, layout, half, shapes, after):
    vmem = pl.BlockSpec(memory_space=pltpu.VMEM)
    return pl.pallas_call(
        functools.partial(unpack_kernel, layout, half),
        in_specs=[pl.BlockSpec(memory_space=pltpu.SMEM), vmem, vmem]
        + [pl.BlockSpec(memory_space=pl.ANY)] * len(after),
        out_specs=[vmem] * len(shapes),
        out_shape=[struct(shape, F32) for shape in shapes],
        compiler_params=params(LIMITS["unpack"]),
        cost_estimate=cost(0, 12 * own.shape[0] * own.shape[1]),
        name="unpack",
    )(core, own, other, *after)


def turned(rows, first, second):
    size = first * second
    to = lax.broadcasted_iota(jnp.int32, (size, size), 0)
    come = lax.broadcasted_iota(jnp.int32, (size, size), 1)
    here = to % first * second + to // first == come
    return dot_nn(jnp.where(here, 1.0, 0.0).astype(BF16), rows).astype(BF16)


def by_row_kernel(rows, memory_ref, out_ref):
    held, count, width = memory_ref.shape
    for g in range(count // rows):
        part = memory_ref[:, g * rows : (g + 1) * rows, :].reshape(held * rows, width)
        out_ref[g * rows : (g + 1) * rows] = turned(part, held, rows).reshape(rows, held, width)


def by_row_first(memory):
    held, count, width = memory.shape
    rows = GROUP // held
    if held % 16 or rows % 16 or count % (4 * rows):
        return jnp.swapaxes(memory, 0, 1)
    return pl.pallas_call(
        functools.partial(by_row_kernel, rows),
        grid=(count // (4 * rows),),
        in_specs=[pl.BlockSpec((held, 4 * rows, width), lambda g: (0, g, 0))],
        out_specs=pl.BlockSpec((4 * rows, held, width), lambda g: (g, 0, 0)),
        out_shape=struct((count, held, width), BF16),
        compiler_params=params(LIMITS["by_row"]),
        cost_estimate=cost(2 * GROUP * count * held * width, 4 * count * held * width),
        name="by_row",
    )(memory)


def by_position_kernel(rows, rows_ref, after_ref, out_ref):
    held, width = rows_ref.shape[3:]
    each = rows_ref.shape[2]
    owners = rows // each
    for g in range(rows_ref.shape[0] // owners):
        part = rows_ref[g * owners : (g + 1) * owners].reshape(rows * held, width)
        part = turned(part, rows, held).reshape(held, rows, width)
        out_ref[:, g * rows : (g + 1) * rows, :] = part


def by_position(returned, after):
    inner, outer, each, held, width = returned.shape
    count = inner * outer * each
    rows = GROUP // held
    if held % 16 or rows % 16 or rows % each or inner * each % rows:
        returned = jnp.swapaxes(returned, 0, 1).reshape(count, held, width)
        return jnp.swapaxes(returned, 0, 1)
    return pl.pallas_call(
        functools.partial(by_position_kernel, rows),
        grid=(outer,),
        in_specs=[
            pl.BlockSpec((inner, 1, each, held, width), lambda g: (0, g, 0, 0, 0)),
            pl.BlockSpec(memory_space=pl.ANY),
        ],
        out_specs=pl.BlockSpec((held, inner * each, width), lambda g: (0, g, 0)),
        out_shape=struct((held, count, width), BF16),
        compiler_params=params(LIMITS["by_position"]),
        cost_estimate=cost(2 * GROUP * count * held * width, 4 * count * held * width),
        name="by_position",
    )(returned, after)


def tied(rows, *after):
    return lax.optimization_barrier((rows, *after))[0]


def swap_cores(rows):
    n = lax.axis_size("dp")
    return lax.ppermute(rows, "dp", [(i, i ^ 1) for i in range(n)])


class Bucket:
    def __init__(self, lanes, carried=0):
        n, me = lax.axis_size("dp"), lax.axis_index("dp")
        self.carried = carried
        self.factors = factors_of(n)
        self.moves, digits, stride = [], [], 1
        for factor in self.factors:
            digits.append((me // stride) % factor)
            self.moves.append([partners(n, stride, factor, j) for j in range(factor)])
            stride *= factor
        self.digits = jnp.stack(digits).astype(jnp.int32)
        self.lanes = lanes

    def send(self, rows, phase, j):
        return lax.ppermute(rows, "dp", self.moves[phase][j])

    def first(self, *after):
        operands, plan, sizes = [], [], []
        for lane, chunks in enumerate(self.lanes):
            start = 0
            for mine, theirs, base, rows in chunks:
                at = []
                for operand in (mine, theirs):
                    if not any(operand is other for other in operands):
                        operands.append(operand)
                    at += [k for k, other in enumerate(operands) if other is operand]
                for j in range(2):
                    plan.append((2 * lane + j, start, at, (base, 1 + lane, j), rows // 2))
                start += rows // 2
            sizes += [start, start]
        if self.carried:
            plan += [(2 + j, sizes[2], at, base + rows, self.carried) for j in range(2)]
            sizes[2] += self.carried
            sizes[3] += self.carried
        own, out, own_too, out_too = move_rows(plan, sizes, operands, self.digits, after)
        self.size = sizes[0]
        self.terms = [[own, self.send(out, 1, 1)], [own_too, self.send(out_too, 2, 1)]]
        return own

    def second(self, *after):
        size = self.size = self.size // 2
        operands = self.terms[0] + self.terms[1]
        plan = []
        for lane in range(2):
            at = [2 * lane, 2 * lane + 1]
            for j in range(2):
                plan.append((2 * lane + j, 0, at, (0, 2 - lane, j), size))
        sizes = [size] * 2 + [size + self.carried] * 2
        if self.carried:
            plan += [(2 + j, size, [2, 3], 2 * size, self.carried) for j in range(2)]
        own, out, own_too, out_too = move_rows(plan, sizes, operands, self.digits, after)
        self.terms = [[own, self.send(out, 2, 1)], [own_too, self.send(out_too, 1, 1)]]
        self.joined = False
        return own

    def third(self, phase, *after):
        parts = self.factors[phase] if phase < len(self.factors) else 1
        size = self.size // parts
        plan = []
        for j in range(parts):
            for lane in range(2):
                if self.joined:
                    at, base = list(range(len(self.terms))), lane * self.size
                else:
                    at, base = [2 * lane, 2 * lane + 1], 0
                come = (base, phase, j) if parts > 1 else base
                plan.append((j, lane * size, at, come, size))
            if self.carried:
                base = 2 * self.size if self.joined else self.size
                plan.append((j, 2 * size, at, base, self.carried))
        operands = self.terms if self.joined else self.terms[0] + self.terms[1]
        total = 2 * size + self.carried
        own, *others = move_rows(plan, [total] * parts, operands, self.digits, after)
        self.size, self.joined = size, True
        if parts > 1:
            self.terms = [own] + [self.send(o, phase, j + 1) for j, o in enumerate(others)]
        else:
            self.sums = own[2 * size :].astype(F32)
            self.pieces = [own[: 2 * size] if self.carried else own]
            self.spread(phase - 1)
        return own

    def spread(self, phase):
        held = self.pieces[0]
        self.pieces += [self.send(held, phase, j) for j in range(1, self.factors[phase])]

    def back(self, phase, *after):
        parts, size = self.factors[phase], self.size
        plan = []
        for j in range(parts):
            for lane in range(2):
                out = 0 if phase > 3 else lane
                base = lane * size * parts if phase > 3 else 0
                plan.append((out, (base, phase, j), [j], lane * size, size))
        self.size = size * parts
        sizes = [2 * self.size] if phase > 3 else [self.size] * 2
        held = move_rows(plan, sizes, self.pieces, self.digits, after)
        if phase > 3:
            self.pieces = list(held)
            self.spread(phase - 1)
        else:
            self.pieces = [held[0], self.send(held[0], 2, 1), held[1], self.send(held[1], 1, 1)]
        return held[0]

    def back_second(self, *after):
        size = self.size
        plan = [
            (lane, (0, 2 - lane, j), [2 * lane + j], 0, size) for lane in range(2) for j in range(2)
        ]
        self.size = 2 * size
        held = move_rows(plan, [self.size] * 2, self.pieces, self.digits, after)
        self.pieces = [held[0], self.send(held[0], 1, 1), held[1], self.send(held[1], 2, 1)]
        return held[0]

    def back_first(self, *after):
        size = self.size
        plan = [
            (0, (2 * lane * size, 1 + lane, j), [2 * lane + j], 0, size)
            for lane in range(2)
            for j in range(2)
        ]
        (held,) = move_rows(plan, [4 * size], self.pieces, self.digits, after)
        self.pieces = [held, self.send(held, 0, 1)]
        return held

    def finish(self, core, layout, half, shapes, *after):
        return unpack(*self.pieces, core, layout, half, shapes, after)


def cost(flops, nbytes, transcendentals=0):
    return pl.CostEstimate(
        flops=int(flops), bytes_accessed=int(nbytes), transcendentals=int(transcendentals)
    )


def whole(*shape):
    return pl.BlockSpec(shape, lambda *_: (0,) * len(shape))


def per_rows(pair, *shape):
    return pl.BlockSpec((pair, *shape), lambda r, *_: (r,) + (0,) * len(shape))


def struct(shape, dtype):
    return jax.ShapeDtypeStruct(shape, dtype)


def params(limit):
    return pltpu.CompilerParams(vmem_limit_bytes=limit * 1024 * 1024)


def body(
    target,
    memory,
    target_segments,
    memory_segments,
    cotangent,
    self_query,
    self_key,
    self_value,
    self_output,
    relative_bias,
    self_gain,
    cross_query,
    cross_key,
    cross_value,
    cross_output,
    cross_gain,
    ffn_gain,
    ffn_in,
    ffn_out,
):
    devices = lax.axis_size("dp")
    rows, length, width = target.shape
    held = memory.shape[0]
    span = held * devices
    heads = relative_bias.shape[1]
    inner = self_query.shape[1]
    head_size = inner // heads
    hidden_width = ffn_in.shape[1]
    chunks = hidden_width // width
    count = rows * length
    stacked = heads * length
    core = (lax.axis_index("dp") % 2).astype(jnp.int32).reshape(1)
    smem = pl.BlockSpec(memory_space=pltpu.SMEM)

    outgoing = by_row_first(memory).reshape(devices, rows, held, width)
    mem = lax.all_to_all(outgoing, "dp", split_axis=0, concat_axis=0, tiled=True)

    gain_one = self_gain.astype(F32).reshape(1, width)
    gain_two = cross_gain.astype(F32).reshape(1, width)
    gain_three = ffn_gain.astype(F32).reshape(1, width)
    table = bucket_table(length)
    onehot = jnp.asarray(table[None, :, :] == np.arange(NB)[:, None, None], dtype=BF16)
    bias = jnp.einsum("bh,bij->hij", relative_bias, onehot, preferred_element_type=F32)
    column = target_segments.reshape(rows, length, 1)
    line = target_segments.reshape(rows, 1, length)
    mem_line = memory_segments.reshape(rows, 1, span)

    tokens = struct((count, inner), BF16)
    h1, q, k, v, p1, o1, y1, h2, cq = pl.pallas_call(
        functools.partial(self_forward_kernel, rows, length, head_size),
        out_shape=[
            tokens,
            tokens,
            tokens,
            tokens,
            struct((rows, stacked, length), BF16),
            tokens,
            struct((count, width), F32),
            tokens,
            tokens,
        ],
        compiler_params=params(LIMITS["self_forward"]),
        cost_estimate=cost(2 * count * width * inner * 5, 12 * count * width),
        name="self_forward",
    )(
        target.reshape(count, width),
        column,
        line,
        bias,
        self_query,
        self_key,
        self_value,
        self_output,
        cross_query,
        gain_one,
        gain_two,
    )
    by_row = (rows, length, width)
    y1 = y1.reshape(by_row)
    cq = cq.reshape(by_row)
    h2 = h2.reshape(by_row)
    h1, q, k, v, o1 = (a.reshape(by_row) for a in (h1, q, k, v, o1))
    half = width // 2
    square = whole(width, inner)
    line_spec = whole(1, width)
    any_spec = pl.BlockSpec(memory_space=pl.ANY)
    pair = 2 if rows % 2 == 0 else 1
    per_row = functools.partial(per_rows, pair)
    here = per_row(length, width)
    mem_spec = pl.BlockSpec((devices, pair, held, width), lambda r: (0, r, 0, 0))
    one_mem_spec = pl.BlockSpec((devices, 1, held, width), lambda r: (0, r, 0, 0))
    one_keys_spec = per_rows(1, span, inner)
    keys_spec = per_row(span, inner)
    keys = struct((rows, span, inner), BF16)
    ck, cv, p2, o2, y2 = pl.pallas_call(
        functools.partial(cross_forward_kernel, length, head_size),
        grid=(rows // pair,),
        in_specs=[
            here,
            mem_spec,
            here,
            per_row(length, 1),
            per_row(1, span),
            square,
            square,
            square,
        ],
        out_specs=[keys_spec, keys_spec, per_row(stacked, span), here, here],
        out_shape=[
            keys,
            keys,
            struct((rows, stacked, span), BF16),
            struct(by_row, BF16),
            struct(by_row, F32),
        ],
        compiler_params=params(LIMITS["cross_forward"]),
        cost_estimate=cost(4 * rows * span * width * inner, 10 * rows * span * width),
        name="cross_forward",
    )(cq, mem, y1, column, mem_line, cross_key, cross_value, cross_output)

    full = whole(count, width)
    part_spec = pl.BlockSpec((2, 1, half, width), lambda c: (0, c, 0, 0))
    part = struct((2, chunks, half, width), BF16)
    layer_out, dy2, ffn_gain_grad, ffn_keep, ffn_send = pl.pallas_call(
        functools.partial(ffn_kernel, chunks),
        grid=(chunks,),
        in_specs=[
            smem,
            full,
            full,
            line_spec,
            pl.BlockSpec((width, width), lambda c: (0, c)),
            pl.BlockSpec((width, width), lambda c: (c, 0)),
        ],
        out_specs=[full, full, line_spec, part_spec, part_spec],
        out_shape=[
            struct((count, width), BF16),
            struct((count, width), F32),
            struct((1, width), F32),
            part,
            part,
        ],
        scratch_shapes=[
            pltpu.VMEM((count, width), BF16),
            pltpu.VMEM((count, width), F32),
            pltpu.VMEM((count, width), F32),
            pltpu.VMEM((2, width, width), F32),
        ],
        compiler_params=params(LIMITS["ffn"]),
        cost_estimate=cost(12 * count * width * hidden_width, 10 * width * hidden_width),
        name="ffn",
    )(core, y2.reshape(count, width), cotangent.reshape(count, width), gain_three, ffn_in, ffn_out)

    ffn_keep = ffn_keep.reshape(-1, width)
    ffn_other = swap_cores(ffn_send.reshape(-1, width))
    rows_each = chunks * half
    ffn_sum = Bucket([[(ffn_keep, ffn_other, lane * rows_each, rows_each)] for lane in range(2)])

    dy1, cross_gain_grad, mem_grad, dq, dk, dv = pl.pallas_call(
        functools.partial(cross_backward_kernel, length, head_size),
        grid=(rows // pair,),
        in_specs=[
            here,
            here,
            keys_spec,
            keys_spec,
            per_row(stacked, span),
            here,
            line_spec,
            square,
            square,
            square,
            square,
        ],
        out_specs=[here, line_spec, mem_spec, here, keys_spec, keys_spec],
        out_shape=[
            struct(by_row, F32),
            struct((1, width), F32),
            struct(mem.shape, BF16),
            struct(by_row, BF16),
            keys,
            keys,
        ],
        compiler_params=params(LIMITS["cross_backward"]),
        cost_estimate=cost(6 * rows * span * width * inner, 10 * rows * span * width),
        name="cross_backward",
    )(
        dy2.reshape(by_row),
        cq,
        ck,
        cv,
        p2,
        y1,
        gain_two,
        cross_query,
        cross_key,
        cross_value,
        cross_output,
    )
    passed = ffn_sum.first(dy1)
    inner_devices = 8 if devices % 8 == 0 else 1
    outer_devices = devices // inner_devices
    lines = [
        [o * inner_devices + i for o in range(outer_devices)] for i in range(inner_devices)
    ]
    blocks_of = [
        [o * inner_devices + i for i in range(inner_devices)] for o in range(outer_devices)
    ]

    def exchange(array, groups):
        return lax.all_to_all(
            array, "dp", split_axis=0, concat_axis=0, tiled=True, axis_index_groups=groups
        )

    halfway = mem_grad.reshape(outer_devices, inner_devices, rows, held, width)
    halfway = exchange(tied(halfway, passed), lines)

    halves = struct((4 * half, width), BF16)
    halves_spec = whole(4 * half, width)
    cross_keep, cross_send = pl.pallas_call(
        functools.partial(cross_grads_kernel, rows),
        grid=(rows,),
        in_specs=[smem, any_spec, one_keys_spec, one_keys_spec, one_mem_spec]
        + [full] * 4,
        out_specs=[halves_spec, halves_spec],
        out_shape=[halves, halves],
        scratch_shapes=[pltpu.VMEM((4, width, inner), F32)],
        compiler_params=params(LIMITS["cross_grads"]),
        cost_estimate=cost(4 * rows * span * width * inner, 10 * rows * span * width),
        name="cross_grads",
    )(
        core,
        passed,
        dk,
        dv,
        mem,
        dq.reshape(count, inner),
        h2.reshape(count, width),
        o2.reshape(count, inner),
        dy2,
    )

    lanes = 256
    buckets = np.zeros((lanes, width), np.float32)
    for n in range(length):
        buckets[length - 1 - n, table[n, 0]] = 1.0
    packed = [struct((size, width), BF16) for size in (2 * half, half, half + CARRIED)] * 2
    target_grad, *self_halves = pl.pallas_call(
        functools.partial(self_backward_kernel, rows, length, head_size),
        grid=(rows // pair,),
        in_specs=[
            smem,
            any_spec,
            here,
            here,
            here,
            here,
            per_row(stacked, length),
            full,
            full,
            here,
            line_spec,
            square,
            square,
            square,
            square,
            line_spec,
            line_spec,
            whole(lanes, width),
        ],
        out_specs=[here] + [whole(*one.shape) for one in packed],
        out_shape=[struct(by_row, BF16)] + packed,
        scratch_shapes=[
            pltpu.VMEM((4, width, inner), F32),
            pltpu.VMEM((count, width), BF16),
            pltpu.VMEM((count, inner), BF16),
            pltpu.VMEM((count, inner), BF16),
            pltpu.VMEM((count, inner), BF16),
            pltpu.VMEM((1, width), F32),
            pltpu.VMEM((heads, length, length), F32),
        ],
        compiler_params=params(LIMITS["self_backward"]),
        cost_estimate=cost(2 * count * width * inner * 12, 12 * count * width),
        name="self_backward",
    )(
        core,
        cross_keep,
        dy1,
        q,
        k,
        v,
        p1,
        o1.reshape(count, inner),
        h1.reshape(count, width),
        target,
        gain_one,
        self_query,
        self_key,
        self_value,
        self_output,
        cross_gain_grad,
        ffn_gain_grad,
        jnp.asarray(buckets),
    )
    passed = ffn_sum.second(target_grad)
    cross_other = swap_cores(tied(cross_send, cross_keep))
    self_chunks = [
        (keep, swap_cores(send), 0, blocks * half)
        for blocks, keep, send in zip((2, 1, 1), self_halves[:3], self_halves[3:])
    ]
    attention_sum = Bucket([[(cross_keep, cross_other, 0, 4 * half)], self_chunks], CARRIED)
    phases = len(ffn_sum.factors)
    ahead = [functools.partial(ffn_sum.third, phase) for phase in range(3, phases + 1)]
    ahead += [functools.partial(ffn_sum.back, phase) for phase in range(phases - 1, 2, -1)]
    ahead += [ffn_sum.back_second, ffn_sum.back_first]
    behind = [attention_sum.first, attention_sum.second]
    behind += [functools.partial(attention_sum.third, phase) for phase in range(3, phases + 1)]
    behind += [functools.partial(attention_sum.back, phase) for phase in range(phases - 1, 2, -1)]
    for k, (one, other) in enumerate(zip(ahead, behind)):
        passed = one(other(passed))
        if k == SECOND_HALF:
            returned = exchange(tied(jnp.swapaxes(halfway, 0, 1), passed), blocks_of)
        if k == len(ahead) - 2:
            memory_grad = by_position(returned, passed)
            passed = memory_grad
    ffn_layout = [(0, 0, c, 0, half) for c in range(chunks)]
    ffn_layout += [(1, c, 0, 0, half) for c in range(chunks)]
    small = attention_sum.sums
    ffn_in_grad, ffn_out_grad = ffn_sum.finish(
        core, ffn_layout, half, [(width, hidden_width), (hidden_width, width)], passed
    )
    passed = attention_sum.back_second(ffn_in_grad, small)
    passed = attention_sum.back_first(passed)
    attention_layout = [(part, 0, 0, 0, half) for part in range(4)]
    for part in range(2):
        attention_layout += [(4 + part, 0, 0, 0, half)]
        attention_layout += [(out, 0, 0, part * half // 2, half // 2) for out in (6, 7)]
    (
        cross_output_grad,
        cross_query_grad,
        cross_key_grad,
        cross_value_grad,
        self_output_grad,
        self_query_grad,
        self_key_grad,
        self_value_grad,
    ) = attention_sum.finish(core, attention_layout, half, [(width, inner)] * 8)
    return (
        layer_out.reshape(by_row),
        target_grad,
        memory_grad,
        self_query_grad,
        self_key_grad,
        self_value_grad,
        self_output_grad,
        small[3 : 3 + heads, :NB].T,
        small[0],
        cross_query_grad,
        cross_key_grad,
        cross_value_grad,
        cross_output_grad,
        small[1],
        small[2],
        ffn_in_grad,
        ffn_out_grad,
    )


def solution(mesh):
    rows3 = P("dp", None, None)
    rows2 = P("dp", None)
    in_specs = (rows3, rows3, rows2, rows2, rows3) + (P(),) * 14
    out_specs = (rows3, rows3, rows3) + (P(),) * 14
    return jax.shard_map(body, mesh=mesh, in_specs=in_specs, out_specs=out_specs, check_vma=False)
```

```python
import functools

import jax
import jax.numpy as jnp
import numpy as np
from jax import lax
from jax.experimental import pallas as pl
from jax.experimental.pallas import tpu as pltpu
from jax.sharding import PartitionSpec as P

NB = 32
MAXDIST = 128
EPS = 1e-06
GROUP = 256
CARRIED = 16
SECOND_HALF = 2
MASKED = -1000000000.0
LIMITS = {
    "by_row": 16,
    "self_forward": 36,
    "cross_forward": 56,
    "ffn": 56,
    "cross_backward": 56,
    "cross_grads": 56,
    "self_backward": 56,
    "by_position": 16,
    "move_rows": 16,
    "unpack": 16,
}
BF16 = jnp.bfloat16
F32 = jnp.float32


def bucket_table(length):
    exact = NB // 2
    offsets = np.arange(length)[:, None] - np.arange(length)[None, :]
    distance = np.maximum(offsets, 0)
    scaled = np.log(np.maximum(distance, exact) / exact) / np.log(MAXDIST / exact) * (NB - exact)
    farther = np.minimum(exact + scaled.astype(np.int32), NB - 1)
    return np.where(distance < exact, distance, farther).astype(np.int32)


def dot_nn(left, right):
    return lax.dot_general(left, right, (((1,), (0,)), ((), ())), preferred_element_type=F32)


def dot_nt(left, right):
    return lax.dot_general(left, right, (((1,), (1,)), ((), ())), preferred_element_type=F32)


def dot_tn(left, right):
    return lax.dot_general(left, right, (((0,), (0,)), ((), ())), preferred_element_type=F32)


def norm_factor(tensor):
    return lax.rsqrt(jnp.mean(tensor * tensor, axis=-1, keepdims=True) + EPS)


def norm_backward(tensor, gain, incoming):
    factor = norm_factor(tensor)
    scaled = tensor * factor
    shaped = incoming * gain
    inner = jnp.mean(scaled * shaped, axis=-1, keepdims=True)
    return factor * (shaped - scaled * inner), incoming * scaled


def head_masks(head_size, dtype):
    lane = lax.broadcasted_iota(jnp.int32, (1, GROUP), 1)
    return [
        jnp.where(lane // head_size == h, 1.0, 0.0).astype(dtype)
        for h in range(GROUP // head_size)
    ]


def stack_heads(tensor, masks):
    return jnp.concatenate([tensor * mask for mask in masks], axis=0)


def merge_heads(stacked, masks, length):
    out = stacked[:length] * masks[0]
    for h in range(1, len(masks)):
        out = out + stacked[h * length : (h + 1) * length] * masks[h]
    return out


def flat(ref):
    return ref[...].reshape(-1, ref.shape[-1])


def row_parts(size, index):
    return pl.ds(pl.multiple_of(index * size, 16), size)


def softmax_rows(scores):
    top = jnp.max(scores, axis=-1, keepdims=True)
    grown = jnp.exp(scores - top)
    return grown * (1.0 / jnp.sum(grown, axis=-1, keepdims=True))


def self_forward_kernel(
    rows,
    length,
    head_size,
    x_ref,
    column_ref,
    line_ref,
    bias_ref,
    query_ref,
    key_ref,
    value_ref,
    output_ref,
    cross_query_ref,
    gain_one_ref,
    gain_two_ref,
    h1_ref,
    q_ref,
    k_ref,
    v_ref,
    p_ref,
    o_ref,
    y1_ref,
    h2_ref,
    cq_ref,
):
    masks = head_masks(head_size, BF16)
    masks_f = head_masks(head_size, F32)
    x = x_ref[...].astype(F32)
    h1 = (x * norm_factor(x) * gain_one_ref[...]).astype(BF16)
    h1_ref[...] = h1
    q_ref[...] = dot_nn(h1, query_ref[...]).astype(BF16)
    k_ref[...] = dot_nn(h1, key_ref[...]).astype(BF16)
    v_ref[...] = dot_nn(h1, value_ref[...]).astype(BF16)
    i = lax.broadcasted_iota(jnp.int32, (length, length), 0)
    j = lax.broadcasted_iota(jnp.int32, (length, length), 1)

    def row(r, carry):
        here = pl.ds(pl.multiple_of(r * length, 16), length)
        allowed = jnp.logical_and(j <= i, column_ref[r] == line_ref[r])
        shift = jnp.where(allowed, 0.0, MASKED)
        for g in range(q_ref.shape[1] // GROUP):
            lanes = pl.ds(g * GROUP, GROUP)
            scores = dot_nt(stack_heads(q_ref[here, lanes], masks), k_ref[here, lanes])
            probs = []
            for h in range(len(masks)):
                one = scores[h * length : (h + 1) * length]
                one = one + bias_ref[g * len(masks) + h] + shift
                probs.append(softmax_rows(one).astype(BF16))
            stacked = jnp.concatenate(probs, axis=0)
            size = stacked.shape[0]
            p_ref[r, g * size : (g + 1) * size, :] = stacked
            mixed = merge_heads(dot_nn(stacked, v_ref[here, lanes]), masks_f, length)
            o_ref[here, lanes] = mixed.astype(BF16)
        return carry

    lax.fori_loop(0, rows, row, 0)
    y1 = x + dot_nn(o_ref[...], output_ref[...])
    y1_ref[...] = y1
    h2 = (y1 * norm_factor(y1) * gain_two_ref[...]).astype(BF16)
    h2_ref[...] = h2
    cq_ref[...] = dot_nn(h2, cross_query_ref[...]).astype(BF16)


def cross_forward_kernel(
    length,
    head_size,
    cq_ref,
    mem_ref,
    y1_ref,
    column_ref,
    line_ref,
    key_ref,
    value_ref,
    output_ref,
    ck_ref,
    cv_ref,
    p_ref,
    o_ref,
    y2_ref,
):
    masks = head_masks(head_size, BF16)
    masks_f = head_masks(head_size, F32)
    pair, span, inner = ck_ref.shape
    for r in range(pair):
        mem = mem_ref[:, r].reshape(span, -1)
        ck_ref[r] = dot_nn(mem, key_ref[...]).astype(BF16)
        cv_ref[r] = dot_nn(mem, value_ref[...]).astype(BF16)
    jobs = [(r, g) for r in range(pair) for g in range(inner // GROUP)]
    shift = [jnp.where(column_ref[r] == line_ref[r], 0.0, MASKED) for r in range(pair)]
    scores = {}
    for r, g in jobs:
        lanes = slice(g * GROUP, (g + 1) * GROUP)
        scores[r, g] = dot_nt(stack_heads(cq_ref[r, :, lanes], masks), ck_ref[r, :, lanes])
    for r, g in jobs:
        lanes = slice(g * GROUP, (g + 1) * GROUP)
        probs = []
        for h in range(len(masks)):
            one = scores[r, g][h * length : (h + 1) * length] + shift[r]
            probs.append(softmax_rows(one).astype(BF16))
        stacked = jnp.concatenate(probs, axis=0)
        size = stacked.shape[0]
        p_ref[r, g * size : (g + 1) * size, :] = stacked
        mixed = merge_heads(dot_nn(stacked, cv_ref[r, :, lanes]), masks_f, length)
        o_ref[r, :, lanes] = mixed.astype(BF16)
    y2 = flat(y1_ref) + dot_nn(flat(o_ref), output_ref[...])
    y2_ref[...] = y2.reshape(y2_ref.shape)


def ffn_kernel(
    chunks,
    core_ref,
    y2_ref,
    cot_ref,
    gain_ref,
    in_ref,
    out_ref,
    layer_ref,
    dy2_ref,
    gain_grad_ref,
    keep_ref,
    send_ref,
    h3_ref,
    total_ref,
    back_ref,
    grad_ref,
):
    step = pl.program_id(0)

    @pl.when(step == 0)
    def _():
        y2 = y2_ref[...]
        h3_ref[...] = (y2 * norm_factor(y2) * gain_ref[...]).astype(BF16)
        total_ref[...] = y2
        back_ref[...] = jnp.zeros_like(back_ref)

    h3 = h3_ref[...]
    cot = cot_ref[...]
    act = dot_nn(h3, in_ref[...])
    square = act * act
    root = float(np.sqrt(2.0 / np.pi))
    tanh = jnp.tanh(root * act * (1.0 + 0.044715 * square))
    gate = 0.5 + 0.5 * tanh
    hidden = (act * gate).astype(BF16)
    slope = gate + (0.5 * root) * act * (1.0 - tanh * tanh) * (1.0 + 3 * 0.044715 * square)
    act_grad = (slope * dot_nt(cot, out_ref[...])).astype(BF16)
    total_ref[...] += dot_nn(hidden, out_ref[...])
    back_ref[...] += dot_nt(act_grad, in_ref[...])
    half = keep_ref.shape[2]
    mine = row_parts(half, core_ref[0])
    other = row_parts(half, 1 - core_ref[0])
    grad_ref[0] = dot_tn(h3, act_grad)
    grad_ref[1] = dot_tn(hidden, cot)
    for part in range(2):
        keep_ref[part, 0] = grad_ref[part, mine, :].astype(BF16)
        send_ref[part, 0] = grad_ref[part, other, :].astype(BF16)

    @pl.when(step == chunks - 1)
    def _():
        layer_ref[...] = total_ref[...].astype(BF16)
        grad, gain_grad = norm_backward(y2_ref[...], gain_ref[...], back_ref[...])
        dy2_ref[...] = cot_ref[...].astype(F32) + grad
        gain_grad_ref[...] = jnp.sum(gain_grad, axis=0, keepdims=True)


def cross_backward_kernel(
    length,
    head_size,
    dy2_ref,
    cq_ref,
    ck_ref,
    cv_ref,
    p_ref,
    y1_ref,
    gain_ref,
    query_ref,
    key_ref,
    value_ref,
    output_ref,
    dy1_ref,
    gain_grad_ref,
    mem_grad_ref,
    dq_ref,
    dk_ref,
    dv_ref,
):
    masks = head_masks(head_size, BF16)
    masks_f = head_masks(head_size, F32)

    @pl.when(pl.program_id(0) == 0)
    def _():
        gain_grad_ref[...] = jnp.zeros_like(gain_grad_ref)

    pair = dy2_ref.shape[0]
    c2 = flat(dy2_ref).astype(BF16)
    do = dot_nt(c2, output_ref[...]).astype(BF16)
    jobs = [(r, g) for r in range(pair) for g in range(cq_ref.shape[2] // GROUP)]
    outs, upstream = {}, {}
    for r, g in jobs:
        lanes = slice(g * GROUP, (g + 1) * GROUP)
        outs[r, g] = stack_heads(do[r * length : (r + 1) * length, lanes], masks)
        upstream[r, g] = dot_nt(outs[r, g], cv_ref[r, :, lanes])
    for r, g in jobs:
        lanes = slice(g * GROUP, (g + 1) * GROUP)
        size = len(masks) * length
        probs = p_ref[r, g * size : (g + 1) * size, :]
        dv_ref[r, :, lanes] = dot_tn(probs, outs[r, g]).astype(BF16)
        pieces = []
        for h in range(len(masks)):
            prob = probs[h * length : (h + 1) * length].astype(F32)
            up = upstream[r, g][h * length : (h + 1) * length]
            pieces.append((prob * (up - jnp.sum(prob * up, axis=-1, keepdims=True))).astype(BF16))
        ds = jnp.concatenate(pieces, axis=0)
        queries = stack_heads(cq_ref[r, :, lanes], masks)
        dk_ref[r, :, lanes] = dot_tn(ds, queries).astype(BF16)
        mixed = merge_heads(dot_nn(ds, ck_ref[r, :, lanes]), masks_f, length)
        dq_ref[r, :, lanes] = mixed.astype(BF16)
    for r in range(pair):
        mem_grad = dot_nt(dk_ref[r], key_ref[...]) + dot_nt(dv_ref[r], value_ref[...])
        shape = (mem_grad_ref.shape[0], *mem_grad_ref.shape[2:])
        mem_grad_ref[:, r] = mem_grad.astype(BF16).reshape(shape)
    back = dot_nt(flat(dq_ref), query_ref[...])
    grad, gain_grad = norm_backward(flat(y1_ref), gain_ref[...], back)
    dy1_ref[...] = (flat(dy2_ref) + grad).reshape(dy1_ref.shape)
    gain_grad_ref[...] += jnp.sum(gain_grad, axis=0, keepdims=True)


def cross_grads_kernel(
    rows,
    core_ref,
    after_ref,
    dk_ref,
    dv_ref,
    mem_ref,
    dq_ref,
    h2_ref,
    o_ref,
    dy2_ref,
    keep_ref,
    send_ref,
    grad_ref,
):
    step = pl.program_id(0)
    pair, span, _ = dk_ref.shape
    key_grad, value_grad = None, None
    for r in range(pair):
        mem = mem_ref[:, r].reshape(span, -1)
        one, other = dot_tn(mem, dk_ref[r]), dot_tn(mem, dv_ref[r])
        key_grad = key_grad + one if r else one
        value_grad = value_grad + other if r else other

    @pl.when(step == 0)
    def _():
        grad_ref[0] = dot_tn(o_ref[...], dy2_ref[...].astype(BF16))
        grad_ref[1] = dot_tn(h2_ref[...], dq_ref[...])
        grad_ref[2] = key_grad
        grad_ref[3] = value_grad

    @pl.when(step > 0)
    def _():
        grad_ref[2] += key_grad
        grad_ref[3] += value_grad

    @pl.when(step == rows // pair - 1)
    def _():
        write_grads(core_ref, grad_ref, [keep_ref], [send_ref])


def write_grads(core_ref, grad_ref, keeps, sends):
    half = grad_ref.shape[1] // 2
    mine = row_parts(half, core_ref[0])
    other = row_parts(half, 1 - core_ref[0])
    part = 0
    for keep_ref, send_ref in zip(keeps, sends):
        for block in range(keep_ref.shape[0] // half):
            here = slice(block * half, (block + 1) * half)
            keep_ref[here, :] = grad_ref[part, mine, :].astype(BF16)
            send_ref[here, :] = grad_ref[part, other, :].astype(BF16)
            part += 1


def self_backward_kernel(
    rows,
    length,
    head_size,
    core_ref,
    after_ref,
    dy1_ref,
    q_ref,
    k_ref,
    v_ref,
    p_ref,
    o_ref,
    h1_ref,
    x_ref,
    gain_ref,
    query_ref,
    key_ref,
    value_ref,
    output_ref,
    cross_gain_ref,
    ffn_gain_ref,
    buckets_ref,
    dx_ref,
    keep_ref,
    next_keep_ref,
    last_keep_ref,
    send_ref,
    next_send_ref,
    last_send_ref,
    grad_ref,
    c1_ref,
    dq_ref,
    dk_ref,
    dv_ref,
    gain_total_ref,
    bias_grad_ref,
):
    step = pl.program_id(0)
    masks = head_masks(head_size, BF16)
    masks_f = head_masks(head_size, F32)
    pair = dy1_ref.shape[0]
    here = pl.ds(pl.multiple_of(step * pair * length, 16), pair * length)

    @pl.when(step == 0)
    def _():
        gain_total_ref[...] = jnp.zeros_like(gain_total_ref)
        bias_grad_ref[...] = jnp.zeros_like(bias_grad_ref)

    c1 = flat(dy1_ref).astype(BF16)
    c1_ref[here, :] = c1
    do = dot_nt(c1, output_ref[...]).astype(BF16)
    jobs = [(r, g) for r in range(pair) for g in range(q_ref.shape[2] // GROUP)]
    outs, upstream, total = {}, {}, {}
    for r, g in jobs:
        lanes = slice(g * GROUP, (g + 1) * GROUP)
        outs[r, g] = stack_heads(do[r * length : (r + 1) * length, lanes], masks)
        upstream[r, g] = dot_nt(outs[r, g], v_ref[r, :, lanes])
    for r, g in jobs:
        lanes = slice(g * GROUP, (g + 1) * GROUP)
        there = pl.ds(pl.multiple_of((step * pair + r) * length, 16), length)
        size = len(masks) * length
        probs = p_ref[r, g * size : (g + 1) * size, :]
        dv_ref[there, lanes] = dot_tn(probs, outs[r, g]).astype(BF16)
        pieces = []
        for h in range(len(masks)):
            prob = probs[h * length : (h + 1) * length].astype(F32)
            up = upstream[r, g][h * length : (h + 1) * length]
            one = (prob * (up - jnp.sum(prob * up, axis=-1, keepdims=True))).astype(BF16)
            pieces.append(one)
            total[g, h] = one.astype(F32) + total[g, h] if r else one.astype(F32)
        ds = jnp.concatenate(pieces, axis=0)
        queries = stack_heads(q_ref[r, :, lanes], masks)
        dk_ref[there, lanes] = dot_tn(ds, queries).astype(BF16)
        mixed = merge_heads(dot_nn(ds, k_ref[r, :, lanes]), masks_f, length)
        dq_ref[there, lanes] = mixed.astype(BF16)
    for (g, h), one in total.items():
        bias_grad_ref[g * len(masks) + h] += one
    back = dot_nt(dq_ref[here, :], query_ref[...])
    back = back + dot_nt(dk_ref[here, :], key_ref[...])
    back = back + dot_nt(dv_ref[here, :], value_ref[...])
    grad, gain_grad = norm_backward(flat(x_ref).astype(F32), gain_ref[...], back)
    dx_ref[...] = (flat(dy1_ref) + grad).astype(BF16).reshape(dx_ref.shape)
    gain_total_ref[...] += jnp.sum(gain_grad, axis=0, keepdims=True)

    @pl.when(step == rows // pair - 1)
    def _():
        h1 = h1_ref[...]
        grad_ref[0] = dot_tn(o_ref[...], c1_ref[...])
        grad_ref[1] = dot_tn(h1, dq_ref[...])
        grad_ref[2] = dot_tn(h1, dk_ref[...])
        grad_ref[3] = dot_tn(h1, dv_ref[...])
        keeps = [keep_ref, next_keep_ref, last_keep_ref]
        sends = [send_ref, next_send_ref, last_send_ref]
        write_grads(core_ref, grad_ref, keeps, sends)
        heads = bias_grad_ref.shape[0]
        lanes = buckets_ref.shape[0]
        flip = jnp.where(
            lax.broadcasted_iota(jnp.int32, (length, length), 0)
            + lax.broadcasted_iota(jnp.int32, (length, length), 1)
            == length - 1,
            1.0,
            0.0,
        ).astype(BF16)
        diagonals = []
        for h in range(heads):
            flipped = dot_nn(flip, bias_grad_ref[h].astype(BF16))
            padded = jnp.concatenate([flipped, jnp.zeros((length, lanes - length), F32)], axis=1)
            skewed = pltpu.roll(padded, 0, 1, stride=1, stride_axis=0)
            diagonals.append(jnp.sum(skewed, axis=0, keepdims=True))
        sums = dot_nn(jnp.concatenate(diagonals, axis=0), buckets_ref[...])
        small = jnp.concatenate(
            [
                gain_total_ref[...],
                cross_gain_ref[...],
                ffn_gain_ref[...],
                sums,
                jnp.zeros((CARRIED - 3 - heads, sums.shape[1]), F32),
            ],
            axis=0,
        ).astype(BF16)
        for result in (last_keep_ref, last_send_ref):
            result[result.shape[0] - CARRIED :, :] = small


def factors_of(n):
    factors = []
    while n > 1:
        factor = next(f for f in range(2, n + 1) if n % f == 0)
        factors.append(factor)
        n //= factor
    return factors


def partners(n, stride, factor, j):
    moves = []
    for i in range(n):
        digit = (i // stride) % factor
        moves.append((i, i + ((digit ^ j) - digit) * stride))
    return moves


def move_kernel(plan, operands, digits_ref, *refs):
    ins, outs = refs[:operands], refs[operands:]

    def rows_at(place, size):
        if isinstance(place, int):
            return slice(place, place + size)
        base, digit, j = place
        start = base + (digits_ref[digit] ^ j) * size
        return pl.ds(pl.multiple_of(start, 16), size)

    for out, to, sources, come, size in plan:
        if len(sources) == 1:
            rows = ins[sources[0]][rows_at(come, size), :]
        else:
            terms = [ins[source][rows_at(come, size), :].astype(F32) for source in sources]
            while len(terms) > 1:
                terms = [terms[i] + terms[i + 1] for i in range(0, len(terms), 2)]
            rows = terms[0].astype(BF16)
        outs[len(outs) - 1 - out][rows_at(to, size), :] = rows


def move_rows(plan, sizes, operands, digits, after):
    columns = operands[0].shape[1]
    vmem = pl.BlockSpec(memory_space=pltpu.VMEM)
    results = pl.pallas_call(
        functools.partial(move_kernel, plan, len(operands)),
        in_specs=[pl.BlockSpec(memory_space=pltpu.SMEM)]
        + [vmem] * len(operands)
        + [pl.BlockSpec(memory_space=pl.ANY)] * len(after),
        out_specs=[vmem] * len(sizes),
        out_shape=[struct((size, columns), BF16) for size in sizes[::-1]],
        compiler_params=params(LIMITS["move_rows"]),
        cost_estimate=cost(0, 4 * sum(sizes) * columns),
        name="move_rows",
    )(digits, *operands, *after)
    return results[::-1]


def unpack_kernel(layout, half, core_ref, own_ref, other_ref, *refs):
    outs = refs[-2 - max(entry[0] for entry in layout) : -1]
    refs[-1][...] = jnp.zeros_like(refs[-1])
    width = own_ref.shape[1]
    start = 0
    for out, row, column, offset, size in layout:
        columns = pl.ds(column * width, width)
        for ref, core in ((own_ref, core_ref[0]), (other_ref, 1 - core_ref[0])):
            first = pl.multiple_of(row * 2 * half + core * half + offset, 16)
            rows = ref[start : start + size, :].astype(F32)
            outs[out][pl.ds(first, size), columns] = rows
        start += size


def unpack(own, other, core, layout, half, shapes, after):
    vmem = pl.BlockSpec(memory_space=pltpu.VMEM)
    return pl.pallas_call(
        functools.partial(unpack_kernel, layout, half),
        in_specs=[pl.BlockSpec(memory_space=pltpu.SMEM), vmem, vmem]
        + [pl.BlockSpec(memory_space=pl.ANY)] * len(after),
        out_specs=[vmem] * (len(shapes) + 1),
        out_shape=[struct(shape, F32) for shape in (*shapes, (8, 128))],
        compiler_params=params(LIMITS["unpack"]),
        cost_estimate=cost(0, 12 * own.shape[0] * own.shape[1]),
        name="unpack",
    )(core, own, other, *after)


def turned(rows, first, second):
    size = first * second
    to = lax.broadcasted_iota(jnp.int32, (size, size), 0)
    come = lax.broadcasted_iota(jnp.int32, (size, size), 1)
    here = to % first * second + to // first == come
    return dot_nn(jnp.where(here, 1.0, 0.0).astype(BF16), rows).astype(BF16)


def by_row_kernel(rows, memory_ref, out_ref):
    held, count, width = memory_ref.shape
    for g in range(count // rows):
        part = memory_ref[:, g * rows : (g + 1) * rows, :].reshape(held * rows, width)
        out_ref[g * rows : (g + 1) * rows] = turned(part, held, rows).reshape(rows, held, width)


def by_row_first(memory):
    held, count, width = memory.shape
    rows = GROUP // held
    if held % 16 or rows % 16 or count % (4 * rows):
        return jnp.swapaxes(memory, 0, 1)
    return pl.pallas_call(
        functools.partial(by_row_kernel, rows),
        grid=(count // (4 * rows),),
        in_specs=[pl.BlockSpec((held, 4 * rows, width), lambda g: (0, g, 0))],
        out_specs=pl.BlockSpec((4 * rows, held, width), lambda g: (g, 0, 0)),
        out_shape=struct((count, held, width), BF16),
        compiler_params=params(LIMITS["by_row"]),
        cost_estimate=cost(2 * GROUP * count * held * width, 4 * count * held * width),
        name="by_row",
    )(memory)


def by_position_kernel(rows, rows_ref, after_ref, out_ref, token_ref):
    token_ref[...] = jnp.zeros_like(token_ref)
    held, width = rows_ref.shape[3:]
    each = rows_ref.shape[2]
    owners = rows // each
    for g in range(rows_ref.shape[0] // owners):
        part = rows_ref[g * owners : (g + 1) * owners].reshape(rows * held, width)
        part = turned(part, rows, held).reshape(held, rows, width)
        out_ref[:, g * rows : (g + 1) * rows, :] = part


def by_position(returned, after):
    inner, outer, each, held, width = returned.shape
    count = inner * outer * each
    rows = GROUP // held
    if held % 16 or rows % 16 or rows % each or inner * each % rows:
        returned = jnp.swapaxes(returned, 0, 1).reshape(count, held, width)
        return jnp.swapaxes(returned, 0, 1), after
    return pl.pallas_call(
        functools.partial(by_position_kernel, rows),
        grid=(outer,),
        in_specs=[
            pl.BlockSpec((inner, 1, each, held, width), lambda g: (0, g, 0, 0, 0)),
            pl.BlockSpec(memory_space=pl.ANY),
        ],
        out_specs=[pl.BlockSpec((held, inner * each, width), lambda g: (0, g, 0)), whole(8, 128)],
        out_shape=[struct((held, count, width), BF16), struct((8, 128), F32)],
        compiler_params=params(LIMITS["by_position"]),
        cost_estimate=cost(2 * GROUP * count * held * width, 4 * count * held * width),
        name="by_position",
    )(returned, after)


def tied(rows, *after):
    return lax.optimization_barrier((rows, *after))[0]


def swap_cores(rows):
    n = lax.axis_size("dp")
    return lax.ppermute(rows, "dp", [(i, i ^ 1) for i in range(n)])


class Bucket:
    def __init__(self, lanes, carried=0):
        n, me = lax.axis_size("dp"), lax.axis_index("dp")
        self.carried = carried
        self.factors = factors_of(n)
        self.moves, digits, stride = [], [], 1
        for factor in self.factors:
            digits.append((me // stride) % factor)
            self.moves.append([partners(n, stride, factor, j) for j in range(factor)])
            stride *= factor
        self.digits = jnp.stack(digits).astype(jnp.int32)
        self.lanes = lanes

    def send(self, rows, phase, j):
        return lax.ppermute(rows, "dp", self.moves[phase][j])

    def first(self, *after):
        operands, plan, sizes = [], [], []
        for lane, chunks in enumerate(self.lanes):
            start = 0
            for mine, theirs, base, rows in chunks:
                at = []
                for operand in (mine, theirs):
                    if not any(operand is other for other in operands):
                        operands.append(operand)
                    at += [k for k, other in enumerate(operands) if other is operand]
                for j in range(2):
                    plan.append((2 * lane + j, start, at, (base, 1 + lane, j), rows // 2))
                start += rows // 2
            sizes += [start, start]
        if self.carried:
            plan += [(2 + j, sizes[2], at, base + rows, self.carried) for j in range(2)]
            sizes[2] += self.carried
            sizes[3] += self.carried
        own, out, own_too, out_too = move_rows(plan, sizes, operands, self.digits, after)
        self.size = sizes[0]
        self.terms = [[own, self.send(out, 1, 1)], [own_too, self.send(out_too, 2, 1)]]
        return own

    def second(self, *after):
        size = self.size = self.size // 2
        operands = self.terms[0] + self.terms[1]
        plan = []
        for lane in range(2):
            at = [2 * lane, 2 * lane + 1]
            for j in range(2):
                plan.append((2 * lane + j, 0, at, (0, 2 - lane, j), size))
        sizes = [size] * 2 + [size + self.carried] * 2
        if self.carried:
            plan += [(2 + j, size, [2, 3], 2 * size, self.carried) for j in range(2)]
        own, out, own_too, out_too = move_rows(plan, sizes, operands, self.digits, after)
        self.terms = [[own, self.send(out, 2, 1)], [own_too, self.send(out_too, 1, 1)]]
        self.joined = False
        return own

    def third(self, phase, *after):
        parts = self.factors[phase] if phase < len(self.factors) else 1
        size = self.size // parts
        plan = []
        for j in range(parts):
            for lane in range(2):
                if self.joined:
                    at, base = list(range(len(self.terms))), lane * self.size
                else:
                    at, base = [2 * lane, 2 * lane + 1], 0
                come = (base, phase, j) if parts > 1 else base
                plan.append((j, lane * size, at, come, size))
            if self.carried:
                base = 2 * self.size if self.joined else self.size
                plan.append((j, 2 * size, at, base, self.carried))
        operands = self.terms if self.joined else self.terms[0] + self.terms[1]
        total = 2 * size + self.carried
        own, *others = move_rows(plan, [total] * parts, operands, self.digits, after)
        self.size, self.joined = size, True
        if parts > 1:
            self.terms = [own] + [self.send(o, phase, j + 1) for j, o in enumerate(others)]
        else:
            self.sums = own[2 * size :].astype(F32)
            self.pieces = [own[: 2 * size] if self.carried else own]
            self.spread(phase - 1)
        return own

    def spread(self, phase):
        held = self.pieces[0]
        self.pieces += [self.send(held, phase, j) for j in range(1, self.factors[phase])]

    def back(self, phase, *after):
        parts, size = self.factors[phase], self.size
        plan = []
        for j in range(parts):
            for lane in range(2):
                out = 0 if phase > 3 else lane
                base = lane * size * parts if phase > 3 else 0
                plan.append((out, (base, phase, j), [j], lane * size, size))
        self.size = size * parts
        sizes = [2 * self.size] if phase > 3 else [self.size] * 2
        held = move_rows(plan, sizes, self.pieces, self.digits, after)
        if phase > 3:
            self.pieces = list(held)
            self.spread(phase - 1)
        else:
            self.pieces = [held[0], self.send(held[0], 2, 1), held[1], self.send(held[1], 1, 1)]
        return held[0]

    def back_second(self, *after):
        size = self.size
        plan = [
            (lane, (0, 2 - lane, j), [2 * lane + j], 0, size) for lane in range(2) for j in range(2)
        ]
        self.size = 2 * size
        held = move_rows(plan, [self.size] * 2, self.pieces, self.digits, after)
        self.pieces = [held[0], self.send(held[0], 1, 1), held[1], self.send(held[1], 2, 1)]
        return held[0]

    def back_first(self, *after):
        size = self.size
        plan = [
            (0, (2 * lane * size, 1 + lane, j), [2 * lane + j], 0, size)
            for lane in range(2)
            for j in range(2)
        ]
        (held,) = move_rows(plan, [4 * size], self.pieces, self.digits, after)
        self.pieces = [held, self.send(held, 0, 1)]
        return held

    def finish(self, core, layout, half, shapes, *after):
        return unpack(*self.pieces, core, layout, half, shapes, after)


def cost(flops, nbytes, transcendentals=0):
    return pl.CostEstimate(
        flops=int(flops), bytes_accessed=int(nbytes), transcendentals=int(transcendentals)
    )


def whole(*shape):
    return pl.BlockSpec(shape, lambda *_: (0,) * len(shape))


def per_rows(pair, *shape):
    return pl.BlockSpec((pair, *shape), lambda r, *_: (r,) + (0,) * len(shape))


def struct(shape, dtype):
    return jax.ShapeDtypeStruct(shape, dtype)


def params(limit):
    return pltpu.CompilerParams(vmem_limit_bytes=limit * 1024 * 1024)


def body(
    target,
    memory,
    target_segments,
    memory_segments,
    cotangent,
    self_query,
    self_key,
    self_value,
    self_output,
    relative_bias,
    self_gain,
    cross_query,
    cross_key,
    cross_value,
    cross_output,
    cross_gain,
    ffn_gain,
    ffn_in,
    ffn_out,
):
    devices = lax.axis_size("dp")
    rows, length, width = target.shape
    held = memory.shape[0]
    span = held * devices
    heads = relative_bias.shape[1]
    inner = self_query.shape[1]
    head_size = inner // heads
    hidden_width = ffn_in.shape[1]
    chunks = hidden_width // width
    count = rows * length
    stacked = heads * length
    core = (lax.axis_index("dp") % 2).astype(jnp.int32).reshape(1)
    smem = pl.BlockSpec(memory_space=pltpu.SMEM)

    outgoing = by_row_first(memory).reshape(devices, rows, held, width)
    mem = lax.all_to_all(outgoing, "dp", split_axis=0, concat_axis=0, tiled=True)

    gain_one = self_gain.astype(F32).reshape(1, width)
    gain_two = cross_gain.astype(F32).reshape(1, width)
    gain_three = ffn_gain.astype(F32).reshape(1, width)
    table = bucket_table(length)
    onehot = jnp.asarray(table[None, :, :] == np.arange(NB)[:, None, None], dtype=BF16)
    bias = jnp.einsum("bh,bij->hij", relative_bias, onehot, preferred_element_type=F32)
    column = target_segments.reshape(rows, length, 1)
    line = target_segments.reshape(rows, 1, length)
    mem_line = memory_segments.reshape(rows, 1, span)

    tokens = struct((count, inner), BF16)
    h1, q, k, v, p1, o1, y1, h2, cq = pl.pallas_call(
        functools.partial(self_forward_kernel, rows, length, head_size),
        out_shape=[
            tokens,
            tokens,
            tokens,
            tokens,
            struct((rows, stacked, length), BF16),
            tokens,
            struct((count, width), F32),
            tokens,
            tokens,
        ],
        compiler_params=params(LIMITS["self_forward"]),
        cost_estimate=cost(2 * count * width * inner * 5, 12 * count * width),
        name="self_forward",
    )(
        target.reshape(count, width),
        column,
        line,
        bias,
        self_query,
        self_key,
        self_value,
        self_output,
        cross_query,
        gain_one,
        gain_two,
    )
    by_row = (rows, length, width)
    y1 = y1.reshape(by_row)
    cq = cq.reshape(by_row)
    h2 = h2.reshape(by_row)
    h1, q, k, v, o1 = (a.reshape(by_row) for a in (h1, q, k, v, o1))
    half = width // 2
    square = whole(width, inner)
    line_spec = whole(1, width)
    any_spec = pl.BlockSpec(memory_space=pl.ANY)
    pair = 2 if rows % 2 == 0 else 1
    per_row = functools.partial(per_rows, pair)
    here = per_row(length, width)
    mem_spec = pl.BlockSpec((devices, pair, held, width), lambda r: (0, r, 0, 0))
    keys_spec = per_row(span, inner)
    keys = struct((rows, span, inner), BF16)
    ck, cv, p2, o2, y2 = pl.pallas_call(
        functools.partial(cross_forward_kernel, length, head_size),
        grid=(rows // pair,),
        in_specs=[
            here,
            mem_spec,
            here,
            per_row(length, 1),
            per_row(1, span),
            square,
            square,
            square,
        ],
        out_specs=[keys_spec, keys_spec, per_row(stacked, span), here, here],
        out_shape=[
            keys,
            keys,
            struct((rows, stacked, span), BF16),
            struct(by_row, BF16),
            struct(by_row, F32),
        ],
        compiler_params=params(LIMITS["cross_forward"]),
        cost_estimate=cost(4 * rows * span * width * inner, 10 * rows * span * width),
        name="cross_forward",
    )(cq, mem, y1, column, mem_line, cross_key, cross_value, cross_output)

    full = whole(count, width)
    part_spec = pl.BlockSpec((2, 1, half, width), lambda c: (0, c, 0, 0))
    part = struct((2, chunks, half, width), BF16)
    layer_out, dy2, ffn_gain_grad, ffn_keep, ffn_send = pl.pallas_call(
        functools.partial(ffn_kernel, chunks),
        grid=(chunks,),
        in_specs=[
            smem,
            full,
            full,
            line_spec,
            pl.BlockSpec((width, width), lambda c: (0, c)),
            pl.BlockSpec((width, width), lambda c: (c, 0)),
        ],
        out_specs=[full, full, line_spec, part_spec, part_spec],
        out_shape=[
            struct((count, width), BF16),
            struct((count, width), F32),
            struct((1, width), F32),
            part,
            part,
        ],
        scratch_shapes=[
            pltpu.VMEM((count, width), BF16),
            pltpu.VMEM((count, width), F32),
            pltpu.VMEM((count, width), F32),
            pltpu.VMEM((2, width, width), F32),
        ],
        compiler_params=params(LIMITS["ffn"]),
        cost_estimate=cost(12 * count * width * hidden_width, 10 * width * hidden_width),
        name="ffn",
    )(core, y2.reshape(count, width), cotangent.reshape(count, width), gain_three, ffn_in, ffn_out)

    ffn_keep = ffn_keep.reshape(-1, width)
    ffn_other = swap_cores(ffn_send.reshape(-1, width))
    rows_each = chunks * half
    ffn_sum = Bucket([[(ffn_keep, ffn_other, lane * rows_each, rows_each)] for lane in range(2)])

    dy1, cross_gain_grad, mem_grad, dq, dk, dv = pl.pallas_call(
        functools.partial(cross_backward_kernel, length, head_size),
        grid=(rows // pair,),
        in_specs=[
            here,
            here,
            keys_spec,
            keys_spec,
            per_row(stacked, span),
            here,
            line_spec,
            square,
            square,
            square,
            square,
        ],
        out_specs=[here, line_spec, mem_spec, here, keys_spec, keys_spec],
        out_shape=[
            struct(by_row, F32),
            struct((1, width), F32),
            struct(mem.shape, BF16),
            struct(by_row, BF16),
            keys,
            keys,
        ],
        compiler_params=params(LIMITS["cross_backward"]),
        cost_estimate=cost(6 * rows * span * width * inner, 10 * rows * span * width),
        name="cross_backward",
    )(
        dy2.reshape(by_row),
        cq,
        ck,
        cv,
        p2,
        y1,
        gain_two,
        cross_query,
        cross_key,
        cross_value,
        cross_output,
    )
    passed = ffn_sum.first(cross_gain_grad)
    inner_devices = 8 if devices % 8 == 0 else 1
    outer_devices = devices // inner_devices
    lines = [
        [o * inner_devices + i for o in range(outer_devices)] for i in range(inner_devices)
    ]
    blocks_of = [
        [o * inner_devices + i for i in range(inner_devices)] for o in range(outer_devices)
    ]

    def exchange(array, groups):
        return lax.all_to_all(
            array, "dp", split_axis=0, concat_axis=0, tiled=True, axis_index_groups=groups
        )

    halfway = mem_grad.reshape(outer_devices, inner_devices, rows, held, width)
    halfway = exchange(tied(halfway, passed), lines)

    halves = struct((4 * half, width), BF16)
    halves_spec = whole(4 * half, width)
    cross_keep, cross_send = pl.pallas_call(
        functools.partial(cross_grads_kernel, rows),
        grid=(rows // pair,),
        in_specs=[smem, any_spec, keys_spec, keys_spec, mem_spec] + [full] * 4,
        out_specs=[halves_spec, halves_spec],
        out_shape=[halves, halves],
        scratch_shapes=[pltpu.VMEM((4, width, inner), F32)],
        compiler_params=params(LIMITS["cross_grads"]),
        cost_estimate=cost(4 * rows * span * width * inner, 10 * rows * span * width),
        name="cross_grads",
    )(
        core,
        passed,
        dk,
        dv,
        mem,
        dq.reshape(count, inner),
        h2.reshape(count, width),
        o2.reshape(count, inner),
        dy2,
    )

    lanes = 256
    buckets = np.zeros((lanes, width), np.float32)
    for n in range(length):
        buckets[length - 1 - n, table[n, 0]] = 1.0
    packed = [struct((size, width), BF16) for size in (2 * half, half, half + CARRIED)] * 2
    target_grad, *self_halves = pl.pallas_call(
        functools.partial(self_backward_kernel, rows, length, head_size),
        grid=(rows // pair,),
        in_specs=[
            smem,
            any_spec,
            here,
            here,
            here,
            here,
            per_row(stacked, length),
            full,
            full,
            here,
            line_spec,
            square,
            square,
            square,
            square,
            line_spec,
            line_spec,
            whole(lanes, width),
        ],
        out_specs=[here] + [whole(*one.shape) for one in packed],
        out_shape=[struct(by_row, BF16)] + packed,
        scratch_shapes=[
            pltpu.VMEM((4, width, inner), F32),
            pltpu.VMEM((count, width), BF16),
            pltpu.VMEM((count, inner), BF16),
            pltpu.VMEM((count, inner), BF16),
            pltpu.VMEM((count, inner), BF16),
            pltpu.VMEM((1, width), F32),
            pltpu.VMEM((heads, length, length), F32),
        ],
        compiler_params=params(LIMITS["self_backward"]),
        cost_estimate=cost(2 * count * width * inner * 12, 12 * count * width),
        name="self_backward",
    )(
        core,
        cross_keep,
        dy1,
        q,
        k,
        v,
        p1,
        o1.reshape(count, inner),
        h1.reshape(count, width),
        target,
        gain_one,
        self_query,
        self_key,
        self_value,
        self_output,
        cross_gain_grad,
        ffn_gain_grad,
        jnp.asarray(buckets),
    )
    passed = ffn_sum.second(self_halves[1])
    cross_other = swap_cores(tied(cross_send, cross_keep))
    self_chunks = [
        (keep, swap_cores(send), 0, blocks * half)
        for blocks, keep, send in zip((2, 1, 1), self_halves[:3], self_halves[3:])
    ]
    attention_sum = Bucket([[(cross_keep, cross_other, 0, 4 * half)], self_chunks], CARRIED)
    phases = len(ffn_sum.factors)
    ahead = [functools.partial(ffn_sum.third, phase) for phase in range(3, phases + 1)]
    ahead += [functools.partial(ffn_sum.back, phase) for phase in range(phases - 1, 2, -1)]
    ahead += [ffn_sum.back_second, ffn_sum.back_first]
    behind = [attention_sum.first, attention_sum.second]
    behind += [functools.partial(attention_sum.third, phase) for phase in range(3, phases + 1)]
    behind += [functools.partial(attention_sum.back, phase) for phase in range(phases - 1, 2, -1)]
    for k, (one, other) in enumerate(zip(ahead, behind)):
        passed = other(passed, *([returned] if k == len(ahead) - 1 else []))
        passed = one(passed, *([halfway] if k == SECOND_HALF else []))
        if k == SECOND_HALF:
            returned = exchange(tied(jnp.swapaxes(halfway, 0, 1), passed), blocks_of)
    ffn_layout = [(0, 0, c, 0, half) for c in range(chunks)]
    ffn_layout += [(1, c, 0, 0, half) for c in range(chunks)]
    small = attention_sum.sums
    ffn_in_grad, ffn_out_grad, passed = ffn_sum.finish(
        core, ffn_layout, half, [(width, hidden_width), (hidden_width, width)], passed
    )
    passed = attention_sum.back_second(passed, small)
    passed = attention_sum.back_first(passed)
    memory_grad, passed = by_position(returned, passed)
    attention_layout = [(part, 0, 0, 0, half) for part in range(4)]
    for part in range(2):
        attention_layout += [(4 + part, 0, 0, 0, half)]
        attention_layout += [(out, 0, 0, part * half // 2, half // 2) for out in (6, 7)]
    (
        cross_output_grad,
        cross_query_grad,
        cross_key_grad,
        cross_value_grad,
        self_output_grad,
        self_query_grad,
        self_key_grad,
        self_value_grad,
        _,
    ) = attention_sum.finish(core, attention_layout, half, [(width, inner)] * 8, passed)
    return (
        layer_out.reshape(by_row),
        target_grad,
        memory_grad,
        self_query_grad,
        self_key_grad,
        self_value_grad,
        self_output_grad,
        small[3 : 3 + heads, :NB].T,
        small[0],
        cross_query_grad,
        cross_key_grad,
        cross_value_grad,
        cross_output_grad,
        small[1],
        small[2],
        ffn_in_grad,
        ffn_out_grad,
    )


def solution(mesh):
    rows3 = P("dp", None, None)
    rows2 = P("dp", None)
    in_specs = (rows3, rows3, rows2, rows2, rows3) + (P(),) * 14
    out_specs = (rows3, rows3, rows3) + (P(),) * 14
    return jax.shard_map(body, mesh=mesh, in_specs=in_specs, out_specs=out_specs, check_vma=False)
```

```python
import functools

import jax
import jax.numpy as jnp
import numpy as np
from jax import lax
from jax.experimental import pallas as pl
from jax.experimental.pallas import tpu as pltpu
from jax.sharding import PartitionSpec as P

NB = 32
MAXDIST = 128
EPS = 1e-06
GROUP = 256
CARRIED = 16
SECOND_HALF = 2
MASKED = -1000000000.0
LIMITS = {
    "by_row": 16,
    "self_forward": 36,
    "cross_forward": 56,
    "ffn": 56,
    "cross_backward": 56,
    "cross_grads": 56,
    "self_backward": 56,
    "by_position": 16,
    "move_rows": 16,
    "unpack": 16,
}
BF16 = jnp.bfloat16
F32 = jnp.float32


def bucket_table(length):
    exact = NB // 2
    offsets = np.arange(length)[:, None] - np.arange(length)[None, :]
    distance = np.maximum(offsets, 0)
    scaled = np.log(np.maximum(distance, exact) / exact) / np.log(MAXDIST / exact) * (NB - exact)
    farther = np.minimum(exact + scaled.astype(np.int32), NB - 1)
    return np.where(distance < exact, distance, farther).astype(np.int32)


def dot_nn(left, right):
    return lax.dot_general(left, right, (((1,), (0,)), ((), ())), preferred_element_type=F32)


def dot_nt(left, right):
    return lax.dot_general(left, right, (((1,), (1,)), ((), ())), preferred_element_type=F32)


def dot_tn(left, right):
    return lax.dot_general(left, right, (((0,), (0,)), ((), ())), preferred_element_type=F32)


def norm_factor(tensor):
    return lax.rsqrt(jnp.mean(tensor * tensor, axis=-1, keepdims=True) + EPS)


def norm_backward(tensor, gain, incoming):
    factor = norm_factor(tensor)
    scaled = tensor * factor
    shaped = incoming * gain
    inner = jnp.mean(scaled * shaped, axis=-1, keepdims=True)
    return factor * (shaped - scaled * inner), incoming * scaled


def head_masks(head_size, dtype):
    lane = lax.broadcasted_iota(jnp.int32, (1, GROUP), 1)
    return [
        jnp.where(lane // head_size == h, 1.0, 0.0).astype(dtype)
        for h in range(GROUP // head_size)
    ]


def stack_heads(tensor, masks):
    return jnp.concatenate([tensor * mask for mask in masks], axis=0)


def merge_heads(stacked, masks, length):
    out = stacked[:length] * masks[0]
    for h in range(1, len(masks)):
        out = out + stacked[h * length : (h + 1) * length] * masks[h]
    return out


def flat(ref):
    return ref[...].reshape(-1, ref.shape[-1])


def row_parts(size, index):
    return pl.ds(pl.multiple_of(index * size, 16), size)


def softmax_rows(scores):
    top = jnp.max(scores, axis=-1, keepdims=True)
    grown = jnp.exp(scores - top)
    return grown * (1.0 / jnp.sum(grown, axis=-1, keepdims=True))


def self_forward_kernel(
    rows,
    length,
    head_size,
    x_ref,
    column_ref,
    line_ref,
    bias_ref,
    query_ref,
    key_ref,
    value_ref,
    output_ref,
    cross_query_ref,
    gain_one_ref,
    gain_two_ref,
    h1_ref,
    q_ref,
    k_ref,
    v_ref,
    p_ref,
    o_ref,
    y1_ref,
    h2_ref,
    cq_ref,
):
    masks = head_masks(head_size, BF16)
    masks_f = head_masks(head_size, F32)
    x = x_ref[...].astype(F32)
    h1 = (x * norm_factor(x) * gain_one_ref[...]).astype(BF16)
    h1_ref[...] = h1
    q_ref[...] = dot_nn(h1, query_ref[...]).astype(BF16)
    k_ref[...] = dot_nn(h1, key_ref[...]).astype(BF16)
    v_ref[...] = dot_nn(h1, value_ref[...]).astype(BF16)
    i = lax.broadcasted_iota(jnp.int32, (length, length), 0)
    j = lax.broadcasted_iota(jnp.int32, (length, length), 1)

    def row(r, carry):
        here = pl.ds(pl.multiple_of(r * length, 16), length)
        allowed = jnp.logical_and(j <= i, column_ref[r] == line_ref[r])
        shift = jnp.where(allowed, 0.0, MASKED)
        for g in range(q_ref.shape[1] // GROUP):
            lanes = pl.ds(g * GROUP, GROUP)
            scores = dot_nt(stack_heads(q_ref[here, lanes], masks), k_ref[here, lanes])
            probs = []
            for h in range(len(masks)):
                one = scores[h * length : (h + 1) * length]
                one = one + bias_ref[g * len(masks) + h] + shift
                probs.append(softmax_rows(one).astype(BF16))
            stacked = jnp.concatenate(probs, axis=0)
            size = stacked.shape[0]
            p_ref[r, g * size : (g + 1) * size, :] = stacked
            mixed = merge_heads(dot_nn(stacked, v_ref[here, lanes]), masks_f, length)
            o_ref[here, lanes] = mixed.astype(BF16)
        return carry

    lax.fori_loop(0, rows, row, 0)
    y1 = x + dot_nn(o_ref[...], output_ref[...])
    y1_ref[...] = y1
    h2 = (y1 * norm_factor(y1) * gain_two_ref[...]).astype(BF16)
    h2_ref[...] = h2
    cq_ref[...] = dot_nn(h2, cross_query_ref[...]).astype(BF16)


def cross_forward_kernel(
    length,
    head_size,
    cq_ref,
    mem_ref,
    y1_ref,
    column_ref,
    line_ref,
    key_ref,
    value_ref,
    output_ref,
    ck_ref,
    cv_ref,
    p_ref,
    o_ref,
    y2_ref,
):
    masks = head_masks(head_size, BF16)
    masks_f = head_masks(head_size, F32)
    pair, span, inner = ck_ref.shape
    for r in range(pair):
        mem = mem_ref[:, r].reshape(span, -1)
        ck_ref[r] = dot_nn(mem, key_ref[...]).astype(BF16)
        cv_ref[r] = dot_nn(mem, value_ref[...]).astype(BF16)
    jobs = [(r, g) for r in range(pair) for g in range(inner // GROUP)]
    shift = [jnp.where(column_ref[r] == line_ref[r], 0.0, MASKED) for r in range(pair)]
    scores = {}
    for r, g in jobs:
        lanes = slice(g * GROUP, (g + 1) * GROUP)
        scores[r, g] = dot_nt(stack_heads(cq_ref[r, :, lanes], masks), ck_ref[r, :, lanes])
    for r, g in jobs:
        lanes = slice(g * GROUP, (g + 1) * GROUP)
        probs = []
        for h in range(len(masks)):
            one = scores[r, g][h * length : (h + 1) * length] + shift[r]
            probs.append(softmax_rows(one).astype(BF16))
        stacked = jnp.concatenate(probs, axis=0)
        size = stacked.shape[0]
        p_ref[r, g * size : (g + 1) * size, :] = stacked
        mixed = merge_heads(dot_nn(stacked, cv_ref[r, :, lanes]), masks_f, length)
        o_ref[r, :, lanes] = mixed.astype(BF16)
    y2 = flat(y1_ref) + dot_nn(flat(o_ref), output_ref[...])
    y2_ref[...] = y2.reshape(y2_ref.shape)


def ffn_kernel(
    chunks,
    core_ref,
    y2_ref,
    cot_ref,
    gain_ref,
    in_ref,
    out_ref,
    layer_ref,
    dy2_ref,
    gain_grad_ref,
    keep_ref,
    send_ref,
    h3_ref,
    total_ref,
    back_ref,
    grad_ref,
):
    step = pl.program_id(0)

    @pl.when(step == 0)
    def _():
        y2 = y2_ref[...]
        h3_ref[...] = (y2 * norm_factor(y2) * gain_ref[...]).astype(BF16)
        total_ref[...] = y2
        back_ref[...] = jnp.zeros_like(back_ref)

    h3 = h3_ref[...]
    cot = cot_ref[...]
    act = dot_nn(h3, in_ref[...])
    square = act * act
    root = float(np.sqrt(2.0 / np.pi))
    tanh = jnp.tanh(root * act * (1.0 + 0.044715 * square))
    gate = 0.5 + 0.5 * tanh
    hidden = (act * gate).astype(BF16)
    slope = gate + (0.5 * root) * act * (1.0 - tanh * tanh) * (1.0 + 3 * 0.044715 * square)
    act_grad = (slope * dot_nt(cot, out_ref[...])).astype(BF16)
    total_ref[...] += dot_nn(hidden, out_ref[...])
    back_ref[...] += dot_nt(act_grad, in_ref[...])
    half = keep_ref.shape[2]
    mine = row_parts(half, core_ref[0])
    other = row_parts(half, 1 - core_ref[0])
    grad_ref[0] = dot_tn(h3, act_grad)
    grad_ref[1] = dot_tn(hidden, cot)
    for part in range(2):
        keep_ref[part, 0] = grad_ref[part, mine, :].astype(BF16)
        send_ref[part, 0] = grad_ref[part, other, :].astype(BF16)

    @pl.when(step == chunks - 1)
    def _():
        layer_ref[...] = total_ref[...].astype(BF16)
        grad, gain_grad = norm_backward(y2_ref[...], gain_ref[...], back_ref[...])
        dy2_ref[...] = cot_ref[...].astype(F32) + grad
        gain_grad_ref[...] = jnp.sum(gain_grad, axis=0, keepdims=True)


def cross_backward_kernel(
    length,
    head_size,
    dy2_ref,
    cq_ref,
    ck_ref,
    cv_ref,
    p_ref,
    y1_ref,
    gain_ref,
    query_ref,
    key_ref,
    value_ref,
    output_ref,
    dy1_ref,
    gain_grad_ref,
    mem_grad_ref,
    dq_ref,
    dk_ref,
    dv_ref,
):
    masks = head_masks(head_size, BF16)
    masks_f = head_masks(head_size, F32)

    @pl.when(pl.program_id(0) == 0)
    def _():
        gain_grad_ref[...] = jnp.zeros_like(gain_grad_ref)

    pair = dy2_ref.shape[0]
    c2 = flat(dy2_ref).astype(BF16)
    do = dot_nt(c2, output_ref[...]).astype(BF16)
    jobs = [(r, g) for r in range(pair) for g in range(cq_ref.shape[2] // GROUP)]
    outs, upstream = {}, {}
    for r, g in jobs:
        lanes = slice(g * GROUP, (g + 1) * GROUP)
        outs[r, g] = stack_heads(do[r * length : (r + 1) * length, lanes], masks)
        upstream[r, g] = dot_nt(outs[r, g], cv_ref[r, :, lanes])
    for r, g in jobs:
        lanes = slice(g * GROUP, (g + 1) * GROUP)
        size = len(masks) * length
        probs = p_ref[r, g * size : (g + 1) * size, :]
        dv_ref[r, :, lanes] = dot_tn(probs, outs[r, g]).astype(BF16)
        pieces = []
        for h in range(len(masks)):
            prob = probs[h * length : (h + 1) * length].astype(F32)
            up = upstream[r, g][h * length : (h + 1) * length]
            pieces.append((prob * (up - jnp.sum(prob * up, axis=-1, keepdims=True))).astype(BF16))
        ds = jnp.concatenate(pieces, axis=0)
        queries = stack_heads(cq_ref[r, :, lanes], masks)
        dk_ref[r, :, lanes] = dot_tn(ds, queries).astype(BF16)
        mixed = merge_heads(dot_nn(ds, ck_ref[r, :, lanes]), masks_f, length)
        dq_ref[r, :, lanes] = mixed.astype(BF16)
    for r in range(pair):
        mem_grad = dot_nt(dk_ref[r], key_ref[...]) + dot_nt(dv_ref[r], value_ref[...])
        shape = (mem_grad_ref.shape[0], *mem_grad_ref.shape[2:])
        mem_grad_ref[:, r] = mem_grad.astype(BF16).reshape(shape)
    back = dot_nt(flat(dq_ref), query_ref[...])
    grad, gain_grad = norm_backward(flat(y1_ref), gain_ref[...], back)
    dy1_ref[...] = (flat(dy2_ref) + grad).reshape(dy1_ref.shape)
    gain_grad_ref[...] += jnp.sum(gain_grad, axis=0, keepdims=True)


def cross_grads_kernel(
    rows,
    core_ref,
    after_ref,
    dk_ref,
    dv_ref,
    mem_ref,
    dq_ref,
    h2_ref,
    o_ref,
    dy2_ref,
    keep_ref,
    send_ref,
    grad_ref,
):
    step = pl.program_id(0)
    pair, span, _ = dk_ref.shape
    key_grad, value_grad = None, None
    for r in range(pair):
        mem = mem_ref[:, r].reshape(span, -1)
        one, other = dot_tn(mem, dk_ref[r]), dot_tn(mem, dv_ref[r])
        key_grad = key_grad + one if r else one
        value_grad = value_grad + other if r else other

    @pl.when(step == 0)
    def _():
        grad_ref[0] = dot_tn(o_ref[...], dy2_ref[...].astype(BF16))
        grad_ref[1] = dot_tn(h2_ref[...], dq_ref[...])
        grad_ref[2] = key_grad
        grad_ref[3] = value_grad

    @pl.when(step > 0)
    def _():
        grad_ref[2] += key_grad
        grad_ref[3] += value_grad

    @pl.when(step == rows // pair - 1)
    def _():
        write_grads(core_ref, grad_ref, [keep_ref], [send_ref])


def write_grads(core_ref, grad_ref, keeps, sends):
    half = grad_ref.shape[1] // 2
    mine = row_parts(half, core_ref[0])
    other = row_parts(half, 1 - core_ref[0])
    part = 0
    for keep_ref, send_ref in zip(keeps, sends):
        for block in range(keep_ref.shape[0] // half):
            here = slice(block * half, (block + 1) * half)
            keep_ref[here, :] = grad_ref[part, mine, :].astype(BF16)
            send_ref[here, :] = grad_ref[part, other, :].astype(BF16)
            part += 1


def self_backward_kernel(
    rows,
    length,
    head_size,
    core_ref,
    after_ref,
    dy1_ref,
    q_ref,
    k_ref,
    v_ref,
    p_ref,
    o_ref,
    h1_ref,
    x_ref,
    gain_ref,
    query_ref,
    key_ref,
    value_ref,
    output_ref,
    cross_gain_ref,
    ffn_gain_ref,
    buckets_ref,
    dx_ref,
    keep_ref,
    next_keep_ref,
    last_keep_ref,
    send_ref,
    next_send_ref,
    last_send_ref,
    grad_ref,
    c1_ref,
    dq_ref,
    dk_ref,
    dv_ref,
    gain_total_ref,
    bias_grad_ref,
):
    step = pl.program_id(0)
    masks = head_masks(head_size, BF16)
    masks_f = head_masks(head_size, F32)
    pair = dy1_ref.shape[0]
    here = pl.ds(pl.multiple_of(step * pair * length, 16), pair * length)

    @pl.when(step == 0)
    def _():
        gain_total_ref[...] = jnp.zeros_like(gain_total_ref)
        bias_grad_ref[...] = jnp.zeros_like(bias_grad_ref)

    c1 = flat(dy1_ref).astype(BF16)
    c1_ref[here, :] = c1
    do = dot_nt(c1, output_ref[...]).astype(BF16)
    jobs = [(r, g) for r in range(pair) for g in range(q_ref.shape[2] // GROUP)]
    outs, upstream, total = {}, {}, {}
    for r, g in jobs:
        lanes = slice(g * GROUP, (g + 1) * GROUP)
        outs[r, g] = stack_heads(do[r * length : (r + 1) * length, lanes], masks)
        upstream[r, g] = dot_nt(outs[r, g], v_ref[r, :, lanes])
    for r, g in jobs:
        lanes = slice(g * GROUP, (g + 1) * GROUP)
        there = pl.ds(pl.multiple_of((step * pair + r) * length, 16), length)
        size = len(masks) * length
        probs = p_ref[r, g * size : (g + 1) * size, :]
        dv_ref[there, lanes] = dot_tn(probs, outs[r, g]).astype(BF16)
        pieces = []
        for h in range(len(masks)):
            prob = probs[h * length : (h + 1) * length].astype(F32)
            up = upstream[r, g][h * length : (h + 1) * length]
            one = (prob * (up - jnp.sum(prob * up, axis=-1, keepdims=True))).astype(BF16)
            pieces.append(one)
            total[g, h] = one.astype(F32) + total[g, h] if r else one.astype(F32)
        ds = jnp.concatenate(pieces, axis=0)
        queries = stack_heads(q_ref[r, :, lanes], masks)
        dk_ref[there, lanes] = dot_tn(ds, queries).astype(BF16)
        mixed = merge_heads(dot_nn(ds, k_ref[r, :, lanes]), masks_f, length)
        dq_ref[there, lanes] = mixed.astype(BF16)
    for (g, h), one in total.items():
        bias_grad_ref[g * len(masks) + h] += one
    back = dot_nt(dq_ref[here, :], query_ref[...])
    back = back + dot_nt(dk_ref[here, :], key_ref[...])
    back = back + dot_nt(dv_ref[here, :], value_ref[...])
    grad, gain_grad = norm_backward(flat(x_ref).astype(F32), gain_ref[...], back)
    dx_ref[...] = (flat(dy1_ref) + grad).astype(BF16).reshape(dx_ref.shape)
    gain_total_ref[...] += jnp.sum(gain_grad, axis=0, keepdims=True)

    @pl.when(step == rows // pair - 1)
    def _():
        h1 = h1_ref[...]
        grad_ref[0] = dot_tn(o_ref[...], c1_ref[...])
        grad_ref[1] = dot_tn(h1, dq_ref[...])
        grad_ref[2] = dot_tn(h1, dk_ref[...])
        grad_ref[3] = dot_tn(h1, dv_ref[...])
        keeps = [keep_ref, next_keep_ref, last_keep_ref]
        sends = [send_ref, next_send_ref, last_send_ref]
        write_grads(core_ref, grad_ref, keeps, sends)
        heads = bias_grad_ref.shape[0]
        lanes = buckets_ref.shape[0]
        flip = jnp.where(
            lax.broadcasted_iota(jnp.int32, (length, length), 0)
            + lax.broadcasted_iota(jnp.int32, (length, length), 1)
            == length - 1,
            1.0,
            0.0,
        ).astype(BF16)
        diagonals = []
        for h in range(heads):
            flipped = dot_nn(flip, bias_grad_ref[h].astype(BF16))
            padded = jnp.concatenate([flipped, jnp.zeros((length, lanes - length), F32)], axis=1)
            skewed = pltpu.roll(padded, 0, 1, stride=1, stride_axis=0)
            diagonals.append(jnp.sum(skewed, axis=0, keepdims=True))
        sums = dot_nn(jnp.concatenate(diagonals, axis=0), buckets_ref[...])
        small = jnp.concatenate(
            [
                gain_total_ref[...],
                cross_gain_ref[...],
                ffn_gain_ref[...],
                sums,
                jnp.zeros((CARRIED - 3 - heads, sums.shape[1]), F32),
            ],
            axis=0,
        ).astype(BF16)
        for result in (last_keep_ref, last_send_ref):
            result[result.shape[0] - CARRIED :, :] = small


def factors_of(n):
    factors = []
    while n > 1:
        factor = next(f for f in range(2, n + 1) if n % f == 0)
        factors.append(factor)
        n //= factor
    return factors


def partners(n, stride, factor, j):
    moves = []
    for i in range(n):
        digit = (i // stride) % factor
        moves.append((i, i + ((digit ^ j) - digit) * stride))
    return moves


def move_kernel(plan, operands, digits_ref, *refs):
    ins, outs = refs[:operands], refs[operands:]

    def rows_at(place, size):
        if isinstance(place, int):
            return slice(place, place + size)
        base, digit, j = place
        start = base + (digits_ref[digit] ^ j) * size
        return pl.ds(pl.multiple_of(start, 16), size)

    for out, to, sources, come, size in plan:
        if len(sources) == 1:
            rows = ins[sources[0]][rows_at(come, size), :]
        else:
            terms = [ins[source][rows_at(come, size), :].astype(F32) for source in sources]
            while len(terms) > 1:
                terms = [terms[i] + terms[i + 1] for i in range(0, len(terms), 2)]
            rows = terms[0].astype(BF16)
        outs[len(outs) - 1 - out][rows_at(to, size), :] = rows


def move_rows(plan, sizes, operands, digits, after):
    columns = operands[0].shape[1]
    vmem = pl.BlockSpec(memory_space=pltpu.VMEM)
    results = pl.pallas_call(
        functools.partial(move_kernel, plan, len(operands)),
        in_specs=[pl.BlockSpec(memory_space=pltpu.SMEM)]
        + [vmem] * len(operands)
        + [pl.BlockSpec(memory_space=pl.ANY)] * len(after),
        out_specs=[vmem] * len(sizes),
        out_shape=[struct((size, columns), BF16) for size in sizes[::-1]],
        compiler_params=params(LIMITS["move_rows"]),
        cost_estimate=cost(0, 4 * sum(sizes) * columns),
        name="move_rows",
    )(digits, *operands, *after)
    return results[::-1]


def unpack_kernel(layout, half, core_ref, own_ref, other_ref, *refs):
    outs = refs[-2 - max(entry[0] for entry in layout) : -1]
    refs[-1][...] = jnp.zeros_like(refs[-1])
    width = own_ref.shape[1]
    start = 0
    for out, row, column, offset, size in layout:
        columns = pl.ds(column * width, width)
        for ref, core in ((own_ref, core_ref[0]), (other_ref, 1 - core_ref[0])):
            first = pl.multiple_of(row * 2 * half + core * half + offset, 16)
            rows = ref[start : start + size, :].astype(F32)
            outs[out][pl.ds(first, size), columns] = rows
        start += size


def unpack(own, other, core, layout, half, shapes, after):
    vmem = pl.BlockSpec(memory_space=pltpu.VMEM)
    return pl.pallas_call(
        functools.partial(unpack_kernel, layout, half),
        in_specs=[pl.BlockSpec(memory_space=pltpu.SMEM), vmem, vmem]
        + [pl.BlockSpec(memory_space=pl.ANY)] * len(after),
        out_specs=[vmem] * (len(shapes) + 1),
        out_shape=[struct(shape, F32) for shape in (*shapes, (8, 128))],
        compiler_params=params(LIMITS["unpack"]),
        cost_estimate=cost(0, 12 * own.shape[0] * own.shape[1]),
        name="unpack",
    )(core, own, other, *after)


def turned(rows, first, second):
    size = first * second
    to = lax.broadcasted_iota(jnp.int32, (size, size), 0)
    come = lax.broadcasted_iota(jnp.int32, (size, size), 1)
    here = to % first * second + to // first == come
    return dot_nn(jnp.where(here, 1.0, 0.0).astype(BF16), rows).astype(BF16)


def by_row_kernel(rows, memory_ref, out_ref):
    held, count, width = memory_ref.shape
    for g in range(count // rows):
        part = memory_ref[:, g * rows : (g + 1) * rows, :].reshape(held * rows, width)
        out_ref[g * rows : (g + 1) * rows] = turned(part, held, rows).reshape(rows, held, width)


def by_row_first(memory):
    held, count, width = memory.shape
    rows = GROUP // held
    if held % 16 or rows % 16 or count % (4 * rows):
        return jnp.swapaxes(memory, 0, 1)
    return pl.pallas_call(
        functools.partial(by_row_kernel, rows),
        grid=(count // (4 * rows),),
        in_specs=[pl.BlockSpec((held, 4 * rows, width), lambda g: (0, g, 0))],
        out_specs=pl.BlockSpec((4 * rows, held, width), lambda g: (g, 0, 0)),
        out_shape=struct((count, held, width), BF16),
        compiler_params=params(LIMITS["by_row"]),
        cost_estimate=cost(2 * GROUP * count * held * width, 4 * count * held * width),
        name="by_row",
    )(memory)


def by_position_kernel(rows, rows_ref, after_ref, out_ref, token_ref):
    token_ref[...] = jnp.zeros_like(token_ref)
    held, width = rows_ref.shape[3:]
    each = rows_ref.shape[2]
    owners = rows // each
    for g in range(rows_ref.shape[0] // owners):
        part = rows_ref[g * owners : (g + 1) * owners].reshape(rows * held, width)
        part = turned(part, rows, held).reshape(held, rows, width)
        out_ref[:, g * rows : (g + 1) * rows, :] = part


def by_position(returned, after):
    inner, outer, each, held, width = returned.shape
    count = inner * outer * each
    rows = GROUP // held
    if held % 16 or rows % 16 or rows % each or inner * each % rows:
        returned = jnp.swapaxes(returned, 0, 1).reshape(count, held, width)
        return jnp.swapaxes(returned, 0, 1), after
    return pl.pallas_call(
        functools.partial(by_position_kernel, rows),
        grid=(outer,),
        in_specs=[
            pl.BlockSpec((inner, 1, each, held, width), lambda g: (0, g, 0, 0, 0)),
            pl.BlockSpec(memory_space=pl.ANY),
        ],
        out_specs=[pl.BlockSpec((held, inner * each, width), lambda g: (0, g, 0)), whole(8, 128)],
        out_shape=[struct((held, count, width), BF16), struct((8, 128), F32)],
        compiler_params=params(LIMITS["by_position"]),
        cost_estimate=cost(2 * GROUP * count * held * width, 4 * count * held * width),
        name="by_position",
    )(returned, after)


def tied(rows, *after):
    return lax.optimization_barrier((rows, *after))[0]


def swap_cores(rows):
    n = lax.axis_size("dp")
    return lax.ppermute(rows, "dp", [(i, i ^ 1) for i in range(n)])


class Bucket:
    def __init__(self, lanes, carried=0):
        n, me = lax.axis_size("dp"), lax.axis_index("dp")
        self.carried = carried
        self.factors = factors_of(n)
        self.moves, digits, stride = [], [], 1
        for factor in self.factors:
            digits.append((me // stride) % factor)
            self.moves.append([partners(n, stride, factor, j) for j in range(factor)])
            stride *= factor
        self.digits = jnp.stack(digits).astype(jnp.int32)
        self.lanes = lanes

    def send(self, rows, phase, j):
        return lax.ppermute(rows, "dp", self.moves[phase][j])

    def first(self, *after):
        operands, plan, sizes = [], [], []
        for lane, chunks in enumerate(self.lanes):
            start = 0
            for mine, theirs, base, rows in chunks:
                at = []
                for operand in (mine, theirs):
                    if not any(operand is other for other in operands):
                        operands.append(operand)
                    at += [k for k, other in enumerate(operands) if other is operand]
                for j in range(2):
                    plan.append((2 * lane + j, start, at, (base, 1 + lane, j), rows // 2))
                start += rows // 2
            sizes += [start, start]
        if self.carried:
            plan += [(2 + j, sizes[2], at, base + rows, self.carried) for j in range(2)]
            sizes[2] += self.carried
            sizes[3] += self.carried
        own, out, own_too, out_too = move_rows(plan, sizes, operands, self.digits, after)
        self.size = sizes[0]
        self.terms = [[own, self.send(out, 1, 1)], [own_too, self.send(out_too, 2, 1)]]
        return own

    def second(self, *after):
        size = self.size = self.size // 2
        operands = self.terms[0] + self.terms[1]
        plan = []
        for lane in range(2):
            at = [2 * lane, 2 * lane + 1]
            for j in range(2):
                plan.append((2 * lane + j, 0, at, (0, 2 - lane, j), size))
        sizes = [size] * 2 + [size + self.carried] * 2
        if self.carried:
            plan += [(2 + j, size, [2, 3], 2 * size, self.carried) for j in range(2)]
        own, out, own_too, out_too = move_rows(plan, sizes, operands, self.digits, after)
        self.terms = [[own, self.send(out, 2, 1)], [own_too, self.send(out_too, 1, 1)]]
        self.joined = False
        return own

    def third(self, phase, *after):
        parts = self.factors[phase] if phase < len(self.factors) else 1
        size = self.size // parts
        plan = []
        for j in range(parts):
            for lane in range(2):
                if self.joined:
                    at, base = list(range(len(self.terms))), lane * self.size
                else:
                    at, base = [2 * lane, 2 * lane + 1], 0
                come = (base, phase, j) if parts > 1 else base
                plan.append((j, lane * size, at, come, size))
            if self.carried:
                base = 2 * self.size if self.joined else self.size
                plan.append((j, 2 * size, at, base, self.carried))
        operands = self.terms if self.joined else self.terms[0] + self.terms[1]
        total = 2 * size + self.carried
        own, *others = move_rows(plan, [total] * parts, operands, self.digits, after)
        self.size, self.joined = size, True
        if parts > 1:
            self.terms = [own] + [self.send(o, phase, j + 1) for j, o in enumerate(others)]
        else:
            self.sums = own[2 * size :].astype(F32)
            self.pieces = [own[: 2 * size] if self.carried else own]
            self.spread(phase - 1)
        return own

    def spread(self, phase):
        held = self.pieces[0]
        self.pieces += [self.send(held, phase, j) for j in range(1, self.factors[phase])]

    def back(self, phase, *after):
        parts, size = self.factors[phase], self.size
        plan = []
        for j in range(parts):
            for lane in range(2):
                out = 0 if phase > 3 else lane
                base = lane * size * parts if phase > 3 else 0
                plan.append((out, (base, phase, j), [j], lane * size, size))
        self.size = size * parts
        sizes = [2 * self.size] if phase > 3 else [self.size] * 2
        held = move_rows(plan, sizes, self.pieces, self.digits, after)
        if phase > 3:
            self.pieces = list(held)
            self.spread(phase - 1)
        else:
            self.pieces = [held[0], self.send(held[0], 2, 1), held[1], self.send(held[1], 1, 1)]
        return held[0]

    def back_second(self, *after):
        size = self.size
        plan = [
            (lane, (0, 2 - lane, j), [2 * lane + j], 0, size) for lane in range(2) for j in range(2)
        ]
        self.size = 2 * size
        held = move_rows(plan, [self.size] * 2, self.pieces, self.digits, after)
        self.pieces = [held[0], self.send(held[0], 1, 1), held[1], self.send(held[1], 2, 1)]
        return held[0]

    def back_first(self, *after):
        size = self.size
        plan = [
            (0, (2 * lane * size, 1 + lane, j), [2 * lane + j], 0, size)
            for lane in range(2)
            for j in range(2)
        ]
        (held,) = move_rows(plan, [4 * size], self.pieces, self.digits, after)
        self.pieces = [held, self.send(held, 0, 1)]
        return held

    def finish(self, core, layout, half, shapes, *after):
        return unpack(*self.pieces, core, layout, half, shapes, after)


def cost(flops, nbytes, transcendentals=0):
    return pl.CostEstimate(
        flops=int(flops), bytes_accessed=int(nbytes), transcendentals=int(transcendentals)
    )


def whole(*shape):
    return pl.BlockSpec(shape, lambda *_: (0,) * len(shape))


def per_rows(pair, *shape):
    return pl.BlockSpec((pair, *shape), lambda r, *_: (r,) + (0,) * len(shape))


def struct(shape, dtype):
    return jax.ShapeDtypeStruct(shape, dtype)


def params(limit):
    return pltpu.CompilerParams(vmem_limit_bytes=limit * 1024 * 1024)


def body(
    target,
    memory,
    target_segments,
    memory_segments,
    cotangent,
    self_query,
    self_key,
    self_value,
    self_output,
    relative_bias,
    self_gain,
    cross_query,
    cross_key,
    cross_value,
    cross_output,
    cross_gain,
    ffn_gain,
    ffn_in,
    ffn_out,
):
    devices = lax.axis_size("dp")
    rows, length, width = target.shape
    held = memory.shape[0]
    span = held * devices
    heads = relative_bias.shape[1]
    inner = self_query.shape[1]
    head_size = inner // heads
    hidden_width = ffn_in.shape[1]
    chunks = hidden_width // width
    count = rows * length
    stacked = heads * length
    core = (lax.axis_index("dp") % 2).astype(jnp.int32).reshape(1)
    smem = pl.BlockSpec(memory_space=pltpu.SMEM)

    outgoing = by_row_first(memory).reshape(devices, rows, held, width)
    mem = lax.all_to_all(outgoing, "dp", split_axis=0, concat_axis=0, tiled=True)

    gain_one = self_gain.astype(F32).reshape(1, width)
    gain_two = cross_gain.astype(F32).reshape(1, width)
    gain_three = ffn_gain.astype(F32).reshape(1, width)
    table = bucket_table(length)
    onehot = jnp.asarray(table[None, :, :] == np.arange(NB)[:, None, None], dtype=BF16)
    bias = jnp.einsum("bh,bij->hij", relative_bias, onehot, preferred_element_type=F32)
    column = target_segments.reshape(rows, length, 1)
    line = target_segments.reshape(rows, 1, length)
    mem_line = memory_segments.reshape(rows, 1, span)

    tokens = struct((count, inner), BF16)
    h1, q, k, v, p1, o1, y1, h2, cq = pl.pallas_call(
        functools.partial(self_forward_kernel, rows, length, head_size),
        out_shape=[
            tokens,
            tokens,
            tokens,
            tokens,
            struct((rows, stacked, length), BF16),
            tokens,
            struct((count, width), F32),
            tokens,
            tokens,
        ],
        compiler_params=params(LIMITS["self_forward"]),
        cost_estimate=cost(2 * count * width * inner * 5, 12 * count * width),
        name="self_forward",
    )(
        target.reshape(count, width),
        column,
        line,
        bias,
        self_query,
        self_key,
        self_value,
        self_output,
        cross_query,
        gain_one,
        gain_two,
    )
    by_row = (rows, length, width)
    y1 = y1.reshape(by_row)
    cq = cq.reshape(by_row)
    h2 = h2.reshape(by_row)
    h1, q, k, v, o1 = (a.reshape(by_row) for a in (h1, q, k, v, o1))
    half = width // 2
    square = whole(width, inner)
    line_spec = whole(1, width)
    any_spec = pl.BlockSpec(memory_space=pl.ANY)
    pair = 2 if rows % 2 == 0 else 1
    per_row = functools.partial(per_rows, pair)
    here = per_row(length, width)
    mem_spec = pl.BlockSpec((devices, pair, held, width), lambda r: (0, r, 0, 0))
    keys_spec = per_row(span, inner)
    keys = struct((rows, span, inner), BF16)
    ck, cv, p2, o2, y2 = pl.pallas_call(
        functools.partial(cross_forward_kernel, length, head_size),
        grid=(rows // pair,),
        in_specs=[
            here,
            mem_spec,
            here,
            per_row(length, 1),
            per_row(1, span),
            square,
            square,
            square,
        ],
        out_specs=[keys_spec, keys_spec, per_row(stacked, span), here, here],
        out_shape=[
            keys,
            keys,
            struct((rows, stacked, span), BF16),
            struct(by_row, BF16),
            struct(by_row, F32),
        ],
        compiler_params=params(LIMITS["cross_forward"]),
        cost_estimate=cost(4 * rows * span * width * inner, 10 * rows * span * width),
        name="cross_forward",
    )(cq, mem, y1, column, mem_line, cross_key, cross_value, cross_output)

    full = whole(count, width)
    part_spec = pl.BlockSpec((2, 1, half, width), lambda c: (0, c, 0, 0))
    part = struct((2, chunks, half, width), BF16)
    layer_out, dy2, ffn_gain_grad, ffn_keep, ffn_send = pl.pallas_call(
        functools.partial(ffn_kernel, chunks),
        grid=(chunks,),
        in_specs=[
            smem,
            full,
            full,
            line_spec,
            pl.BlockSpec((width, width), lambda c: (0, c)),
            pl.BlockSpec((width, width), lambda c: (c, 0)),
        ],
        out_specs=[full, full, line_spec, part_spec, part_spec],
        out_shape=[
            struct((count, width), BF16),
            struct((count, width), F32),
            struct((1, width), F32),
            part,
            part,
        ],
        scratch_shapes=[
            pltpu.VMEM((count, width), BF16),
            pltpu.VMEM((count, width), F32),
            pltpu.VMEM((count, width), F32),
            pltpu.VMEM((2, width, width), F32),
        ],
        compiler_params=params(LIMITS["ffn"]),
        cost_estimate=cost(12 * count * width * hidden_width, 10 * width * hidden_width),
        name="ffn",
    )(core, y2.reshape(count, width), cotangent.reshape(count, width), gain_three, ffn_in, ffn_out)

    ffn_keep = ffn_keep.reshape(-1, width)
    ffn_other = swap_cores(ffn_send.reshape(-1, width))
    rows_each = chunks * half
    ffn_sum = Bucket([[(ffn_keep, ffn_other, lane * rows_each, rows_each)] for lane in range(2)])

    dy1, cross_gain_grad, mem_grad, dq, dk, dv = pl.pallas_call(
        functools.partial(cross_backward_kernel, length, head_size),
        grid=(rows // pair,),
        in_specs=[
            here,
            here,
            keys_spec,
            keys_spec,
            per_row(stacked, span),
            here,
            line_spec,
            square,
            square,
            square,
            square,
        ],
        out_specs=[here, line_spec, mem_spec, here, keys_spec, keys_spec],
        out_shape=[
            struct(by_row, F32),
            struct((1, width), F32),
            struct(mem.shape, BF16),
            struct(by_row, BF16),
            keys,
            keys,
        ],
        compiler_params=params(LIMITS["cross_backward"]),
        cost_estimate=cost(6 * rows * span * width * inner, 10 * rows * span * width),
        name="cross_backward",
    )(
        dy2.reshape(by_row),
        cq,
        ck,
        cv,
        p2,
        y1,
        gain_two,
        cross_query,
        cross_key,
        cross_value,
        cross_output,
    )
    passed = ffn_sum.first(cross_gain_grad)
    inner_devices = 8 if devices % 8 == 0 else 1
    outer_devices = devices // inner_devices
    lines = [
        [o * inner_devices + i for o in range(outer_devices)] for i in range(inner_devices)
    ]
    blocks_of = [
        [o * inner_devices + i for i in range(inner_devices)] for o in range(outer_devices)
    ]

    def exchange(array, groups):
        return lax.all_to_all(
            array, "dp", split_axis=0, concat_axis=0, tiled=True, axis_index_groups=groups
        )

    halfway = mem_grad.reshape(outer_devices, inner_devices, rows, held, width)
    halfway = exchange(tied(halfway, passed), lines)

    halves = struct((4 * half, width), BF16)
    halves_spec = whole(4 * half, width)
    cross_keep, cross_send = pl.pallas_call(
        functools.partial(cross_grads_kernel, rows),
        grid=(rows // pair,),
        in_specs=[smem, any_spec, keys_spec, keys_spec, mem_spec] + [full] * 4,
        out_specs=[halves_spec, halves_spec],
        out_shape=[halves, halves],
        scratch_shapes=[pltpu.VMEM((4, width, inner), F32)],
        compiler_params=params(LIMITS["cross_grads"]),
        cost_estimate=cost(4 * rows * span * width * inner, 10 * rows * span * width),
        name="cross_grads",
    )(
        core,
        passed,
        dk,
        dv,
        mem,
        dq.reshape(count, inner),
        h2.reshape(count, width),
        o2.reshape(count, inner),
        dy2,
    )

    lanes = 256
    buckets = np.zeros((lanes, width), np.float32)
    for n in range(length):
        buckets[length - 1 - n, table[n, 0]] = 1.0
    packed = [struct((size, width), BF16) for size in (2 * half, half, half + CARRIED)] * 2
    target_grad, *self_halves = pl.pallas_call(
        functools.partial(self_backward_kernel, rows, length, head_size),
        grid=(rows // pair,),
        in_specs=[
            smem,
            any_spec,
            here,
            here,
            here,
            here,
            per_row(stacked, length),
            full,
            full,
            here,
            line_spec,
            square,
            square,
            square,
            square,
            line_spec,
            line_spec,
            whole(lanes, width),
        ],
        out_specs=[here] + [whole(*one.shape) for one in packed],
        out_shape=[struct(by_row, BF16)] + packed,
        scratch_shapes=[
            pltpu.VMEM((4, width, inner), F32),
            pltpu.VMEM((count, width), BF16),
            pltpu.VMEM((count, inner), BF16),
            pltpu.VMEM((count, inner), BF16),
            pltpu.VMEM((count, inner), BF16),
            pltpu.VMEM((1, width), F32),
            pltpu.VMEM((heads, length, length), F32),
        ],
        compiler_params=params(LIMITS["self_backward"]),
        cost_estimate=cost(2 * count * width * inner * 12, 12 * count * width),
        name="self_backward",
    )(
        core,
        cross_keep,
        dy1,
        q,
        k,
        v,
        p1,
        o1.reshape(count, inner),
        h1.reshape(count, width),
        target,
        gain_one,
        self_query,
        self_key,
        self_value,
        self_output,
        cross_gain_grad,
        ffn_gain_grad,
        jnp.asarray(buckets),
    )
    passed = ffn_sum.second(self_halves[1])
    cross_other = swap_cores(tied(cross_send, cross_keep))
    self_chunks = [
        (keep, swap_cores(send), 0, blocks * half)
        for blocks, keep, send in zip((2, 1, 1), self_halves[:3], self_halves[3:])
    ]
    attention_sum = Bucket([[(cross_keep, cross_other, 0, 4 * half)], self_chunks], CARRIED)
    phases = len(ffn_sum.factors)
    ahead = [functools.partial(ffn_sum.third, phase) for phase in range(3, phases + 1)]
    ahead += [functools.partial(ffn_sum.back, phase) for phase in range(phases - 1, 2, -1)]
    ahead += [ffn_sum.back_second, ffn_sum.back_first]
    behind = [attention_sum.first, attention_sum.second]
    behind += [functools.partial(attention_sum.third, phase) for phase in range(3, phases + 1)]
    behind += [functools.partial(attention_sum.back, phase) for phase in range(phases - 1, 2, -1)]
    for k, (one, other) in enumerate(zip(ahead, behind)):
        passed = other(passed, *([returned] if k == len(ahead) - 1 else []))
        passed = one(passed, *([halfway] if k == SECOND_HALF else []))
        if k == SECOND_HALF:
            returned = exchange(tied(jnp.swapaxes(halfway, 0, 1), passed), blocks_of)
    ffn_layout = [(0, 0, c, 0, half) for c in range(chunks)]
    ffn_layout += [(1, c, 0, 0, half) for c in range(chunks)]
    small = attention_sum.sums
    ffn_in_grad, ffn_out_grad, passed = ffn_sum.finish(
        core, ffn_layout, half, [(width, hidden_width), (hidden_width, width)], passed
    )
    passed = attention_sum.back_second(passed)
    passed = attention_sum.back_first(passed)
    memory_grad, passed = by_position(returned, passed)
    attention_layout = [(part, 0, 0, 0, half) for part in range(4)]
    for part in range(2):
        attention_layout += [(4 + part, 0, 0, 0, half)]
        attention_layout += [(out, 0, 0, part * half // 2, half // 2) for out in (6, 7)]
    (
        cross_output_grad,
        cross_query_grad,
        cross_key_grad,
        cross_value_grad,
        self_output_grad,
        self_query_grad,
        self_key_grad,
        self_value_grad,
        _,
    ) = attention_sum.finish(core, attention_layout, half, [(width, inner)] * 8, passed)
    return (
        layer_out.reshape(by_row),
        target_grad,
        memory_grad,
        self_query_grad,
        self_key_grad,
        self_value_grad,
        self_output_grad,
        small[3 : 3 + heads, :NB].T,
        small[0],
        cross_query_grad,
        cross_key_grad,
        cross_value_grad,
        cross_output_grad,
        small[1],
        small[2],
        ffn_in_grad,
        ffn_out_grad,
    )


def solution(mesh):
    rows3 = P("dp", None, None)
    rows2 = P("dp", None)
    in_specs = (rows3, rows3, rows2, rows2, rows3) + (P(),) * 14
    out_specs = (rows3, rows3, rows3) + (P(),) * 14
    return jax.shard_map(body, mesh=mesh, in_specs=in_specs, out_specs=out_specs, check_vma=False)
```
